256 devices in a mesh: gz: 4 (over y), gy: 4 (over z_lo, core), gx: 16 (over x, z_hi).
Axes of the slice: x: 4, y: 4, z: 8 (z_hi: 4, z_lo: 2; z = z_hi * 2 + z_lo), core: 2. Of those that a mesh axis runs over, the one named last changes fastest.
Arguments:
- filtered: float32 [64, 512, 2048], P('gz', 'gy', 'gx'), may hold values from 0.3 to 1
- printed: float32 [64, 512, 2048], P('gz', 'gy', 'gx'), may hold values from 0.3 to 0.7
- sensitivity: float32 [64, 512, 2048], P('gz', 'gy', 'gx'), may hold values from -6 to 6
- passive: int32 [64, 512, 2048], P('gz', 'gy', 'gx'), may hold values 0 or 1
Outputs:
- design_grad: float32 [64, 512, 2048], P('gz', 'gy', 'gx')
The draws below stay inside these ranges and needn't reach their ends.
All inputs are finite; a program needn't handle non-finite values. No bound on the sum of `passive` on one device may be relied on, other than what follows from the above.
Results may differ from the reference program's by a relative error of at most 0.000064.
Values sent between devices are 32-bit elements; how exact they have to be, the bound alone decides.
No kernel may reach another device: no remote copies, remote signals or barrier semaphores. Data moves between devices by JAX's collectives and lax.ppermute only.
A program may use at most 128 MiB of HBM per device.

```python
import math
import jax
import jax.numpy as jnp
from jax import lax

RADIUS = 4
DEPTH = 64
ROWS = 512
COLS = 2048


def draw_filtered(key, part):
    key = jax.random.fold_in(key, 7)
    key_base, key_layers, key_voxel_grid, key_values = jax.random.split(key, 4)
    grid_shape = (DEPTH, ROWS, COLS)
    uniform_base = jax.random.uniform(key_base, grid_shape, jnp.float32)
    floor_value = 0.76 + 0.24 * uniform_base
    fraction_part = 3
    count = 3
    selected_entry = jax.random.permutation(key_layers, DEPTH - 1)[:count] + 1
    index_of_layer = jnp.arange(DEPTH, dtype=jnp.int32)
    spike_layer = jnp.any(index_of_layer[:, None] == selected_entry[None, :].astype(jnp.int32), axis=1)
    spike_cell = jax.random.randint(key_voxel_grid, grid_shape, 0, fraction_part) == 0
    value_beneath = 0.3 + 0.3 * jax.random.uniform(key_values, grid_shape, jnp.float32)
    selected_value = jnp.where(spike_layer[:, None, None] & spike_cell, value_beneath, floor_value)
    return selected_value.astype(jnp.float32)


def with_ends(drawn, own_key, smallest, high):
    longest = drawn.shape.index(max(drawn.shape))
    spots = []
    for shift in (0, 1):
        where = [jax.random.randint(jax.random.fold_in(own_key, axis), (), 0, length) for axis, length in enumerate(drawn.shape)]
        where[longest] = (where[longest] + shift) % drawn.shape[longest]
        spots.append(tuple(where))
    return drawn.at[spots[0]].set(smallest).at[spots[1]].set(high)


def level_of(stream_key, shape, pieces, low, high):
    def one(dim, shards_of):
        draws = jax.random.uniform(jax.random.fold_in(jax.random.fold_in(stream_key, 6), dim), (shards_of,), jnp.float32, low / len(pieces), high / len(pieces))
        return jnp.repeat(jnp.exp(draws), shape[dim] // shards_of).reshape((-1,) + (1,) * (len(shape) - dim - 1))

    factor_of = one(*pieces[0])
    for cut in pieces[1:]:
        factor_of = factor_of * one(*cut)
    return factor_of


def centred(key, shape, deviation, limit, cuts=(), kind=jnp.bfloat16):
    array = jax.random.normal(key, shape, jnp.float32) * deviation
    if len(cuts) > 0:
        array = level_of(key, shape, cuts, -0.22, 0.18) * array
    return jnp.clip(array, min=-limit, max=limit).astype(kind)


def setup_inputs(seed: int = 0) -> dict:
    arg_keys = jax.random.split(jax.random.key(seed), 5)
    return {
        "filtered": draw_filtered(jax.random.fold_in(arg_keys[4], 71), 0),
        "printed": jnp.clip(0.3 + 0.39999998 * jax.random.uniform(arg_keys[1], (DEPTH, ROWS, COLS), jnp.float32) ** level_of(arg_keys[1], (DEPTH, ROWS, COLS), ((0, 4), (1, 4), (2, 16)), -0.2, 0.2), 0.3, 0.7),
        "sensitivity": centred(arg_keys[2], (DEPTH, ROWS, COLS), 1.0, 6.0, ((0, 4), (1, 4), (2, 16)), jnp.float32),
        "passive": with_ends((jax.random.randint(arg_keys[3], (DEPTH, ROWS, COLS), 0, 8) < 1).astype(jnp.int32), jax.random.fold_in(arg_keys[3], 1), 0, 1),
    }


PENALTY = 40.0
EXPONENT = PENALTY + math.log(5.0) / math.log(0.5)
SMOOTH = 0.001

def support_terms(lower_plane, density, valid):
    members = (lower_plane[..., 1:-1, 1:-1], lower_plane[..., :-2, 1:-1], lower_plane[..., 2:, 1:-1], lower_plane[..., 1:-1, :-2], lower_plane[..., 1:-1, 2:])
    largest = members[0]
    for member in members[1:]:
        largest = jnp.maximum(largest, member)
    largest = jnp.where(valid, largest, 1.0)
    powers = [jnp.power(member / largest, PENALTY - 1.0) for member in members]
    total = powers[0] * (members[0] / largest)
    for power_term, member in zip(powers[1:], members[1:]):
        total = total + power_term * (member / largest)
    smooth_max = jnp.power(largest, PENALTY / EXPONENT) * jnp.power(total, 1.0 / EXPONENT)
    gap = density - smooth_max
    radical = jnp.sqrt(gap * gap + SMOOTH)
    weight_low = 0.5 * (1.0 - gap / radical)
    weight_high = 0.5 * (1.0 + gap / radical)
    factor = jnp.where(valid, weight_high * (PENALTY / EXPONENT) * smooth_max / (largest * total), 0.0)
    ratios = tuple((jnp.where(valid, power_term, 0.0) for power_term in powers))
    return (factor, ratios, weight_low)

def tent_pass(padded, dim, count):
    total = None
    for offset in range(-RADIUS, RADIUS + 1):
        sliced = lax.slice_in_dim(padded, RADIUS + offset, RADIUS + offset + count, axis=dim) * float(RADIUS + 1 - abs(offset))
        total = sliced if total is None else total + sliced
    return total

def axis_norm(start, count, extent):
    position = start + jnp.arange(count, dtype=jnp.int32)
    total = jnp.zeros((count,), jnp.float32)
    for offset in range(-RADIUS, RADIUS + 1):
        inside = ((position + offset >= 0) & (position + offset < extent)).astype(jnp.float32)
        total = total + inside * float(RADIUS + 1 - abs(offset))
    return total

def reference(filtered, printed, sensitivity, passive):

    def layer_step(sens_above, planes):
        lower_plane, density, extra = planes
        factor, ratios, weight_low = support_terms(jnp.pad(lower_plane, 1), density, True)
        scaled = sens_above * factor
        sens_below = extra + scaled * ratios[0] + jnp.pad(scaled * ratios[1], 1)[2:, 1:-1] + jnp.pad(scaled * ratios[2], 1)[:-2, 1:-1] + jnp.pad(scaled * ratios[3], 1)[1:-1, 2:] + jnp.pad(scaled * ratios[4], 1)[1:-1, :-2]
        return (sens_below, sens_above * weight_low)
    bottom, upper_terms = lax.scan(layer_step, sensitivity[-1], (printed[:-1], filtered[1:], sensitivity[:-1]), reverse=True)
    raw = jnp.concatenate([bottom[None], upper_terms], axis=0)
    depth_all, rows_all, cols_all = raw.shape
    norm_z = axis_norm(0, depth_all, depth_all)
    norm_y = axis_norm(0, rows_all, rows_all)
    norm_x = axis_norm(0, cols_all, cols_all)
    weighted = raw / (norm_z[:, None, None] * norm_y[None, :, None] * norm_x[None, None, :])
    along_z = tent_pass(jnp.pad(weighted, ((RADIUS, RADIUS), (0, 0), (0, 0))), 0, depth_all)
    along_y = tent_pass(jnp.pad(along_z, ((0, 0), (RADIUS, RADIUS), (0, 0))), 1, rows_all)
    smoothed = tent_pass(jnp.pad(along_y, ((0, 0), (0, 0), (RADIUS, RADIUS))), 2, cols_all)
    return jnp.where(passive > 0, 0.0, smoothed)
```

```python
import functools
import math

import jax
import jax.numpy as jnp
from jax import lax
from jax.experimental import pallas as pl
from jax.experimental.pallas import tpu as pltpu
from jax.sharding import PartitionSpec as P

RADIUS = 4
PENALTY = 40.0
EXPONENT = PENALTY + math.log(5.0) / math.log(0.5)
SMOOTH = 0.001
AXES = ("gz", "gy", "gx")
F32 = jnp.float32

GROUPS = ((13, 16, 24), (9, 13, 16), (3, 9, 16), (0, 3, 8))
PAD = 24
RING = 8


def strips_of(group):
    first, end, _ = GROUPS[group]
    strips, at = [], 0
    for layer in range(end - 1, first - 1, -1):
        for name in ("u", "v"):
            strips.append((name, layer, at, RADIUS + layer))
            at += RADIUS + layer
    if first == 0:
        for layer in range(16):
            strips.append(("w", layer, at, RADIUS))
            at += RADIUS
    assert at <= 128
    return strips


def send(value, dz, dy, dx):
    sizes = tuple(lax.axis_size(axis) for axis in AXES)
    pairs = []
    for z in range(sizes[0]):
        for y in range(sizes[1]):
            for x in range(sizes[2]):
                tz, ty, tx = z + dz, y + dy, x + dx
                if 0 <= tz < sizes[0] and 0 <= ty < sizes[1] and 0 <= tx < sizes[2]:
                    pairs.append(
                        ((z * sizes[1] + y) * sizes[2] + x, (tz * sizes[1] + ty) * sizes[2] + tx)
                    )
    return lax.ppermute(value, AXES, pairs)


def shape(*dims):
    return jax.ShapeDtypeStruct(dims, F32)


def call(kernel, outs, *args, scratch=(), cost=None):
    return pl.pallas_call(
        kernel,
        out_shape=outs,
        scratch_shapes=list(scratch),
        compiler_params=pltpu.CompilerParams(vmem_limit_bytes=56 * 1024 * 1024),
        name=kernel.func.__name__ if isinstance(kernel, functools.partial) else kernel.__name__,
    )(*args)


def lanes(rows):
    return lax.broadcasted_iota(jnp.int32, (rows, 128), 1)


def power40(p):
    x = p + p
    x2 = x * x
    x4 = x2 * x2
    x8 = x4 * x4
    x32 = x8 * x8
    x32 = x32 * x32
    return x32 * x8


def power39(p):
    x = p + p
    x2 = x * x
    x4 = x2 * x2
    x8 = x4 * x4
    x32 = x8 * x8
    x32 = x32 * x32
    return x32 * (x4 * (x2 * x))


def edges(p_ref, top_ref, bottom_ref, left_ref, right_ref, turned):
    lane = lanes(128)
    packed = jnp.zeros((128, 128), F32)
    for layer in range(16):
        top_ref[pl.ds(layer, 1), :] = p_ref[layer, pl.ds(0, 1), :]
        bottom_ref[pl.ds(layer, 1), :] = p_ref[layer, pl.ds(127, 1), :]
        moved = pltpu.roll(p_ref[layer], 2 * layer + 1, 1)
        packed = jnp.where((lane >> 1) == layer, moved, packed)
    turned[...] = packed.T
    right_ref[...] = turned[pl.ds(0, 16, stride=2), :]
    left_ref[...] = turned[pl.ds(1, 16, stride=2), :]


def norm_of(position, extent):
    def missing(k):
        k = jnp.maximum(k, 0)
        return (k * (k + 1)) >> 1

    return ((RADIUS + 1) ** 2 - missing(RADIUS - position) - missing(RADIUS - (extent - 1 - position))).astype(F32)


def terms(total, density, sens, p39):
    total = jnp.maximum(total, 1e-30)
    offset = PENALTY * math.log(2.0) / EXPONENT
    smax = jnp.exp(jnp.log(total) * (1.0 / EXPONENT) - offset)
    gap = density - smax
    half = 0.5 * gap * lax.rsqrt(gap * gap + SMOOTH)
    low = 0.5 - half
    top = (0.5 + half) * (2.0 * PENALTY / EXPONENT) * smax
    h = top / total
    return h * sens, h * p39, low, total / top


def plane_norms(sizes):
    row0 = lax.axis_index("gy") * 128
    col0 = lax.axis_index("gx") * 128
    rows = lax.broadcasted_iota(jnp.int32, (128, 128), 0) + row0
    cols = lax.broadcasted_iota(jnp.int32, (128, 128), 1) + col0
    return norm_of(rows, sizes[1] * 128) * norm_of(cols, sizes[2] * 128)


def terms_upper(
    sizes, p_ref, f_ref, s_ref, up_ref, down_ref, left_ref, right_ref, u_ref, v_ref, w_ref, above_ref, powers, turned
):
    lane = lanes(128)
    turned[...] = jnp.zeros((128, 128), F32)
    turned[pl.ds(0, 16, stride=2), :] = right_ref[...]
    turned[pl.ds(1, 16, stride=2), :] = left_ref[...]
    beside = power40(turned[...].T)
    norms = 1.0 / plane_norms(sizes)
    layer0 = lax.axis_index("gz") * 16
    for layer in range(16):
        own = power40(p_ref[layer])
        powers[pl.ds(8, 128), :] = own
        powers[pl.ds(7, 1), :] = power40(up_ref[pl.ds(layer, 1), :])
        powers[pl.ds(136, 1), :] = power40(down_ref[pl.ds(layer, 1), :])
        side = pltpu.roll(beside, (128 - (2 * layer + 1)) % 128, 1)
        right = jnp.where(lane == 127, side, pltpu.roll(own, 127, 1))
        left = jnp.where(lane == 0, side, pltpu.roll(own, 1, 1))
        total = (own + right) + left + (powers[pl.ds(7, 128), :] + powers[pl.ds(9, 128), :])
        if layer == 15:
            above_ref[...] = total
        else:
            k = layer + 1
            u, v, low, inverse = terms(total, f_ref[k], s_ref[k], power39(p_ref[k]))
            u_ref[k] = u
            v_ref[k] = v
            norm_z = norm_of(layer0 + k, sizes[0] * 16)
            w_ref[k] = low * inverse * (norms * (1.0 / norm_z))


def terms_lowest(sizes, p_ref, f_ref, s_ref, total_ref, u_ref, v_ref, w_ref):
    norms = 1.0 / plane_norms(sizes)
    layer0 = lax.axis_index("gz") * 16
    p39 = power39(p_ref[...])
    s = s_ref[...]
    u, v, low, inverse = terms(total_ref[...], f_ref[...], s, p39)
    ground = layer0 == 0
    norm_z = norm_of(layer0, sizes[0] * 16)
    u_ref[...] = jnp.where(ground, s, u)
    v_ref[...] = jnp.where(ground, p39, v)
    w_ref[...] = jnp.where(ground, 1.0, low * inverse) * (norms * (1.0 / norm_z))


def pack(group, u_ref, v_ref, w_ref, left_ref, right_ref, top_ref, bottom_ref):
    first, end, rows = GROUPS[group]
    lane = lanes(128)
    left = jnp.zeros((128, 128), F32)
    right = jnp.zeros((128, 128), F32)
    refs = {"u": u_ref, "v": v_ref, "w": w_ref}
    for place, (name, layer, at, width) in enumerate(strips_of(group)):
        ref = refs[name]
        if name != "w":
            index = layer - first
        else:
            index = layer
        moved = pltpu.roll(ref[index], at, 1) if at else ref[index]
        left = jnp.where((lane >= at) & (lane < at + width), moved, left)
        back = (at - width) % 128
        right = jnp.where((lane >= back) & (lane < back + width), moved, right)
        top_ref[place] = ref[index, pl.ds(0, rows), :]
        bottom_ref[place] = ref[index, pl.ds(128 - rows, rows), :]
    left_ref[...] = left
    right_ref[...] = right


def unpack(
    group, u_ref, v_ref, w_ref,
    left, right, top, bottom, top_left, top_right, bottom_left, bottom_right,
    *outs,
):
    first, end, rows = GROUPS[group]
    refs = {"u": u_ref, "v": v_ref, "w": w_ref}
    targets = dict(zip(("u", "v", "w"), outs))
    for name, target in targets.items():
        if name != "w":
            target[...] = jnp.zeros(target.shape, F32)
    for place, (name, layer, at, width) in enumerate(strips_of(group)):
        index = layer if name == "w" else layer - first
        pad = RING if name == "w" else PAD
        target = targets[name]
        target[index, pl.ds(pad, 128), pl.ds(0, 128)] = refs[name][index]
        target[index, pl.ds(pad - rows, rows), pl.ds(0, 128)] = top[place]
        target[index, pl.ds(pad + 128, rows), pl.ds(0, 128)] = bottom[place]
        for left_one, right_one, start, count in (
            (top_left, top_right, pad - rows, rows),
            (left, right, pad, 128),
            (bottom_left, bottom_right, pad + 128, rows),
        ):
            lane = lanes(count)
            both = jnp.where((lane >= at) & (lane < at + width), right_one[...], left_one[...])
            both = pltpu.roll(both, 128 - at, 1) if at else both
            both = jnp.where((lane < width) | (lane >= 128 - width), both, 0.0)
            target[index, pl.ds(start, count), pl.ds(128, 128)] = both


def five(value):
    rows = value.shape[0]
    return (value + pltpu.roll(value, 1, 1)) + pltpu.roll(value, 255, 1) + (
        pltpu.roll(value, 1, 0) + pltpu.roll(value, rows - 1, 0)
    )


def set_carry(carry, center, top, bottom, left, right, top_left, top_right, bottom_left, bottom_right, turned):
    lane = lanes(24)
    carry[pl.ds(24, 128), pl.ds(0, 128)] = center[...]
    carry[pl.ds(0, 24), pl.ds(0, 128)] = top[...]
    carry[pl.ds(152, 24), pl.ds(0, 128)] = bottom[...]
    carry[pl.ds(0, 24), pl.ds(128, 128)] = jnp.where(lane < 64, top_right[...], top_left[...])
    carry[pl.ds(152, 24), pl.ds(128, 128)] = jnp.where(lane < 64, bottom_right[...], bottom_left[...])
    turned[...] = jnp.zeros((128, 128), F32)
    turned[pl.ds(0, 24), :] = right[...]
    turned[pl.ds(104, 24), :] = left[...]
    carry[pl.ds(24, 128), pl.ds(128, 128)] = turned[...].T


def section(first, *refs):
    us, vs = refs[0:4], refs[4:8]
    refs = refs[8:]
    pieces = () if first else refs[:9]
    refs = refs[len(pieces):]
    center, top, bottom, left, right, carry, turned = refs
    if first:
        carry[...] = jnp.zeros((176, 256), F32)
    else:
        set_carry(carry, *pieces, turned)
    value = carry[...]
    for (begin, end, _), u_ref, v_ref in zip(GROUPS, us, vs):
        def step(i, value):
            at = end - 1 - begin - i
            return u_ref[at] + v_ref[at] * five(value)
        value = lax.fori_loop(0, end - begin, step, value)
    carry[...] = value
    center[...] = carry[pl.ds(24, 128), pl.ds(0, 128)]
    top[...] = carry[pl.ds(24, 24), pl.ds(0, 128)]
    bottom[...] = carry[pl.ds(128, 24), pl.ds(0, 128)]
    turned[...] = carry[pl.ds(24, 128), pl.ds(0, 128)].T
    left[...] = turned[pl.ds(0, 24), :]
    right[...] = turned[pl.ds(104, 24), :]


def tent_rows(ref, start):
    total = ref[pl.ds(start, 128), :] * 5.0
    for offset in range(1, RADIUS + 1):
        total = total + (ref[pl.ds(start - offset, 128), :] + ref[pl.ds(start + offset, 128), :]) * (5.0 - offset)
    return total


def tent_cols(value):
    total = value * 5.0
    for offset in range(1, RADIUS + 1):
        total = total + (pltpu.roll(value, offset, 1) + pltpu.roll(value, 256 - offset, 1)) * (5.0 - offset)
    return total


def last_section(*refs):
    us, vs = refs[0:4], refs[4:8]
    w_ref = refs[8]
    pieces = refs[9:18]
    out_ref, carry, turned, weighted = refs[18:]
    set_carry(carry, *pieces, turned)
    value = carry[...]
    for (begin, end, _), u_ref, v_ref in zip(GROUPS, us, vs):
        def step(i, value):
            at = end - 1 - begin - i
            value = u_ref[at] + v_ref[at] * five(value)
            weighted[...] = value[PAD - RING:PAD + 128 + RING] * w_ref[begin + at]
            out_ref[begin + at] = tent_cols(tent_rows(weighted, RING))[:, :128]
            return value
        value = lax.fori_loop(0, end - begin, step, value)


def finish(own_ref, below_ref, above_ref, passive_ref, out_ref):
    def layer(k):
        if k < 0:
            return below_ref[k + RADIUS]
        if k >= 16:
            return above_ref[k - 16]
        return own_ref[k]

    for k in range(16):
        total = layer(k) * 5.0
        for offset in range(1, RADIUS + 1):
            total = total + (layer(k - offset) + layer(k + offset)) * (5.0 - offset)
        out_ref[k] = jnp.where(passive_ref[k] > 0, 0.0, total)


def per_device(filtered, printed, sensitivity, passive):
    sizes = tuple(lax.axis_size(axis) for axis in AXES)
    plane = shape(128, 128)
    edge = shape(16, 128)
    top, bottom, left, right = call(edges, [edge] * 4, printed, scratch=[pltpu.VMEM((128, 128), F32)])
    up = send(bottom, 0, 1, 0)
    down = send(top, 0, -1, 0)
    from_left = send(right, 0, 0, 1)
    from_right = send(left, 0, 0, -1)
    block = shape(16, 128, 128)
    u, v, w, above = call(
        functools.partial(terms_upper, sizes),
        [block, block, block, plane],
        printed, filtered, sensitivity, up, down, from_left, from_right,
        scratch=[pltpu.VMEM((144, 128), F32), pltpu.VMEM((128, 128), F32)],
    )
    total0 = send(above, 1, 0, 0)
    u0, v0, w0 = call(
        functools.partial(terms_lowest, sizes), [plane] * 3, printed[0], filtered[0], sensitivity[0], total0
    )
    u = u.at[0].set(u0)
    v = v.at[0].set(v0)
    w = w.at[0].set(w0)
    us, vs, w_ext = [], [], None
    for group, (first, end, rows) in enumerate(GROUPS):
        count = len(strips_of(group))
        strip = shape(count, rows, 128)
        args = (u[first:end], v[first:end], w)
        left, right, top, bottom = call(functools.partial(pack, group), [plane, plane, strip, strip], *args)
        outs = [shape(end - first, 176, 256)] * 2
        if first == 0:
            outs = outs + [shape(16, 144, 256)]
        got = call(
            functools.partial(unpack, group),
            outs,
            *args,
            send(right, 0, 0, 1),
            send(left, 0, 0, -1),
            send(bottom, 0, 1, 0),
            send(top, 0, -1, 0),
            send(right[128 - rows:], 0, 1, 1),
            send(left[128 - rows:], 0, 1, -1),
            send(right[:rows], 0, -1, 1),
            send(left[:rows], 0, -1, -1),
        )
        us.append(got[0])
        vs.append(got[1])
        if first == 0:
            w_ext = got[2]
    strip = shape(24, 128)
    scratch = [pltpu.VMEM((176, 256), F32), pltpu.VMEM((128, 128), F32)]
    pieces = ()
    for step in range(sizes[0]):
        if step < sizes[0] - 1:
            center, top, bottom, left, right = call(
                functools.partial(section, step == 0),
                [plane, strip, strip, strip, strip],
                *us, *vs, *pieces,
                scratch=scratch,
            )
            pieces = (
                send(center, -1, 0, 0),
                send(bottom, -1, 1, 0),
                send(top, -1, -1, 0),
                send(right, -1, 0, 1),
                send(left, -1, 0, -1),
                send(bottom, -1, 1, 1),
                send(bottom, -1, 1, -1),
                send(top, -1, -1, 1),
                send(top, -1, -1, -1),
            )
    smoothed = call(
        last_section, block, *us, *vs, w_ext, *pieces,
        scratch=scratch + [pltpu.VMEM((144, 256), F32)],
    )
    below = send(smoothed[16 - RADIUS:], 1, 0, 0)
    over = send(smoothed[:RADIUS], -1, 0, 0)
    return call(finish, block, smoothed, below, over, passive)


def solution(mesh):
    spec = P(*AXES)
    return jax.shard_map(
        per_device, mesh=mesh, in_specs=(spec,) * 4, out_specs=spec, check_vma=False
    )
```

```python
import functools
import math

import jax
import jax.numpy as jnp
from jax import lax
from jax.experimental import pallas as pl
from jax.experimental.pallas import tpu as pltpu
from jax.sharding import PartitionSpec as P

RADIUS = 4
PENALTY = 40.0
EXPONENT = PENALTY + math.log(5.0) / math.log(0.5)
SMOOTH = 0.001
AXES = ("gz", "gy", "gx")
F32 = jnp.float32

GROUPS = ((13, 16, 24), (9, 13, 16), (3, 9, 16), (0, 3, 8))
PLANE = 288
LAYERS = 16


def strips_of(group):
    first, end, _ = GROUPS[group]
    strips, at = [], 0
    for layer in range(end - 1, first - 1, -1):
        for _ in range(2):
            strips.append((at, RADIUS + layer))
            at += RADIUS + layer
    if first == 0:
        for layer in range(LAYERS):
            strips.append((at, RADIUS))
            at += RADIUS
    assert at <= 128
    return strips


def moved(value, where):
    sizes = tuple(lax.axis_size(axis) for axis in AXES)
    pairs = []
    for z in range(sizes[0]):
        for y in range(sizes[1]):
            for x in range(sizes[2]):
                to = where(z, y, x)
                if to is not None and all(0 <= t < n for t, n in zip(to, sizes)):
                    pairs.append(((z * sizes[1] + y) * sizes[2] + x, (to[0] * sizes[1] + to[1]) * sizes[2] + to[2]))
    return lax.ppermute(value, AXES, pairs)


def shape(*dims):
    return jax.ShapeDtypeStruct(dims, F32)


def call(kernel, outs, *args, scratch=(), in_specs=None, **params):
    name = kernel.func.__name__ if isinstance(kernel, functools.partial) else kernel.__name__
    more = {} if in_specs is None else {"in_specs": in_specs}
    return pl.pallas_call(
        kernel,
        out_shape=outs,
        scratch_shapes=list(scratch),
        compiler_params=pltpu.CompilerParams(vmem_limit_bytes=40 * 1024 * 1024),
        name=name,
        **more,
    )(*args)


def lanes(rows):
    return lax.broadcasted_iota(jnp.int32, (rows, 128), 1)


def core():
    return lax.axis_index("gy") & 1


def seam():
    return lax.axis_index("gy") >> 1


def aligned(value, to):
    return pl.multiple_of(value, to)


def power40(p):
    x = p + p
    x2 = x * x
    x4 = x2 * x2
    x8 = x4 * x4
    x32 = x8 * x8
    x32 = x32 * x32
    return x32 * x8


def power39(p):
    x = p + p
    x2 = x * x
    x4 = x2 * x2
    x8 = x4 * x4
    x32 = x8 * x8
    x32 = x32 * x32
    return x32 * (x4 * (x2 * x))


def edges(p_ref, inner_ref, outer_ref, left_ref, right_ref, turned):
    lane = lanes(128)
    c = core()
    packed = jnp.zeros((128, 128), F32)
    for layer in range(LAYERS):
        inner_ref[pl.ds(layer, 1), :] = p_ref[layer, pl.ds(127 * (1 - c), 1), :]
        outer_ref[pl.ds(layer, 1), :] = p_ref[layer, pl.ds(127 * c, 1), :]
        rolled = pltpu.roll(p_ref[layer], 2 * layer + 1, 1)
        packed = jnp.where((lane >> 1) == layer, rolled, packed)
    turned[...] = packed.T
    right_ref[...] = turned[pl.ds(0, 16, stride=2), :]
    left_ref[...] = turned[pl.ds(1, 16, stride=2), :]


def norm_of(position, extent):
    def missing(k):
        k = jnp.maximum(k, 0)
        return (k * (k + 1)) >> 1

    return ((RADIUS + 1) ** 2 - missing(RADIUS - position) - missing(RADIUS - (extent - 1 - position))).astype(F32)


def terms(total, density, sens, p39):
    total = jnp.maximum(total, 1e-30)
    offset = PENALTY * math.log(2.0) / EXPONENT
    smax = jnp.exp(jnp.log(total) * (1.0 / EXPONENT) - offset)
    gap = density - smax
    half = 0.5 * gap * lax.rsqrt(gap * gap + SMOOTH)
    low = 0.5 - half
    top = (0.5 + half) * (2.0 * PENALTY / EXPONENT) * smax
    h = top / total
    return h * sens, h * p39, low, total / top


def plane_norms(sizes):
    row0 = lax.axis_index("gy") * 128
    col0 = lax.axis_index("gx") * 128
    rows = lax.broadcasted_iota(jnp.int32, (128, 128), 0) + row0
    cols = lax.broadcasted_iota(jnp.int32, (128, 128), 1) + col0
    return norm_of(rows, sizes[1] * 128) * norm_of(cols, sizes[2] * 128)


def terms_upper(
    sizes, p_ref, f_ref, s_ref, inner_ref, outer_ref, left_ref, right_ref,
    uv0_ref, uv1_ref, uv2_ref, uv3_ref, y0_ref, y1_ref, y2_ref, above_ref, powers, turned,
):
    c = core()
    lane = lanes(128)
    turned[...] = jnp.zeros((128, 128), F32)
    turned[pl.ds(0, 16, stride=2), :] = right_ref[...]
    turned[pl.ds(1, 16, stride=2), :] = left_ref[...]
    beside = power40(turned[...].T)
    norms = 1.0 / plane_norms(sizes)
    layer0 = lax.axis_index("gz") * LAYERS
    uvs = (uv0_ref, uv1_ref, uv2_ref, uv3_ref)
    ys = (y0_ref, y1_ref, y2_ref)
    for layer in range(LAYERS):
        own = power40(p_ref[layer])
        powers[pl.ds(8, 128), :] = own
        powers[pl.ds(7 + 129 * (1 - c), 1), :] = power40(inner_ref[pl.ds(layer, 1), :])
        powers[pl.ds(7 + 129 * c, 1), :] = power40(outer_ref[pl.ds(layer, 1), :])
        side = pltpu.roll(beside, (128 - (2 * layer + 1)) % 128, 1)
        right = jnp.where(lane == 127, side, pltpu.roll(own, 127, 1))
        left = jnp.where(lane == 0, side, pltpu.roll(own, 1, 1))
        total = (own + right) + left + (powers[pl.ds(7, 128), :] + powers[pl.ds(9, 128), :])
        if layer == LAYERS - 1:
            above_ref[...] = total
            continue
        k = layer + 1
        u, v, low, inverse = terms(total, f_ref[k], s_ref[k], power39(p_ref[k]))
        norm_z = norm_of(layer0 + k, sizes[0] * LAYERS)
        uv3_ref[6 + k] = low * inverse * (norms * (1.0 / norm_z))
        for group, (first, end, rows) in enumerate(GROUPS):
            if first <= k < end:
                place = 2 * (end - 1 - k)
                uvs[group][place] = u
                uvs[group][place + 1] = v
                if group < 3:
                    start = aligned(c * (128 - rows), 8)
                    for i in range(2):
                        ys[group][place + i] = uvs[group][place + i, pl.ds(start, rows), :]
    uv3_ref[4] = jnp.zeros((128, 128), F32)
    uv3_ref[5] = jnp.zeros((128, 128), F32)
    uv3_ref[6] = jnp.zeros((128, 128), F32)


def terms_lowest(sizes, p_ref, f_ref, s_ref, total_ref, uvw_ref, out_ref, y_ref):
    norms = 1.0 / plane_norms(sizes)
    layer0 = lax.axis_index("gz") * LAYERS
    p39 = power39(p_ref[...])
    s = s_ref[...]
    u, v, low, inverse = terms(total_ref[...], f_ref[...], s, p39)
    ground = layer0 == 0
    norm_z = norm_of(layer0, sizes[0] * LAYERS)
    out_ref[...] = uvw_ref[...]
    out_ref[4] = jnp.where(ground, s, u)
    out_ref[5] = jnp.where(ground, p39, v)
    out_ref[6] = jnp.where(ground, 1.0, low * inverse) * (norms * (1.0 / norm_z))
    rows = GROUPS[3][2]
    y_ref[...] = out_ref[:, pl.ds(aligned(core() * (128 - rows), 8), rows), :]


def regions(rows):
    c = core()
    return ((aligned(c * 128, 128), 128), (aligned((1 - c) * 128, 128), 128), (256, rows))


def pack(group, own_ref, other_ref, halo_ref, slab_ref):
    rows = GROUPS[group][2]
    c = core()
    for ref, (start, count) in zip((own_ref, other_ref, halo_ref), regions(rows)):
        lane = lanes(count)
        slab = jnp.zeros((count, 128), F32)
        for place, (at, width) in enumerate(strips_of(group)):
            rolled = pltpu.roll(ref[place], at, 1) if at else ref[place]
            begin = (at + 128 - c * width) & 127
            slab = jnp.where(((lane - begin) & 127) < width, rolled, slab)
        slab_ref[pl.ds(start, count), :] = slab


def assemble(group, own_ref, other_ref, halo_ref, slab_ref, uv_ref, *w_refs):
    first, end, rows = GROUPS[group]
    c = core()
    here = regions(rows)
    to = aligned(256 + seam() * (32 - rows), 8)
    for place, (at, width) in enumerate(strips_of(group)):
        target = uv_ref if place < 2 * (end - first) else w_refs[0]
        index = place if place < 2 * (end - first) else place - 2 * (end - first)
        target[index, pl.ds(256, 32), :] = jnp.zeros((32, 128), F32)
        for ref, (start, count), into in zip(
            (own_ref, other_ref, halo_ref), here, (here[0][0], here[1][0], to)
        ):
            lane = lanes(count)
            got = slab_ref[pl.ds(start, count), :]
            got = pltpu.roll(got, 128 - at, 1) if at else got
            begin = (1 - c) * (128 - width)
            outer = (lane >= begin) & (lane < begin + width)
            target[index, pl.ds(into, count), :] = jnp.where(outer, got, ref[place])


def five(value):
    return (value + pltpu.roll(value, 1, 1)) + pltpu.roll(value, 127, 1) + (
        pltpu.roll(value, 1, 0) + pltpu.roll(value, PLANE - 1, 0)
    )


def set_carry(carry, main_ref, other_ref, outer_ref, halo_ref, halo_other_ref, halo_outer_ref):
    c = core()
    lane = lanes(64)
    mine = (lane >> 6) == c
    for i in range(4):
        rows = pl.ds(64 * (i % 2), 64)
        own, other = main_ref[rows, :], other_ref[rows, :]
        if i < 2:
            value = jnp.where(mine, own, other)
        else:
            value = pltpu.roll(jnp.where(mine, other, own), 64, 1)
        outer = pltpu.roll(outer_ref[...], (128 - 32 * i) % 128, 1) if i else outer_ref[...]
        begin = (1 - c) * 108
        value = jnp.where((lane >= begin) & (lane < begin + 20), outer, value)
        carry[pl.ds(64 * i, 64), :] = value
    lane = lanes(24)
    value = jnp.where((lane >> 6) == c, halo_ref[...], halo_other_ref[...])
    begin = (1 - c) * 108
    value = jnp.where((lane >= begin) & (lane < begin + 20), halo_outer_ref[...], value)
    carry[pl.ds(256, 32), :] = jnp.zeros((32, 128), F32)
    carry[pl.ds(aligned(256 + 8 * seam(), 8), 24), :] = value


def section(active, *refs):
    uv_refs, refs = refs[:4], refs[4:]
    pieces = refs[:6] if len(refs) > 6 else ()
    refs = refs[len(pieces):]
    if len(refs) == 5:
        layers_ref, main_ref, outer_ref, halo_ref, carry = refs
    else:
        layers_ref, carry = refs
        main_ref = None

    @pl.when(lax.axis_index("gz") == active)
    def _():
        if pieces:
            set_carry(carry, *pieces)
            value = carry[...]
        else:
            value = jnp.zeros((PLANE, 128), F32)
        for (first, end, _), uv_ref in zip(GROUPS, uv_refs):
            def step(i, value):
                value = uv_ref[2 * i] + uv_ref[2 * i + 1] * five(value)
                layers_ref[end - 1 - i] = value
                return value
            value = lax.fori_loop(0, end - first, step, value)
        if main_ref is None:
            return
        c = core()
        lane = lanes(128)
        bottom = layers_ref.at[0]
        mine = (lane >> 6) == c
        main_ref[...] = jnp.where(mine, bottom[pl.ds(0, 128), :], pltpu.roll(bottom[pl.ds(128, 128), :], 64, 1))
        lane = lanes(64)
        slab = jnp.zeros((64, 128), F32)
        for i in range(4):
            rolled = bottom[pl.ds(64 * i, 64), :]
            rolled = pltpu.roll(rolled, 32 * i, 1) if i else rolled
            begin = (32 * i + 128 - c * 32) & 127
            slab = jnp.where(((lane - begin) & 127) < 32, rolled, slab)
        outer_ref[...] = slab
        halo_ref[...] = bottom[pl.ds(aligned((1 - seam()) * 232, 8), 24), :]


def smooth(active, layers_ref, w_ref, out_ref, give_ref, top_ref, bottom_ref, weighted):
    @pl.when(lax.axis_index("gz") == active)
    def _():
        c = core()
        lane = lanes(128)
        mine = (lane >> 6) == c

        def layer(k, _):
            weighted[pl.ds(8, PLANE), :] = layers_ref[k] * w_ref[k]
            weighted[pl.ds(0, 8), :] = weighted[pl.ds(PLANE, 8), :]
            halves = []
            for half in range(2):
                start = 8 + 128 * half
                total = weighted[pl.ds(start, 128), :] * 5.0
                for offset in range(1, RADIUS + 1):
                    total = total + (
                        weighted[pl.ds(start - offset, 128), :] + weighted[pl.ds(start + offset, 128), :]
                    ) * (5.0 - offset)
                value = total * 5.0
                for offset in range(1, RADIUS + 1):
                    value = value + (pltpu.roll(total, offset, 1) + pltpu.roll(total, 128 - offset, 1)) * (5.0 - offset)
                halves.append(value)
            out_ref[k] = jnp.where(mine, halves[0], pltpu.roll(halves[1], 64, 1))
            return 0

        lax.fori_loop(0, LAYERS, layer, 0)
        top_ref[...] = out_ref[pl.ds(LAYERS - RADIUS, RADIUS)]
        bottom_ref[...] = out_ref[pl.ds(0, RADIUS)]
        give(out_ref, give_ref)


def give(from_ref, to_ref):
    count = to_ref.shape[0]
    low = (lanes(128) >> 6) == 0
    for k in range(count):
        to_ref[k] = jnp.where(low, pltpu.roll(from_ref[k + count], 64, 1), from_ref[k])


def finish(depth, *refs):
    (q_refs, got_refs, below_refs, below_got_refs, above_refs, above_got_refs) = (
        refs[0:depth], refs[depth:2 * depth],
        refs[2 * depth:3 * depth - 1], refs[3 * depth - 1:4 * depth - 2],
        refs[4 * depth - 2:5 * depth - 3], refs[5 * depth - 3:6 * depth - 4],
    )
    passive_ref, out_ref, packed, got, sem = refs[6 * depth - 4:]
    gz = lax.axis_index("gz")
    c = core()
    low = (lanes(128) >> 6) == 0

    def load(active, pairs):
        @pl.when(gz == active)
        def _():
            copies = [pltpu.make_async_copy(src, dst, sem.at[i]) for i, (src, dst) in enumerate(pairs)]
            for copy in copies:
                copy.start()
            for copy in copies:
                copy.wait()

    zeros = jnp.zeros((RADIUS, 128, 128), F32)

    @pl.when(gz == 0)
    def _():
        packed[pl.ds(0, RADIUS)] = zeros
        got[pl.ds(0, RADIUS // 2)] = zeros[:RADIUS // 2]

    @pl.when(gz == depth - 1)
    def _():
        packed[pl.ds(LAYERS + RADIUS, RADIUS)] = zeros
        got[pl.ds(LAYERS // 2 + RADIUS // 2, RADIUS // 2)] = zeros[:RADIUS // 2]

    for z in range(depth):
        pairs = [
            (q_refs[z], packed.at[pl.ds(RADIUS, LAYERS)]),
            (got_refs[z], got.at[pl.ds(RADIUS // 2, LAYERS // 2)]),
        ]
        if z > 0:
            pairs += [
                (below_refs[z - 1], packed.at[pl.ds(0, RADIUS)]),
                (below_got_refs[z - 1], got.at[pl.ds(0, RADIUS // 2)]),
            ]
        if z < depth - 1:
            pairs += [
                (above_refs[z], packed.at[pl.ds(LAYERS + RADIUS, RADIUS)]),
                (above_got_refs[z], got.at[pl.ds(LAYERS // 2 + RADIUS // 2, RADIUS // 2)]),
            ]
        load(z, pairs)

    mine = low == (c == 0)

    def layer(k):
        if k < RADIUS:
            base, count, i = 0, RADIUS // 2, k
        elif k < RADIUS + LAYERS:
            base, count, i = RADIUS // 2, LAYERS // 2, k - RADIUS
        else:
            base, count, i = RADIUS // 2 + LAYERS // 2, RADIUS // 2, k - RADIUS - LAYERS
        own = packed[k]
        other = got[base + i % count]
        own = jnp.where(c == 0, own, pltpu.roll(own, 64, 1))
        first = i < count
        upper = other if first else pltpu.roll(other, 64, 1)
        value = jnp.where(c == 0, upper, pltpu.roll(upper, 64, 1))
        return jnp.where(mine, own, value)

    for k in range(LAYERS + 2 * RADIUS):
        packed[k] = layer(k)
    for k in range(LAYERS):
        total = packed[k + RADIUS] * 5.0
        for offset in range(1, RADIUS + 1):
            total = total + (packed[k + RADIUS - offset] + packed[k + RADIUS + offset]) * (5.0 - offset)
        out_ref[k] = jnp.where(passive_ref[k] > 0, 0.0, total)


def to_other(value):
    return moved(value, lambda z, y, x: (z, y ^ 1, x))


def per_device(filtered, printed, sensitivity, passive):
    sizes = tuple(lax.axis_size(axis) for axis in AXES)
    depth = sizes[0]
    plane = shape(128, 128)
    edge = shape(16, 128)
    inner, outer, left, right = call(edges, [edge] * 4, printed, scratch=[pltpu.VMEM((128, 128), F32)])

    def across(z, y, x):
        return (z, y ^ 3, x) if y in (1, 2) else None

    def beside(z, y, x):
        return (z, y ^ 1, x + (1 if y & 1 else -1))

    inner = to_other(inner)
    outer = moved(outer, across)
    from_left = moved(right, lambda z, y, x: (z, y, x + 1))
    from_right = moved(left, lambda z, y, x: (z, y, x - 1))
    counts = [len(strips_of(group)) for group in range(4)]
    blocks = [shape(count, 128, 128) for count in counts]
    halos = [shape(count, rows, 128) for count, (_, _, rows) in zip(counts, GROUPS)]
    *owns, y0, y1, y2, above = call(
        functools.partial(terms_upper, sizes),
        blocks + halos[:3] + [plane],
        printed, filtered, sensitivity, inner, outer, from_left, from_right,
        scratch=[pltpu.VMEM((144, 128), F32), pltpu.VMEM((128, 128), F32)],
    )
    total0 = moved(above, lambda z, y, x: (z + 1, y, x))
    owns[3], y3 = call(
        functools.partial(terms_lowest, sizes), [blocks[3], halos[3]],
        printed[0], filtered[0], sensitivity[0], total0, owns[3],
    )
    uvs, ws = [], None
    for group, (y, own) in enumerate(zip((y0, y1, y2, y3), owns)):
        first, end, rows = GROUPS[group]
        other = to_other(own)
        got = moved(y, across)
        shared = moved(got, lambda z, y, x: (z, y ^ 1, x) if y in (1, 2) else None)
        halo = jnp.where((lax.axis_index("gy") == 1) | (lax.axis_index("gy") == 2), got, shared)
        slab = call(functools.partial(pack, group), shape(256 + rows, 128), own, other, halo)
        slab = moved(slab, beside)
        outs = [shape(2 * (end - first), PLANE, 128)]
        if first == 0:
            outs = outs + [shape(LAYERS, PLANE, 128)]
        outs = call(functools.partial(assemble, group), outs, own, other, halo, slab)
        uvs.append(outs[0])
        if first == 0:
            ws = outs[1]
    pieces = ()
    stack = shape(LAYERS, PLANE, 128)
    quarter = shape(RADIUS, 128, 128)
    tiles, gots, belows, below_gots, aboves, above_gots = [], [], [], [], [], []
    for active in range(depth - 1, -1, -1):
        outs = [stack]
        if active > 0:
            outs = outs + [plane, shape(64, 128), shape(24, 128)]
        layers, *ends = call(
            functools.partial(section, active), outs, *uvs, *pieces, scratch=[pltpu.VMEM((PLANE, 128), F32)]
        )
        if active > 0:
            main, side, strip = ends

            def down(where):
                def to(z, y, x):
                    _, ty, tx = where(z, y, x)
                    return (z - 1, ty, tx) if z == active else None
                return to

            def over(z, y, x):
                return (z, y ^ 2, x)

            def corner(z, y, x):
                _, ty, tx = beside(z, y, x)
                return (z, ty ^ 2, tx)

            def sibling(z, y, x):
                return (z, y ^ 1, x) if z == active - 1 else None

            main = moved(main, down(lambda z, y, x: (z, y, x)))
            halo = moved(strip, down(over))
            pieces = (
                main,
                moved(main, sibling),
                moved(side, down(beside)),
                halo,
                moved(halo, sibling),
                moved(strip, down(corner)),
            )
        tile, given, top, bottom = call(
            functools.partial(smooth, active),
            [shape(LAYERS, 128, 128), shape(LAYERS // 2, 128, 128), quarter, quarter],
            layers, ws,
            scratch=[pltpu.VMEM((PLANE + 8, 128), F32)],
        )
        tiles.insert(0, tile)
        gots.insert(0, moved(given, lambda z, y, x: (z, y ^ 1, x) if z == active else None))
        if active < depth - 1:
            below = moved(top, lambda z, y, x: (z + 1, y, x) if z == active else None)
            belows.insert(0, below)
            half = call(give_part, shape(RADIUS // 2, 128, 128), below)
            below_gots.insert(0, moved(half, lambda z, y, x: (z, y ^ 1, x) if z == active + 1 else None))
        if active > 0:
            above = moved(bottom, lambda z, y, x: (z - 1, y, x) if z == active else None)
            aboves.insert(0, above)
            half = call(give_part, shape(RADIUS // 2, 128, 128), above)
            above_gots.insert(0, moved(half, lambda z, y, x: (z, y ^ 1, x) if z == active - 1 else None))
    hbm = pl.BlockSpec(memory_space=pl.ANY)
    operands = tiles + gots + belows + below_gots + aboves + above_gots
    return call(
        functools.partial(finish, depth),
        shape(LAYERS, 128, 128),
        *operands,
        passive,
        in_specs=[hbm] * len(operands) + [pl.BlockSpec(memory_space=pltpu.VMEM)],
        scratch=[
            pltpu.VMEM((LAYERS + 2 * RADIUS, 128, 128), F32),
            pltpu.VMEM((LAYERS // 2 + RADIUS, 128, 128), F32),
            pltpu.SemaphoreType.DMA((6,)),
        ],
    )


def give_part(from_ref, to_ref):
    give(from_ref, to_ref)


def solution(mesh):
    spec = P(*AXES)
    return jax.shard_map(
        per_device, mesh=mesh, in_specs=(spec,) * 4, out_specs=spec, check_vma=False
    )
```

```python
import functools
import math

import jax
import jax.numpy as jnp
from jax import lax
from jax.experimental import pallas as pl
from jax.experimental.pallas import tpu as pltpu
from jax.sharding import PartitionSpec as P

RADIUS = 4
PENALTY = 40.0
EXPONENT = PENALTY + math.log(5.0) / math.log(0.5)
SMOOTH = 0.001
AXES = ("gz", "gy", "gx")
F32 = jnp.float32

LAYERS = 16
PLANE = 288
SLABS = ((15, 14, 13, 6), (12, 11, 10, 9, 2), (8, 7, 5, 4, 3, 1, 0))
SLAB_ROWS = 3 * 128 + 64
CORNER_ROWS = 3 * 24 + 8


def width_of(layer):
    return RADIUS + layer


def rows_of(layer):
    return -(-width_of(layer) // 8) * 8


MICROSECONDS = {"terms_upper": 2.7, "assemble": 2.5, "section": 2.6, "smooth": 4.0, "finish": 3.0, "ends": 1.0}


def strips():
    out = []
    for slab, layers in enumerate(SLABS):
        at = 0
        for layer in layers:
            for name in ("u", "v"):
                out.append((name, layer, slab, at))
                at += width_of(layer)
        assert at <= 128
    return out


def row_places():
    places, at = {}, 0
    for layer in range(LAYERS):
        for name in ("u", "v"):
            places[name, layer] = (at, rows_of(layer))
            at += rows_of(layer)
    for layer in range(LAYERS):
        places["w", layer] = (at, 8)
        at += 8
    return places, at


ROW_PLACES, ROW_TOTAL = row_places()


def moved(value, where):
    sizes = tuple(lax.axis_size(axis) for axis in AXES)
    pairs = []
    for z in range(sizes[0]):
        for y in range(sizes[1]):
            for x in range(sizes[2]):
                to = where(z, y, x)
                if to is not None and all(0 <= t < n for t, n in zip(to, sizes)):
                    pairs.append(((z * sizes[1] + y) * sizes[2] + x, (to[0] * sizes[1] + to[1]) * sizes[2] + to[2]))
    return lax.ppermute(value, AXES, pairs)


def shape(*dims):
    return jax.ShapeDtypeStruct(dims, F32)


def call(kernel, outs, *args, scratch=(), in_specs=None, **params):
    name = kernel.func.__name__ if isinstance(kernel, functools.partial) else kernel.__name__
    more = {} if in_specs is None else {"in_specs": in_specs}
    return pl.pallas_call(
        kernel,
        out_shape=outs,
        scratch_shapes=list(scratch),
        compiler_params=pltpu.CompilerParams(vmem_limit_bytes=40 * 1024 * 1024),
        cost_estimate=pl.CostEstimate(flops=0, bytes_accessed=int(MICROSECONDS.get(name, 0.5) * 3e6), transcendentals=0),
        name=name,
        **more,
    )(*args)


def lanes(rows):
    return lax.broadcasted_iota(jnp.int32, (rows, 128), 1)


def core():
    return lax.axis_index("gy") & 1


def seam():
    return lax.axis_index("gy") >> 1


def aligned(value, to):
    return pl.multiple_of(value, to)


def power40(p):
    x = p + p
    x2 = x * x
    x4 = x2 * x2
    x8 = x4 * x4
    x32 = x8 * x8
    x32 = x32 * x32
    return x32 * x8


def power39(p):
    x = p + p
    x2 = x * x
    x4 = x2 * x2
    x8 = x4 * x4
    x32 = x8 * x8
    x32 = x32 * x32
    return x32 * (x4 * (x2 * x))


def edges(p_ref, inner_ref, outer_ref, left_ref, right_ref, turned):
    lane = lanes(128)
    c = core()
    packed = jnp.zeros((128, 128), F32)
    for layer in range(LAYERS):
        inner_ref[pl.ds(layer, 1), :] = p_ref[layer, pl.ds(127 * (1 - c), 1), :]
        outer_ref[pl.ds(layer, 1), :] = p_ref[layer, pl.ds(127 * c, 1), :]
        rolled = pltpu.roll(p_ref[layer], 2 * layer + 1, 1)
        packed = jnp.where((lane >> 1) == layer, rolled, packed)
    turned[...] = packed.T
    right_ref[...] = turned[pl.ds(0, 16, stride=2), :]
    left_ref[...] = turned[pl.ds(1, 16, stride=2), :]


def norm_of(position, extent):
    def missing(k):
        k = jnp.maximum(k, 0)
        return (k * (k + 1)) >> 1

    return ((RADIUS + 1) ** 2 - missing(RADIUS - position) - missing(RADIUS - (extent - 1 - position))).astype(F32)


def terms(total, density, sens, p39):
    total = jnp.maximum(total, 1e-30)
    offset = PENALTY * math.log(2.0) / EXPONENT
    smax = jnp.exp(jnp.log(total) * (1.0 / EXPONENT) - offset)
    gap = density - smax
    half = 0.5 * gap * lax.rsqrt(gap * gap + SMOOTH)
    low = 0.5 - half
    top = (0.5 + half) * (2.0 * PENALTY / EXPONENT) * smax
    h = top / total
    return h * sens, h * p39, low, total / top


def plane_norms(sizes):
    row0 = lax.axis_index("gy") * 128
    col0 = lax.axis_index("gx") * 128
    rows = lax.broadcasted_iota(jnp.int32, (128, 128), 0) + row0
    cols = lax.broadcasted_iota(jnp.int32, (128, 128), 1) + col0
    return norm_of(rows, sizes[1] * 128) * norm_of(cols, sizes[2] * 128)


def neighbours(p, layer, inner_ref, outer_ref, beside, powers):
    c = core()
    lane = lanes(128)
    own = power40(p)
    powers[pl.ds(8, 128), :] = own
    powers[pl.ds(7 + 129 * (1 - c), 1), :] = power40(inner_ref[pl.ds(layer, 1), :])
    powers[pl.ds(7 + 129 * c, 1), :] = power40(outer_ref[pl.ds(layer, 1), :])
    side = pltpu.roll(beside, (128 - (2 * layer + 1)) % 128, 1)
    right = jnp.where(lane == 127, side, pltpu.roll(own, 127, 1))
    left = jnp.where(lane == 0, side, pltpu.roll(own, 1, 1))
    return (own + right) + left + (powers[pl.ds(7, 128), :] + powers[pl.ds(9, 128), :])


def columns_beside(left_ref, right_ref, turned):
    turned[...] = jnp.zeros((128, 128), F32)
    turned[pl.ds(0, 16, stride=2), :] = right_ref[...]
    turned[pl.ds(1, 16, stride=2), :] = left_ref[...]
    return power40(turned[...].T)


def reach(p_ref, inner_ref, outer_ref, left_ref, right_ref, total_ref, powers, turned):
    beside = columns_beside(left_ref, right_ref, turned)
    total_ref[...] = neighbours(p_ref[LAYERS - 1], LAYERS - 1, inner_ref, outer_ref, beside, powers)


def terms_upper(sizes, p_ref, f_ref, s_ref, inner_ref, outer_ref, left_ref, right_ref, uvw_ref, powers, turned):
    beside = columns_beside(left_ref, right_ref, turned)
    norms = 1.0 / plane_norms(sizes)
    layer0 = lax.axis_index("gz") * LAYERS
    for layer in range(1, LAYERS):
        total = neighbours(p_ref[layer - 1], layer - 1, inner_ref, outer_ref, beside, powers)
        u, v, low, inverse = terms(total, f_ref[layer], s_ref[layer], power39(p_ref[layer]))
        norm_z = norm_of(layer0 + layer, sizes[0] * LAYERS)
        uvw_ref[layer - 1] = u
        uvw_ref[14 + layer] = v
        uvw_ref[29 + layer] = low * inverse * (norms * (1.0 / norm_z))


def terms_lowest(sizes, p_ref, f_ref, s_ref, total_ref, uvw_ref):
    norms = 1.0 / plane_norms(sizes)
    layer0 = lax.axis_index("gz") * LAYERS
    p39 = power39(p_ref[0])
    s = s_ref[0]
    u, v, low, inverse = terms(total_ref[...], f_ref[0], s, p39)
    ground = layer0 == 0
    norm_z = norm_of(layer0, sizes[0] * LAYERS)
    uvw_ref[0] = jnp.where(ground, s, u)
    uvw_ref[1] = jnp.where(ground, p39, v)
    uvw_ref[2] = jnp.where(ground, 1.0, low * inverse) * (norms * (1.0 / norm_z))


def plane_of(upper_ref, low_ref, name, layer):
    kind = "uvw".index(name)
    if layer == 0:
        return low_ref.at[kind]
    return upper_ref.at[15 * kind + layer - 1]


def pack(upper_ref, low_ref, same_ref, cross_ref, corner_left_ref, corner_right_ref):
    c = core()
    lane = lanes(128)
    zero = jnp.zeros((128, 128), F32)

    def put(at, count, corner_at, corner_rows, left, right):
        same_ref[pl.ds(at, count), :] = jnp.where(c == 0, right, left)
        cross_ref[pl.ds(at, count), :] = jnp.where(c == 0, left, right)
        here = pl.ds(corner_at, corner_rows)
        first, last = slice(0, corner_rows), slice(count - corner_rows, count)
        corner_left_ref[here, :] = jnp.where(c == 0, left[first], left[last])
        corner_right_ref[here, :] = jnp.where(c == 0, right[first], right[last])

    for slab in range(3):
        left, right = zero, zero
        for name, layer, where, at in strips():
            if where != slab:
                continue
            width = width_of(layer)
            plane = plane_of(upper_ref, low_ref, name, layer)[...]
            inside = (lane >= at) & (lane < at + width)
            left = jnp.where(inside, pltpu.roll(plane, at, 1) if at else plane, left)
            right = jnp.where(inside, pltpu.roll(plane, (at + width) % 128, 1), right)
        put(128 * slab, 128, 24 * slab, 24, left, right)
    lane = lanes(64)
    left, right = zero[:64], zero[:64]
    for layer in range(LAYERS):
        ref = plane_of(upper_ref, low_ref, "w", layer)
        for half in range(2):
            plane = ref[pl.ds(64 * half, 64), :]
            at = 64 * half + RADIUS * layer
            inside = (lane >= at) & (lane < at + RADIUS)
            left = jnp.where(inside, pltpu.roll(plane, at, 1) if at else plane, left)
            right = jnp.where(inside, pltpu.roll(plane, (at + RADIUS) % 128, 1), right)
    put(384, 64, 72, 8, left, right)


def pack_rows(upper_ref, low_ref, rows_ref):
    c = core()
    for (name, layer), (at, rows) in ROW_PLACES.items():
        start = aligned(c * (128 - rows), 8)
        rows_ref[pl.ds(at, rows), :] = plane_of(upper_ref, low_ref, name, layer)[pl.ds(start, rows), :]


def row_halo(got_ref, shared_ref, at, rows):
    across = (core() ^ seam()) == 1
    return jnp.where(across, got_ref[pl.ds(at, rows), :], shared_ref[pl.ds(at, rows), :])


def place(target, index, at, count, value, halo, lane_at, width):
    c = core()
    lane = lanes(count)
    halo = pltpu.roll(halo, (128 - lane_at - (1 - c) * width) & 127, 1)
    begin = (1 - c) * (128 - width)
    outer = (lane >= begin) & (lane < begin + width)
    target[index, pl.ds(at, count), :] = jnp.where(outer, halo, value)


def place_rows(target, index, key, got_ref, shared_ref, corner, lane_at, width):
    start, rows = ROW_PLACES[key]
    to = aligned(256 + seam() * (32 - rows), 8)
    target[index, pl.ds(256, 32), :] = jnp.zeros((32, 128), F32)
    place(target, index, to, rows, row_halo(got_ref, shared_ref, start, rows), corner(rows), lane_at, width)


def assemble(
    upper_ref, low_ref, upper_other_ref, low_other_ref, got_ref, shared_ref, same_ref, cross_ref,
    corner_left_ref, corner_right_ref, uv_ref,
):
    c = core()
    own_at = aligned(c * 128, 128)
    other_at = aligned((1 - c) * 128, 128)
    for name, layer, slab, at in strips():
        width = width_of(layer)
        index = 2 * (LAYERS - 1 - layer) + (name == "v")
        here = pl.ds(128 * slab, 128)
        own = plane_of(upper_ref, low_ref, name, layer)[...]
        other = plane_of(upper_other_ref, low_other_ref, name, layer)[...]
        place(uv_ref, index, own_at, 128, own, same_ref[here, :], at, width)
        place(uv_ref, index, other_at, 128, other, cross_ref[here, :], at, width)

        def corner(rows):
            here = pl.ds(aligned(24 * slab + seam() * (24 - rows), 8), rows)
            return jnp.where(c == 0, corner_right_ref[here, :], corner_left_ref[here, :])

        place_rows(uv_ref, index, (name, layer), got_ref, shared_ref, corner, at, width)


def assemble_w(
    upper_ref, low_ref, upper_other_ref, low_other_ref, got_ref, shared_ref, same_ref, cross_ref,
    corner_left_ref, corner_right_ref, w_ref,
):
    c = core()
    own_at = aligned(c * 128, 128)
    other_at = aligned((1 - c) * 128, 128)
    slab = pl.ds(384, 64)

    def corner(rows):
        here = pl.ds(72, rows)
        return jnp.where(c == 0, corner_right_ref[here, :], corner_left_ref[here, :])

    for layer in range(LAYERS):
        own = plane_of(upper_ref, low_ref, "w", layer)
        other = plane_of(upper_other_ref, low_other_ref, "w", layer)
        for half in range(2):
            rows = pl.ds(64 * half, 64)
            at = 64 * half + RADIUS * layer
            place(w_ref, layer, aligned(own_at + 64 * half, 64), 64, own[rows, :], same_ref[slab, :], at, RADIUS)
            place(w_ref, layer, aligned(other_at + 64 * half, 64), 64, other[rows, :], cross_ref[slab, :], at, RADIUS)
        place_rows(
            w_ref, layer, ("w", layer), got_ref, shared_ref, corner, RADIUS * layer + 64 * seam(), RADIUS
        )


def five(value):
    return (value + pltpu.roll(value, 1, 1)) + pltpu.roll(value, 127, 1) + (
        pltpu.roll(value, 1, 0) + pltpu.roll(value, PLANE - 1, 0)
    )


def set_carry(carry, main_ref, other_ref, outer_ref, halo_ref, halo_other_ref, halo_outer_ref):
    c = core()
    lane = lanes(64)
    mine = (lane >> 6) == c
    for i in range(4):
        rows = pl.ds(64 * (i % 2), 64)
        own, other = main_ref[rows, :], other_ref[rows, :]
        if i < 2:
            value = jnp.where(mine, own, other)
        else:
            value = pltpu.roll(jnp.where(mine, other, own), 64, 1)
        outer = pltpu.roll(outer_ref[...], (128 - 32 * i) % 128, 1) if i else outer_ref[...]
        begin = (1 - c) * 108
        value = jnp.where((lane >= begin) & (lane < begin + 20), outer, value)
        carry[pl.ds(64 * i, 64), :] = value
    lane = lanes(24)
    value = jnp.where((lane >> 6) == c, halo_ref[...], halo_other_ref[...])
    begin = (1 - c) * 108
    value = jnp.where((lane >= begin) & (lane < begin + 20), halo_outer_ref[...], value)
    carry[pl.ds(256, 32), :] = jnp.zeros((32, 128), F32)
    carry[pl.ds(aligned(256 + 8 * seam(), 8), 24), :] = value


def section(active, *refs):
    uv_ref, refs = refs[0], refs[1:]
    pieces, before_ref = (), None
    if active is not None and len(refs) > 5:
        pieces, before_ref, refs = refs[:6], refs[6], refs[7:]
    if len(refs) == 5:
        layers_ref, main_ref, outer_ref, halo_ref, carry = refs
    else:
        layers_ref, carry = refs
        main_ref = None

    @pl.when(lax.axis_index("gz") == active)
    def _():
        if pieces:
            set_carry(carry, *pieces)
            value = carry[...]
        else:
            value = jnp.zeros((PLANE, 128), F32)

        def step(i, value):
            value = uv_ref[2 * i] + uv_ref[2 * i + 1] * five(value)
            layers_ref[LAYERS - 1 - i] = value
            return value

        lax.fori_loop(0, LAYERS, step, value)
        if main_ref is None:
            return
        c = core()
        lane = lanes(128)
        bottom = layers_ref.at[0]
        mine = (lane >> 6) == c
        main_ref[...] = jnp.where(mine, bottom[pl.ds(0, 128), :], pltpu.roll(bottom[pl.ds(128, 128), :], 64, 1))
        lane = lanes(64)
        slab = jnp.zeros((64, 128), F32)
        for i in range(4):
            rolled = bottom[pl.ds(64 * i, 64), :]
            rolled = pltpu.roll(rolled, 32 * i, 1) if i else rolled
            begin = (32 * i + 128 - c * 32) & 127
            slab = jnp.where(((lane - begin) & 127) < 32, rolled, slab)
        outer_ref[...] = slab
        halo_ref[...] = bottom[pl.ds(aligned((1 - seam()) * 232, 8), 24), :]

    if before_ref is not None:
        @pl.when(lax.axis_index("gz") != active)
        def _():
            layers_ref[...] = before_ref[...]


def tent(value, turn):
    for _ in range(2):
        two = value + turn(value, 1)
        value = (two + turn(two, 2)) + turn(value, 4)
    return value


def smooth(layers_ref, w_ref, out_ref, give_ref, weighted):
    mine = (lanes(128) >> 6) == core()

    def layer(k, _):
        weighted[pl.ds(8, PLANE), :] = layers_ref[k] * w_ref[k]
        weighted[pl.ds(0, 8), :] = weighted[pl.ds(PLANE, 8), :]
        halves = []
        for half in range(2):
            start = 8 + 128 * half
            total = weighted[pl.ds(start, 128), :] * 5.0
            for offset in range(1, RADIUS + 1):
                total = total + (
                    weighted[pl.ds(start - offset, 128), :] + weighted[pl.ds(start + offset, 128), :]
                ) * (5.0 - offset)
            value = tent(total, lambda x, i: pltpu.roll(x, i, 1))
            halves.append(pltpu.roll(value, 124, 1))
        out_ref[k] = jnp.where(mine, halves[0], pltpu.roll(halves[1], 64, 1))
        return 0

    lax.fori_loop(0, LAYERS, layer, 0)
    give(out_ref, give_ref)


def give(from_ref, to_ref):
    count = to_ref.shape[0]
    low = (lanes(128) >> 6) == 0
    for k in range(count):
        to_ref[k] = jnp.where(low, pltpu.roll(from_ref[k + count], 64, 1), from_ref[k])


def merge(keep_ref, got_ref, out_ref):
    c = core()
    count = keep_ref.shape[0] // 2
    mine = (lanes(128) >> 6) == c
    for k in range(2 * count):
        own, other = keep_ref[k], got_ref[k % count]
        own = pltpu.roll(own, 64 * c, 1)
        other = pltpu.roll(other, 64 * c if k < count else 64 * (1 - c), 1)
        out_ref[k] = jnp.where(mine, own, other)


def ends(keep_ref, got_ref, out_ref, top_ref, bottom_ref):
    merge(keep_ref, got_ref, out_ref)
    top_ref[...] = out_ref[pl.ds(LAYERS - RADIUS, RADIUS)]
    bottom_ref[...] = out_ref[pl.ds(0, RADIUS)]


def finish(tile_ref, below_ref, above_ref, passive_ref, out_ref):
    def layer(k):
        if k < 0:
            return below_ref[k + RADIUS]
        if k >= LAYERS:
            return above_ref[k - LAYERS]
        return tile_ref[k]

    for k in range(LAYERS):
        total = layer(k) * 5.0
        for offset in range(1, RADIUS + 1):
            total = total + (layer(k - offset) + layer(k + offset)) * (5.0 - offset)
        out_ref[k] = jnp.where(passive_ref[k] > 0, 0.0, total)


def to_other(value):
    return moved(value, lambda z, y, x: (z, y ^ 1, x))


def after(value, *others):
    return lax.optimization_barrier((value,) + others)[0]


def per_device(filtered, printed, sensitivity, passive):
    sizes = tuple(lax.axis_size(axis) for axis in AXES)
    depth = sizes[0]
    plane = shape(128, 128)
    edge = shape(16, 128)
    inner, outer, left, right = call(edges, [edge] * 4, printed, scratch=[pltpu.VMEM((128, 128), F32)])

    def across(z, y, x):
        return (z, y ^ 3, x) if y in (1, 2) else None

    def beside(z, y, x):
        return (z, y ^ 1, x + (1 if y & 1 else -1))

    def same(z, y, x):
        return (z, y, x + (-1 if y & 1 else 1))

    outer = moved(outer, across)
    from_left = moved(right, lambda z, y, x: (z, y, x + 1))
    from_right = moved(left, lambda z, y, x: (z, y, x - 1))
    inner = to_other(inner)
    near = (inner, outer, from_left, from_right)
    work = [pltpu.VMEM((144, 128), F32), pltpu.VMEM((128, 128), F32)]
    above = call(reach, plane, printed, *near, scratch=work)
    total0 = moved(above, lambda z, y, x: (z + 1, y, x))
    upper = call(
        functools.partial(terms_upper, sizes), shape(45, 128, 128),
        after(printed, above), filtered, sensitivity, *near, scratch=work,
    )
    low = call(functools.partial(terms_lowest, sizes), shape(3, 128, 128), printed, filtered, sensitivity, total0)
    slab = shape(SLAB_ROWS, 128)
    corner = shape(CORNER_ROWS, 128)
    rows = call(pack_rows, shape(ROW_TOTAL, 128), upper, low)
    got = moved(rows, across)
    to_same, to_cross, corner_left, corner_right = call(pack, [slab, slab, corner, corner], after(upper, rows), low)
    from_same = moved(to_same, same)
    from_cross = moved(to_cross, beside)
    corner_right = moved(corner_right, lambda z, y, x: (z, 2 * (2 - y), x + 1) if y in (1, 2) else None)
    corner_left = moved(corner_left, lambda z, y, x: (z, 5 - 2 * y, x - 1) if y in (1, 2) else None)
    got = after(got, from_same, from_cross, corner_left, corner_right)
    shared = moved(got, lambda z, y, x: (z, y ^ 1, x) if y in (1, 2) else None)
    upper_other, low_other = to_other(upper), to_other(low)
    parts = (upper, low, upper_other, low_other, got, shared, from_same, from_cross, corner_left, corner_right)
    uvs = call(assemble, shape(2 * LAYERS, PLANE, 128), *parts)
    ws = None
    pieces, before = (), ()
    stack = shape(LAYERS, PLANE, 128)
    for active in range(depth - 1, -1, -1):
        outs = [stack]
        if active > 0:
            outs = outs + [plane, shape(64, 128), shape(24, 128)]
        layers, *sent = call(
            functools.partial(section, active), outs, uvs, *pieces, *before, scratch=[pltpu.VMEM((PLANE, 128), F32)]
        )
        before = (layers,)
        if active > 0:
            main, side, strip = sent

            def down(where):
                def to(z, y, x):
                    _, ty, tx = where(z, y, x)
                    return (z - 1, ty, tx) if z == active else None
                return to

            def over(z, y, x):
                return (z, y ^ 2, x)

            def corner_of(z, y, x):
                _, ty, tx = beside(z, y, x)
                return (z, ty ^ 2, tx)

            def sibling(z, y, x):
                return (z, y ^ 1, x) if z == active - 1 else None

            main = moved(main, down(lambda z, y, x: (z, y, x)))
            halo = moved(strip, down(over))
            side = moved(side, down(beside))
            edge_piece = moved(strip, down(corner_of))
            main, halo, side, edge_piece = lax.optimization_barrier((main, halo, side, edge_piece))
            pieces = (main, moved(main, sibling), side, halo, moved(halo, sibling), edge_piece)
            if ws is None:
                ws = call(assemble_w, stack, after(upper, side), *parts[1:])
    kept, given = call(
        smooth,
        [shape(LAYERS, 128, 128), shape(LAYERS // 2, 128, 128)],
        layers, ws,
        scratch=[pltpu.VMEM((PLANE + 8, 128), F32)],
    )
    given = to_other(given)
    quarter = shape(RADIUS, 128, 128)
    tile, top, bottom = call(ends, [shape(LAYERS, 128, 128), quarter, quarter], kept, given)
    below = moved(top, lambda z, y, x: (z + 1, y, x))
    over = moved(bottom, lambda z, y, x: (z - 1, y, x))
    return call(finish, shape(LAYERS, 128, 128), tile, below, over, passive)


def solution(mesh):
    spec = P(*AXES)
    return jax.shard_map(
        per_device, mesh=mesh, in_specs=(spec,) * 4, out_specs=spec, check_vma=False
    )
```

```python
import functools
import math

import jax
import jax.numpy as jnp
from jax import lax
from jax.experimental import pallas as pl
from jax.experimental.pallas import tpu as pltpu
from jax.sharding import PartitionSpec as P

RADIUS = 4
PENALTY = 40.0
EXPONENT = PENALTY + math.log(5.0) / math.log(0.5)
SMOOTH = 0.001
AXES = ("gz", "gy", "gx")
F32 = jnp.float32

LAYERS = 16
STEPS = LAYERS + 1
PLANE = 288
VECTORS = PLANE // 8
REACH = RADIUS + STEPS
SLABS = ((16, 15, 14, 3), (13, 12, 11, 8, 0), (10, 9, 7, 6, 5, 2), (4, 1))
FOLDED = 32
SLAB_ROWS = 3 * 128 + FOLDED + 64
CORNER_ROWS = 3 * 24 + 16 + 8


def width_of(layer):
    return RADIUS + layer


def rows_of(layer):
    return -(-width_of(layer) // 8) * 8


MICROSECONDS = {"all_terms": 2.5, "assemble": 2.5, "section": 2.6, "smooth": 4.0, "finish": 3.0, "ends": 1.0}


def strips():
    out = []
    for slab, layers in enumerate(SLABS):
        at = 0
        for layer in layers:
            for name in ("u", "v"):
                out.append((name, layer, slab, at))
                at += width_of(layer)
        assert at <= (128 if slab < 3 else FOLDED)
    return out


def row_places():
    places, at = {}, 0
    for layer in range(STEPS):
        for name in ("u", "v", "w"):
            if (name, layer) == ("w", 0):
                continue
            rows = 8 if name == "w" else rows_of(layer)
            places[name, layer] = (at, rows)
            at += rows
    return places, at


ROW_PLACES, ROW_TOTAL = row_places()


def moved(value, where):
    sizes = tuple(lax.axis_size(axis) for axis in AXES)
    pairs = []
    for z in range(sizes[0]):
        for y in range(sizes[1]):
            for x in range(sizes[2]):
                to = where(z, y, x)
                if to is not None:
                    tz, ty, tx = to[0] % sizes[0], to[1], to[2] % sizes[2]
                    pairs.append(((z * sizes[1] + y) * sizes[2] + x, (tz * sizes[1] + ty) * sizes[2] + tx))
    return lax.ppermute(value, AXES, pairs)


def shape(*dims):
    return jax.ShapeDtypeStruct(dims, F32)


def call(kernel, outs, *args, scratch=(), in_specs=None, **more):
    name = kernel.func.__name__ if isinstance(kernel, functools.partial) else kernel.__name__
    if in_specs is not None:
        more["in_specs"] = in_specs
    return pl.pallas_call(
        kernel,
        out_shape=outs,
        scratch_shapes=list(scratch),
        compiler_params=pltpu.CompilerParams(vmem_limit_bytes=40 * 1024 * 1024),
        cost_estimate=pl.CostEstimate(flops=0, bytes_accessed=int(MICROSECONDS.get(name, 0.5) * 3e6), transcendentals=0),
        name=name,
        **more,
    )(*args)


def lanes(rows):
    return lax.broadcasted_iota(jnp.int32, (rows, 128), 1)


def core():
    return lax.axis_index("gy") & 1


def seam():
    return lax.axis_index("gy") >> 1


def one_if(condition):
    return jnp.where(condition, 1.0, 0.0)


def outside():
    x, c = lax.axis_index("gx"), core()
    return ((c == 0) & (x == 0)) | ((c == 1) & (x == lax.axis_size("gx") - 1))


def plain_to_plane(ref):
    return jnp.concatenate([ref[pl.ds(t, 8, stride=VECTORS), :] for t in range(VECTORS)], axis=0)


def plane_to_plain(value, ref):
    for t in range(VECTORS):
        ref[pl.ds(t, 8, stride=VECTORS), :] = value[8 * t:8 * t + 8]


def aligned(value, to):
    return pl.multiple_of(value, to)


def power40(p):
    x = p + p
    x2 = x * x
    x4 = x2 * x2
    x8 = x4 * x4
    x32 = x8 * x8
    x32 = x32 * x32
    return x32 * x8


def power39(p):
    x = p + p
    x2 = x * x
    x4 = x2 * x2
    x8 = x4 * x4
    x32 = x8 * x8
    x32 = x32 * x32
    return x32 * (x4 * (x2 * x))


def edges(p_ref, inner_ref, outer_ref, left_ref, right_ref, turned):
    lane = lanes(128)
    c = core()
    packed = jnp.zeros((128, 128), F32)
    for layer in range(LAYERS):
        inner_ref[pl.ds(layer, 1), :] = p_ref[layer, pl.ds(127 * (1 - c), 1), :]
        outer_ref[pl.ds(layer, 1), :] = p_ref[layer, pl.ds(127 * c, 1), :]
        rolled = pltpu.roll(p_ref[layer], 2 * layer + 1, 1)
        packed = jnp.where((lane >> 1) == layer, rolled, packed)
    turned[...] = packed.T
    right_ref[...] = turned[pl.ds(0, 16, stride=2), :]
    left_ref[...] = turned[pl.ds(1, 16, stride=2), :]


def norm_of(position, extent):
    def missing(k):
        k = jnp.maximum(k, 0)
        return (k * (k + 1)) >> 1

    return ((RADIUS + 1) ** 2 - missing(RADIUS - position) - missing(RADIUS - (extent - 1 - position))).astype(F32)


def terms(total, density, sens, p39):
    total = jnp.maximum(total, 1e-30)
    offset = PENALTY * math.log(2.0) / EXPONENT
    smax = jnp.exp(jnp.log(total) * (1.0 / EXPONENT) - offset)
    gap = density - smax
    half = 0.5 * gap * lax.rsqrt(gap * gap + SMOOTH)
    low = 0.5 - half
    top = (0.5 + half) * (2.0 * PENALTY / EXPONENT) * smax
    h = top / total
    return h * sens, h * p39, low, total / top


def plane_norms(sizes):
    row0 = lax.axis_index("gy") * 128
    col0 = lax.axis_index("gx") * 128
    rows = lax.broadcasted_iota(jnp.int32, (128, 128), 0) + row0
    cols = lax.broadcasted_iota(jnp.int32, (128, 128), 1) + col0
    return norm_of(rows, sizes[1] * 128) * norm_of(cols, sizes[2] * 128)


def neighbours(p, layer, inner_ref, outer_ref, beside, powers):
    c = core()
    lane = lanes(128)
    own = power40(p)
    powers[pl.ds(8, 128), :] = own
    y = lax.axis_index("gy")
    there = one_if((y == 1) | (y == 2))
    powers[pl.ds(7 + 129 * (1 - c), 1), :] = power40(inner_ref[pl.ds(layer, 1), :])
    powers[pl.ds(7 + 129 * c, 1), :] = power40(outer_ref[pl.ds(layer, 1), :]) * there
    side = pltpu.roll(beside, (128 - (2 * layer + 1)) % 128, 1)
    right = jnp.where(lane == 127, side, pltpu.roll(own, 127, 1))
    left = jnp.where(lane == 0, side, pltpu.roll(own, 1, 1))
    return (own + right) + left + (powers[pl.ds(7, 128), :] + powers[pl.ds(9, 128), :])


def columns_beside(left_ref, right_ref, turned):
    x = lax.axis_index("gx")
    turned[...] = jnp.zeros((128, 128), F32)
    turned[pl.ds(0, 16, stride=2), :] = right_ref[...] * one_if(x < lax.axis_size("gx") - 1)
    turned[pl.ds(1, 16, stride=2), :] = left_ref[...] * one_if(x > 0)
    return power40(turned[...].T)


def lowest(p_ref, f_ref, s_ref, out_ref):
    out_ref[0] = p_ref[0]
    out_ref[1] = f_ref[0]
    out_ref[2] = s_ref[0]


def all_terms(sizes, p_ref, f_ref, s_ref, above_ref, inner_ref, outer_ref, left_ref, right_ref, uvw_ref, powers, turned):
    beside = columns_beside(left_ref, right_ref, turned)
    norms = 1.0 / plane_norms(sizes)
    gz = lax.axis_index("gz")
    layer0 = gz * LAYERS
    uvw_ref[0] = s_ref[0]
    uvw_ref[STEPS] = power39(p_ref[0])
    uvw_ref[2 * STEPS] = norms * (1.0 / norm_of(0 * layer0, sizes[0] * LAYERS))
    for layer in range(1, STEPS):
        total = neighbours(p_ref[layer - 1], layer - 1, inner_ref, outer_ref, beside, powers)
        if layer < LAYERS:
            p, f, s = p_ref[layer], f_ref[layer], s_ref[layer]
        else:
            p, f, s = above_ref[0], above_ref[1], above_ref[2]
        u, v, low, inverse = terms(total, f, s, power39(p))
        if layer == LAYERS:
            there = one_if(gz < sizes[0] - 1)
            u, v = u * there, v * there
        norm_z = norm_of(layer0 + layer, sizes[0] * LAYERS)
        uvw_ref[layer] = u
        uvw_ref[STEPS + layer] = v
        uvw_ref[2 * STEPS + layer] = low * inverse * (norms * (1.0 / norm_z))


def plane_of(uvw_ref, name, layer):
    return uvw_ref.at[STEPS * "uvw".index(name) + layer]


def pack_rows(uvw_ref, rows_ref):
    c = core()
    for (name, layer), (at, rows) in ROW_PLACES.items():
        start = aligned(c * (128 - rows), 8)
        rows_ref[pl.ds(at, rows), :] = plane_of(uvw_ref, name, layer)[pl.ds(start, rows), :]


def pack(uvw_ref, same_ref, cross_ref, corner_left_ref, corner_right_ref):
    c = core()

    def put(at, left, right):
        count = left.shape[0]
        same_ref[pl.ds(at, count), :] = jnp.where(c == 0, right, left)
        cross_ref[pl.ds(at, count), :] = jnp.where(c == 0, left, right)

    def put_corner(at, rows, left, right):
        first, last = slice(0, rows), slice(left.shape[0] - rows, left.shape[0])
        corner_left_ref[pl.ds(at, rows), :] = jnp.where(c == 0, left[first], left[last])
        corner_right_ref[pl.ds(at, rows), :] = jnp.where(c == 0, right[first], right[last])

    lane = lanes(128)
    for slab in range(4):
        left = right = jnp.zeros((128, 128), F32)
        for name, layer, where, at in strips():
            if where == slab:
                width = width_of(layer)
                plane = plane_of(uvw_ref, name, layer)[...]
                inside = (lane >= at) & (lane < at + width)
                left = jnp.where(inside, pltpu.roll(plane, at, 1) if at else plane, left)
                right = jnp.where(inside, pltpu.roll(plane, (at + width) % 128, 1), right)
        if slab < 3:
            put(128 * slab, left, right)
            put_corner(24 * slab, 24, left, right)
            continue
        put_corner(72, 16, left, right)
        folded = []
        for value in (left, right):
            total = value[:FOLDED]
            for i in range(1, 4):
                total = total + pltpu.roll(value[FOLDED * i:FOLDED * (i + 1)], FOLDED * i, 1)
            folded.append(total)
        put(384, *folded)
    lane = lanes(64)
    left = right = jnp.zeros((64, 128), F32)
    for layer in range(1, STEPS):
        ref = plane_of(uvw_ref, "w", layer)
        for half in range(2):
            plane = ref[pl.ds(64 * half, 64), :]
            at = 64 * half + RADIUS * (layer - 1)
            inside = (lane >= at) & (lane < at + RADIUS)
            left = jnp.where(inside, pltpu.roll(plane, at, 1) if at else plane, left)
            right = jnp.where(inside, pltpu.roll(plane, (at + RADIUS) % 128, 1), right)
    put(384 + FOLDED, left, right)
    put_corner(88, 8, left, right)


def slab_plane(plain, same, cross, corner):
    c = core()
    inside = one_if(jnp.logical_not(outside()))
    plain[pl.ds(256, 32), :] = jnp.zeros((32, 128), F32)
    plain[pl.ds(aligned(c * 128, 128), 128), :] = same * inside
    plain[pl.ds(aligned((1 - c) * 128, 128), 128), :] = cross * inside
    rows = corner.shape[0]
    plain[pl.ds(aligned(256 + seam() * (32 - rows), 8), rows), :] = corner * inside


def full_plane(plain, name, layer, uvw_ref, other_ref, got_ref, shared_ref):
    c = core()
    plain[pl.ds(aligned(c * 128, 128), 128), :] = plane_of(uvw_ref, name, layer)[...]
    plain[pl.ds(aligned((1 - c) * 128, 128), 128), :] = plane_of(other_ref, name, layer)[...]
    plain[pl.ds(256, 32), :] = jnp.zeros((32, 128), F32)
    start, rows = ROW_PLACES[name, layer]
    here = pl.ds(start, rows)
    to = aligned(256 + seam() * (32 - rows), 8)
    plain[pl.ds(to, rows), :] = jnp.where((c ^ seam()) == 1, got_ref[here, :], shared_ref[here, :])
    return plain_to_plane(plain)


def with_columns(base, columns, at, width):
    c = core()
    lane = lanes(PLANE)
    columns = pltpu.roll(columns, (128 - at - (1 - c) * width) & 127, 1)
    begin = (1 - c) * (128 - width)
    return jnp.where((lane >= begin) & (lane < begin + width), columns, base)


def assemble(
    uvw_ref, other_ref, got_ref, shared_ref, same_ref, cross_ref, corner_left_ref, corner_right_ref, uv_ref, plain, slabs
):
    c = core()
    for slab in range(4):
        if slab < 3:
            here = pl.ds(128 * slab, 128)
            same, cross = same_ref[here, :], cross_ref[here, :]
            here = pl.ds(24 * slab, 24)
        else:
            here = pl.ds(384, FOLDED)
            same, cross = (
                jnp.concatenate([value] + [pltpu.roll(value, 128 - FOLDED * i, 1) for i in range(1, 4)], axis=0)
                for value in (same_ref[here, :], cross_ref[here, :])
            )
            here = pl.ds(72, 16)
        corner = jnp.where(c == 0, corner_right_ref[here, :], corner_left_ref[here, :])
        slot = plain.at[slab % 2]
        slab_plane(slot, same, cross, corner)
        slabs[slab] = plain_to_plane(slot)
    for place, (name, layer, slab, at) in enumerate(strips()):
        base = full_plane(plain.at[place % 2], name, layer, uvw_ref, other_ref, got_ref, shared_ref)
        uv_ref[2 * (LAYERS - layer) + (name == "v")] = with_columns(base, slabs[slab], at, width_of(layer))


def assemble_w(
    uvw_ref, other_ref, got_ref, shared_ref, same_ref, cross_ref, corner_left_ref, corner_right_ref, w_ref, plain, slabs
):
    c = core()

    def unfolded(ref):
        value = ref[pl.ds(384 + FOLDED, 64), :]
        return jnp.concatenate([value, pltpu.roll(value, 64, 1)], axis=0)

    here = pl.ds(88, 8)
    corner = jnp.where(c == 0, corner_right_ref[here, :], corner_left_ref[here, :])
    corner = pltpu.roll(corner, 64 * seam(), 1)
    slab_plane(plain.at[0], unfolded(same_ref), unfolded(cross_ref), corner)
    slabs[0] = plain_to_plane(plain.at[0])
    for layer in range(1, STEPS):
        base = full_plane(plain.at[layer % 2], "w", layer, uvw_ref, other_ref, got_ref, shared_ref)
        w_ref[layer] = with_columns(base, slabs[0], RADIUS * (layer - 1), RADIUS)
    row = lax.broadcasted_iota(jnp.int32, (PLANE, 128), 0)
    col = lax.broadcasted_iota(jnp.int32, (PLANE, 128), 1)
    a = seam()
    row = jnp.where((a == 1) & (row >= 256), row - PLANE, row) + 256 * a
    width = jnp.where(c == 0, 108, 20)
    col = jnp.where((c == 0) & (col >= width), col - 128, jnp.where((c == 1) & (col < width), col + 128, col))
    col = col + 128 * lax.axis_index("gx")
    rows, cols = 128 * lax.axis_size("gy"), 128 * lax.axis_size("gx")
    norm = norm_of(row, rows) * norm_of(col, cols) * norm_of(0 * a, LAYERS * lax.axis_size("gz"))
    inside = (row >= 0) & (row < rows) & (col >= 0) & (col < cols)
    plain[0] = jnp.where(inside, 1.0 / jnp.where(inside, norm, 1.0), 0.0)
    w_ref[0] = plain_to_plane(plain.at[0])


def five(value):
    before = jnp.concatenate([pltpu.roll(value[PLANE - 8:], 1, 0), value[:PLANE - 8]], axis=0)
    behind = jnp.concatenate([value[8:], pltpu.roll(value[:8], 7, 0)], axis=0)
    return (value + before + behind) + (pltpu.roll(value, 1, 1) + pltpu.roll(value, 127, 1))


def set_carry(carry, main_ref, other_ref, outer_ref, halo_ref, halo_other_ref, halo_outer_ref):
    c = core()
    lane = lanes(64)
    mine = (lane >> 6) == c
    inside = one_if(jnp.logical_not(outside()))
    for i in range(4):
        rows = pl.ds(64 * (i % 2), 64)
        own, other = main_ref[rows, :], other_ref[rows, :]
        if i < 2:
            value = jnp.where(mine, own, other)
        else:
            value = pltpu.roll(jnp.where(mine, other, own), 64, 1)
        outer = pltpu.roll(outer_ref[...], (128 - 32 * i) % 128, 1) if i else outer_ref[...]
        outer = outer * inside
        begin = (1 - c) * (128 - REACH)
        value = jnp.where((lane >= begin) & (lane < begin + REACH), outer, value)
        carry[pl.ds(64 * i, 64), :] = value
    lane = lanes(24)
    value = jnp.where((lane >> 6) == c, halo_ref[...], halo_other_ref[...])
    begin = (1 - c) * (128 - REACH)
    value = jnp.where((lane >= begin) & (lane < begin + REACH), halo_outer_ref[...] * inside, value)
    carry[pl.ds(256, 32), :] = jnp.zeros((32, 128), F32)
    carry[pl.ds(aligned(256 + 8 * seam(), 8), 24), :] = value


def section(active, *refs):
    uv_ref, refs = refs[0], refs[1:]
    pieces, before_ref = (), None
    if active is not None and len(refs) > 5:
        pieces, before_ref, refs = refs[:6], refs[6], refs[7:]
    if len(refs) == 5:
        layers_ref, main_ref, outer_ref, halo_ref, carry = refs
    else:
        layers_ref, carry = refs
        main_ref = None

    @pl.when(lax.axis_index("gz") == active)
    def _():
        if pieces:
            set_carry(carry, *pieces)
            value = plain_to_plane(carry)
        else:
            value = jnp.zeros((PLANE, 128), F32)

        def step(i, value):
            value = uv_ref[2 * i] + uv_ref[2 * i + 1] * five(value)
            layers_ref[LAYERS - i] = value
            return value

        value = lax.fori_loop(0, LAYERS, step, value)
        layers_ref[0] = uv_ref[2 * LAYERS] + uv_ref[2 * LAYERS + 1] * five(value)
        if main_ref is None:
            return
        c = core()
        lane = lanes(128)
        plane_to_plain(value, carry)
        bottom = carry
        mine = (lane >> 6) == c
        main_ref[...] = jnp.where(mine, bottom[pl.ds(0, 128), :], pltpu.roll(bottom[pl.ds(128, 128), :], 64, 1))
        lane = lanes(64)
        slab = jnp.zeros((64, 128), F32)
        for i in range(4):
            rolled = bottom[pl.ds(64 * i, 64), :]
            rolled = pltpu.roll(rolled, 32 * i, 1) if i else rolled
            begin = (32 * i + 128 - c * 32) & 127
            slab = jnp.where(((lane - begin) & 127) < 32, rolled, slab)
        outer_ref[...] = slab
        halo_ref[...] = bottom[pl.ds(aligned((1 - seam()) * 232, 8), 24), :]

    if before_ref is not None:
        @pl.when(lax.axis_index("gz") != active)
        def _():
            layers_ref[...] = before_ref[...]


def box(values):
    two = [values[i] + values[i + 1] for i in range(len(values) - 1)]
    four = [two[i] + two[i + 2] for i in range(len(two) - 2)]
    return [four[i] + values[i + 4] for i in range(len(values) - 4)]


def smooth(layers_ref, w_ref, kept_ref, give_ref, plain, others, tent):
    c = core()
    mine = (lanes(128) >> 6) == c
    row = lax.broadcasted_iota(jnp.int32, (256, 128), 0)
    col = lax.broadcasted_iota(jnp.int32, (256, 128), 1)
    distance = (row - col + RADIUS) & 127
    weight = jnp.where(distance <= 2 * RADIUS, RADIUS + 1 - jnp.abs(distance - RADIUS), 0)
    tent[...] = weight.astype(F32).astype(jnp.bfloat16)

    def layer(k, _):
        values = [layers_ref[k, pl.ds(8 * t, 8), :] * w_ref[k, pl.ds(8 * t, 8), :] for t in range(VECTORS)]
        first = [pltpu.roll(value, 1, 0) for value in values[VECTORS - RADIUS:]]
        last = [pltpu.roll(value, 7, 0) for value in values[:RADIUS]]
        total = jnp.concatenate(box(box(first + values + last)), axis=0)
        high = total.astype(jnp.bfloat16)
        rest = total - high.astype(F32)
        middle = rest.astype(jnp.bfloat16)
        small = (rest - middle.astype(F32)).astype(jnp.bfloat16)
        value = jnp.dot(jnp.concatenate([high, middle], axis=1), tent[...], preferred_element_type=F32)
        value = value + jnp.dot(small, tent[pl.ds(0, 128), :], preferred_element_type=F32)
        plane_to_plain(value, plain)
        kept_ref[k] = plain[pl.ds(aligned(c * 128, 128), 128), :]
        others[k] = plain[pl.ds(aligned((1 - c) * 128, 128), 128), :]
        return 0

    lax.fori_loop(0, STEPS, layer, 0)
    count = give_ref.shape[0]
    for k in range(count):
        second = others[k + count] if k + count < STEPS else jnp.zeros((128, 128), F32)
        give_ref[k] = jnp.where(mine, others[k], pltpu.roll(second, 64, 1))


def ends(kept_ref, got_ref, out_ref, top_ref, bottom_ref):
    mine = (lanes(128) >> 6) == core()
    count = got_ref.shape[0]
    for k in range(STEPS):
        other = got_ref[k] if k < count else pltpu.roll(got_ref[k - count], 64, 1)
        out_ref[k] = jnp.where(mine, kept_ref[k], other)
    top_ref[...] = out_ref[pl.ds(STEPS - RADIUS - 1, RADIUS + 1)]
    bottom_ref[...] = out_ref[pl.ds(1, RADIUS - 1)]


def finish(tile_ref, below_ref, above_ref, passive_ref, out_ref):
    gz = lax.axis_index("gz")
    has_below, has_above = one_if(gz > 0), one_if(gz < lax.axis_size("gz") - 1)

    def layer(k):
        if k < 0:
            return below_ref[k + RADIUS] * has_below
        if k == 0:
            return jnp.where(gz == 0, tile_ref[0], below_ref[RADIUS])
        if k > LAYERS:
            return above_ref[k - STEPS] * has_above
        return tile_ref[k]

    for k in range(LAYERS):
        total = layer(k) * 5.0
        for offset in range(1, RADIUS + 1):
            total = total + (layer(k - offset) + layer(k + offset)) * (5.0 - offset)
        out_ref[k] = jnp.where(passive_ref[k] > 0, 0.0, total)


def to_other(value):
    return moved(value, lambda z, y, x: (z, y ^ 1, x))


def after(value, *others):
    return lax.optimization_barrier((value,) + others)[0]


def per_device(filtered, printed, sensitivity, passive):
    sizes = tuple(lax.axis_size(axis) for axis in AXES)
    depth = sizes[0]
    plane = shape(128, 128)
    edge = shape(16, 128)

    def across(z, y, x):
        return (z, y ^ 3, x) if y in (1, 2) else None

    def beside(z, y, x):
        return (z, y ^ 1, x + (1 if y & 1 else -1))

    def same(z, y, x):
        return (z, y, x + (-1 if y & 1 else 1))

    one = pl.BlockSpec((1, 128, 128), lambda i: (0, 0, 0))
    lowest_planes = call(lowest, shape(3, 128, 128), printed, filtered, sensitivity, in_specs=[one] * 3, grid=(1,))
    above = moved(lowest_planes, lambda z, y, x: (z - 1, y, x))
    inner, outer, left, right = call(edges, [edge] * 4, printed, scratch=[pltpu.VMEM((128, 128), F32)])
    from_left = moved(right, lambda z, y, x: (z, y, x + 1))
    from_right = moved(left, lambda z, y, x: (z, y, x - 1))
    outer = moved(outer, lambda z, y, x: (z, y ^ 3, x))
    inner = to_other(inner)
    uvw = call(
        functools.partial(all_terms, sizes), shape(3 * STEPS, 128, 128),
        printed, filtered, sensitivity, above, inner, outer, from_left, from_right,
        scratch=[pltpu.VMEM((144, 128), F32), pltpu.VMEM((128, 128), F32)],
    )
    slab, corner = shape(SLAB_ROWS, 128), shape(CORNER_ROWS, 128)
    rows = call(pack_rows, shape(ROW_TOTAL, 128), uvw)
    got = moved(rows, across)
    to_same, to_cross, corner_left, corner_right = call(pack, [slab, slab, corner, corner], after(uvw, rows))
    from_same = moved(to_same, same)
    from_cross = moved(to_cross, beside)
    corner_right = moved(corner_right, lambda z, y, x: (z, 2 * (2 - y), x + 1) if y in (1, 2) else None)
    corner_left = moved(corner_left, lambda z, y, x: (z, 5 - 2 * y, x - 1) if y in (1, 2) else None)
    other = to_other(uvw)
    shared = to_other(after(got, from_same, from_cross, corner_left, corner_right))
    parts = (uvw, other, got, shared, from_same, from_cross, corner_left, corner_right)
    stack = shape(STEPS, PLANE, 128)
    work = [pltpu.VMEM((2, PLANE, 128), F32), pltpu.VMEM((4, PLANE, 128), F32)]
    uvs = call(assemble, shape(2 * STEPS, PLANE, 128), *parts, scratch=work)
    ws = None
    pieces, before = (), ()
    for active in range(depth - 1, -1, -1):
        outs = [stack]
        if active > 0:
            outs = outs + [plane, shape(64, 128), shape(24, 128)]
        layers, *sent = call(
            functools.partial(section, active), outs, uvs, *pieces, *before, scratch=[pltpu.VMEM((PLANE, 128), F32)]
        )
        before = (layers,)
        if active > 0:
            main, side, strip = sent

            def down(where):
                def to(z, y, x):
                    _, ty, tx = where(z, y, x)
                    return (z - 1, ty, tx)
                return to

            def over(z, y, x):
                return (z, y ^ 2, x)

            def corner_of(z, y, x):
                _, ty, tx = beside(z, y, x)
                return (z, ty ^ 2, tx)

            main = moved(main, down(lambda z, y, x: (z, y, x)))
            halo = moved(strip, down(over))
            side = moved(side, down(beside))
            edge_piece = moved(strip, down(corner_of))
            main, halo, side, edge_piece = lax.optimization_barrier((main, halo, side, edge_piece))
            pieces = (main, to_other(main), side, halo, to_other(halo), edge_piece)
            if ws is None:
                ws = call(assemble_w, stack, after(uvw, side), *parts[1:], scratch=work)
    count = STEPS // 2 + 1
    kept, given = call(
        smooth,
        [shape(STEPS, 128, 128), shape(count, 128, 128)],
        layers, ws,
        scratch=[
            pltpu.VMEM((PLANE, 128), F32), pltpu.VMEM((STEPS, 128, 128), F32), pltpu.VMEM((256, 128), jnp.bfloat16)
        ],
    )
    given = to_other(given)
    tile, top, bottom = call(
        ends, [shape(STEPS, 128, 128), shape(RADIUS + 1, 128, 128), shape(RADIUS - 1, 128, 128)], kept, given
    )
    below = moved(top, lambda z, y, x: (z + 1, y, x))
    over = moved(bottom, lambda z, y, x: (z - 1, y, x))
    return call(finish, shape(LAYERS, 128, 128), tile, below, over, passive)


def solution(mesh):
    spec = P(*AXES)
    return jax.shard_map(
        per_device, mesh=mesh, in_specs=(spec,) * 4, out_specs=spec, check_vma=False
    )
```

```python
import functools
import math

import jax
import jax.numpy as jnp
from jax import lax
from jax.experimental import pallas as pl
from jax.experimental.pallas import tpu as pltpu
from jax.sharding import PartitionSpec as P

RADIUS = 4
PENALTY = 40.0
EXPONENT = PENALTY + math.log(5.0) / math.log(0.5)
SMOOTH = 0.001
AXES = ("gz", "gy", "gx")
F32 = jnp.float32

LAYERS = 16
STEPS = LAYERS + 1
PLANE = 288
VECTORS = PLANE // 8
REACH = RADIUS + STEPS
SLABS = ((16, 15, 14, 3), (13, 12, 11, 8, 0), (10, 9, 7, 6, 5, 2), (4, 1))
FOLDED = 32
SLAB_ROWS = 3 * 128 + FOLDED + 64
CORNER_ROWS = 3 * 24 + 16 + 8


def width_of(layer):
    return RADIUS + layer


def rows_of(layer):
    return -(-width_of(layer) // 8) * 8


MICROSECONDS = {"all_terms": 2.5, "assemble": 2.5, "section": 2.6, "smooth": 4.0, "finish": 3.0, "ends": 1.0}


def strips():
    out = []
    for slab, layers in enumerate(SLABS):
        at = 0
        for layer in layers:
            for name in ("u", "v"):
                out.append((name, layer, slab, at))
                at += width_of(layer)
        assert at <= (128 if slab < 3 else FOLDED)
    return out


def row_places():
    places, at = {}, 0
    for layer in range(STEPS):
        for name in ("u", "v", "w"):
            if (name, layer) == ("w", 0):
                continue
            rows = 8 if name == "w" else rows_of(layer)
            places[name, layer] = (at, rows)
            at += rows
    return places, at


ROW_PLACES, ROW_TOTAL = row_places()


def moved(value, where):
    sizes = tuple(lax.axis_size(axis) for axis in AXES)
    pairs = []
    for z in range(sizes[0]):
        for y in range(sizes[1]):
            for x in range(sizes[2]):
                to = where(z, y, x)
                if to is not None:
                    tz, ty, tx = to[0] % sizes[0], to[1], to[2] % sizes[2]
                    pairs.append(((z * sizes[1] + y) * sizes[2] + x, (tz * sizes[1] + ty) * sizes[2] + tx))
    return lax.ppermute(value, AXES, pairs)


def shape(*dims):
    return jax.ShapeDtypeStruct(dims, F32)


def call(kernel, outs, *args, scratch=(), in_specs=None, **more):
    name = kernel.func.__name__ if isinstance(kernel, functools.partial) else kernel.__name__
    if in_specs is not None:
        more["in_specs"] = in_specs
    return pl.pallas_call(
        kernel,
        out_shape=outs,
        scratch_shapes=list(scratch),
        compiler_params=pltpu.CompilerParams(vmem_limit_bytes=40 * 1024 * 1024),
        cost_estimate=pl.CostEstimate(flops=0, bytes_accessed=int(MICROSECONDS.get(name, 0.5) * 3e6), transcendentals=0),
        name=name,
        **more,
    )(*args)


def lanes(rows):
    return lax.broadcasted_iota(jnp.int32, (rows, 128), 1)


def core():
    return lax.axis_index("gy") & 1


def seam():
    return lax.axis_index("gy") >> 1


def one_if(condition):
    return jnp.where(condition, 1.0, 0.0)


def outside():
    x, c = lax.axis_index("gx"), core()
    return ((c == 0) & (x == 0)) | ((c == 1) & (x == lax.axis_size("gx") - 1))


def plain_to_plane(ref):
    return jnp.concatenate([ref[pl.ds(t, 8, stride=VECTORS), :] for t in range(VECTORS)], axis=0)


def plane_to_plain(value, ref):
    for t in range(VECTORS):
        ref[pl.ds(t, 8, stride=VECTORS), :] = value[8 * t:8 * t + 8]


def aligned(value, to):
    return pl.multiple_of(value, to)


def power40(p):
    x = p + p
    x2 = x * x
    x4 = x2 * x2
    x8 = x4 * x4
    x32 = x8 * x8
    x32 = x32 * x32
    return x32 * x8


def power39(p):
    x = p + p
    x2 = x * x
    x4 = x2 * x2
    x8 = x4 * x4
    x32 = x8 * x8
    x32 = x32 * x32
    return x32 * (x4 * (x2 * x))


def edges(p_ref, inner_ref, outer_ref, left_ref, right_ref, turned):
    lane = lanes(128)
    c = core()
    packed = jnp.zeros((128, 128), F32)
    for layer in range(LAYERS):
        inner_ref[pl.ds(layer, 1), :] = p_ref[layer, pl.ds(127 * (1 - c), 1), :]
        outer_ref[pl.ds(layer, 1), :] = p_ref[layer, pl.ds(127 * c, 1), :]
        rolled = pltpu.roll(p_ref[layer], 2 * layer + 1, 1)
        packed = jnp.where((lane >> 1) == layer, rolled, packed)
    turned[...] = packed.T
    right_ref[...] = turned[pl.ds(0, 16, stride=2), :]
    left_ref[...] = turned[pl.ds(1, 16, stride=2), :]


def norm_of(position, extent):
    def missing(k):
        k = jnp.maximum(k, 0)
        return (k * (k + 1)) >> 1

    return ((RADIUS + 1) ** 2 - missing(RADIUS - position) - missing(RADIUS - (extent - 1 - position))).astype(F32)


def terms(total, density, sens, p39):
    total = jnp.maximum(total, 1e-30)
    offset = PENALTY * math.log(2.0) / EXPONENT
    smax = jnp.exp(jnp.log(total) * (1.0 / EXPONENT) - offset)
    gap = density - smax
    half = 0.5 * gap * lax.rsqrt(gap * gap + SMOOTH)
    low = 0.5 - half
    top = (0.5 + half) * (2.0 * PENALTY / EXPONENT) * smax
    h = top / total
    return h * sens, h * p39, low, total / top


def plane_norms(sizes):
    row0 = lax.axis_index("gy") * 128
    col0 = lax.axis_index("gx") * 128
    rows = lax.broadcasted_iota(jnp.int32, (128, 128), 0) + row0
    cols = lax.broadcasted_iota(jnp.int32, (128, 128), 1) + col0
    return norm_of(rows, sizes[1] * 128) * norm_of(cols, sizes[2] * 128)


def neighbours(p, layer, inner_ref, outer_ref, beside, powers):
    c = core()
    lane = lanes(128)
    own = power40(p)
    powers[pl.ds(8, 128), :] = own
    y = lax.axis_index("gy")
    there = one_if((y == 1) | (y == 2))
    powers[pl.ds(7 + 129 * (1 - c), 1), :] = power40(inner_ref[pl.ds(layer, 1), :])
    powers[pl.ds(7 + 129 * c, 1), :] = power40(outer_ref[pl.ds(layer, 1), :]) * there
    side = pltpu.roll(beside, (128 - (2 * layer + 1)) % 128, 1)
    right = jnp.where(lane == 127, side, pltpu.roll(own, 127, 1))
    left = jnp.where(lane == 0, side, pltpu.roll(own, 1, 1))
    return (own + right) + left + (powers[pl.ds(7, 128), :] + powers[pl.ds(9, 128), :])


def columns_beside(left_ref, right_ref, turned):
    x = lax.axis_index("gx")
    turned[...] = jnp.zeros((128, 128), F32)
    turned[pl.ds(0, 16, stride=2), :] = right_ref[...] * one_if(x < lax.axis_size("gx") - 1)
    turned[pl.ds(1, 16, stride=2), :] = left_ref[...] * one_if(x > 0)
    return power40(turned[...].T)


def all_terms(sizes, p_ref, f_ref, s_ref, above_ref, inner_ref, outer_ref, left_ref, right_ref, uvw_ref, powers, turned):
    beside = columns_beside(left_ref, right_ref, turned)
    norms = 1.0 / plane_norms(sizes)
    gz = lax.axis_index("gz")
    layer0 = gz * LAYERS
    uvw_ref[0] = s_ref[0]
    uvw_ref[STEPS] = power39(p_ref[0])
    uvw_ref[2 * STEPS] = norms * (1.0 / norm_of(0 * layer0, sizes[0] * LAYERS))
    for layer in range(1, STEPS):
        total = neighbours(p_ref[layer - 1], layer - 1, inner_ref, outer_ref, beside, powers)
        if layer < LAYERS:
            p, f, s = p_ref[layer], f_ref[layer], s_ref[layer]
        else:
            p, f, s = above_ref[0], above_ref[1], above_ref[2]
        u, v, low, inverse = terms(total, f, s, power39(p))
        if layer == LAYERS:
            there = one_if(gz < sizes[0] - 1)
            u, v = u * there, v * there
        norm_z = norm_of(layer0 + layer, sizes[0] * LAYERS)
        uvw_ref[layer] = u
        uvw_ref[STEPS + layer] = v
        uvw_ref[2 * STEPS + layer] = low * inverse * (norms * (1.0 / norm_z))


def plane_of(uvw_ref, name, layer):
    return uvw_ref.at[STEPS * "uvw".index(name) + layer]


def pack_rows(uvw_ref, rows_ref):
    c = core()
    for (name, layer), (at, rows) in ROW_PLACES.items():
        start = aligned(c * (128 - rows), 8)
        rows_ref[pl.ds(at, rows), :] = plane_of(uvw_ref, name, layer)[pl.ds(start, rows), :]


def pack(uvw_ref, same_ref, cross_ref, keep_ref, give_ref):
    c = core()

    def put(at, left, right):
        count = left.shape[0]
        same_ref[pl.ds(at, count), :] = jnp.where(c == 0, right, left)
        cross_ref[pl.ds(at, count), :] = jnp.where(c == 0, left, right)

    def put_corner(at, rows, left, right):
        first, last = slice(0, rows), slice(left.shape[0] - rows, left.shape[0])
        keep_ref[pl.ds(at, rows), :] = jnp.where(c == 0, left[first], right[last])
        give_ref[pl.ds(at, rows), :] = jnp.where(c == 0, right[first], left[last])

    lane = lanes(128)
    for slab in range(4):
        left = right = jnp.zeros((128, 128), F32)
        for name, layer, where, at in strips():
            if where == slab:
                width = width_of(layer)
                plane = plane_of(uvw_ref, name, layer)[...]
                inside = (lane >= at) & (lane < at + width)
                left = jnp.where(inside, pltpu.roll(plane, at, 1) if at else plane, left)
                right = jnp.where(inside, pltpu.roll(plane, (at + width) % 128, 1), right)
        if slab < 3:
            put(128 * slab, left, right)
            put_corner(24 * slab, 24, left, right)
            continue
        put_corner(72, 16, left, right)
        folded = []
        for value in (left, right):
            total = value[:FOLDED]
            for i in range(1, 4):
                total = total + pltpu.roll(value[FOLDED * i:FOLDED * (i + 1)], FOLDED * i, 1)
            folded.append(total)
        put(384, *folded)
    lane = lanes(64)
    left = right = jnp.zeros((64, 128), F32)
    for layer in range(1, STEPS):
        ref = plane_of(uvw_ref, "w", layer)
        for half in range(2):
            plane = ref[pl.ds(64 * half, 64), :]
            at = 64 * half + RADIUS * (layer - 1)
            inside = (lane >= at) & (lane < at + RADIUS)
            left = jnp.where(inside, pltpu.roll(plane, at, 1) if at else plane, left)
            right = jnp.where(inside, pltpu.roll(plane, (at + RADIUS) % 128, 1), right)
    put(384 + FOLDED, left, right)
    put_corner(88, 8, left, right)


def pick_corner(keep_ref, got_ref, corner_ref):
    corner_ref[...] = jnp.where((core() ^ seam()) == 1, keep_ref[...], got_ref[...])


def slab_plane(plain, same, cross, corner):
    c = core()
    inside = one_if(jnp.logical_not(outside()))
    plain[pl.ds(256, 32), :] = jnp.zeros((32, 128), F32)
    plain[pl.ds(aligned(c * 128, 128), 128), :] = same * inside
    plain[pl.ds(aligned((1 - c) * 128, 128), 128), :] = cross * inside
    rows = corner.shape[0]
    plain[pl.ds(aligned(256 + seam() * (32 - rows), 8), rows), :] = corner * inside


def full_plane(plain, name, layer, uvw_ref, other_ref, got_ref, shared_ref):
    c = core()
    plain[pl.ds(aligned(c * 128, 128), 128), :] = plane_of(uvw_ref, name, layer)[...]
    plain[pl.ds(aligned((1 - c) * 128, 128), 128), :] = plane_of(other_ref, name, layer)[...]
    plain[pl.ds(256, 32), :] = jnp.zeros((32, 128), F32)
    start, rows = ROW_PLACES[name, layer]
    here = pl.ds(start, rows)
    to = aligned(256 + seam() * (32 - rows), 8)
    plain[pl.ds(to, rows), :] = jnp.where((c ^ seam()) == 1, got_ref[here, :], shared_ref[here, :])
    return plain_to_plane(plain)


def with_columns(base, columns, at, width):
    c = core()
    lane = lanes(PLANE)
    columns = pltpu.roll(columns, (128 - at - (1 - c) * width) & 127, 1)
    begin = (1 - c) * (128 - width)
    return jnp.where((lane >= begin) & (lane < begin + width), columns, base)


def assemble(
    uvw_ref, other_ref, got_ref, shared_ref, same_ref, cross_ref, corner_ref, uv_ref, plain, slabs
):
    c = core()
    for slab in range(4):
        if slab < 3:
            here = pl.ds(128 * slab, 128)
            same, cross = same_ref[here, :], cross_ref[here, :]
            here = pl.ds(24 * slab, 24)
        else:
            here = pl.ds(384, FOLDED)
            same, cross = (
                jnp.concatenate([value] + [pltpu.roll(value, 128 - FOLDED * i, 1) for i in range(1, 4)], axis=0)
                for value in (same_ref[here, :], cross_ref[here, :])
            )
            here = pl.ds(72, 16)
        corner = corner_ref[here, :]
        slot = plain.at[slab % 2]
        slab_plane(slot, same, cross, corner)
        slabs[slab] = plain_to_plane(slot)
    for place, (name, layer, slab, at) in enumerate(strips()):
        base = full_plane(plain.at[place % 2], name, layer, uvw_ref, other_ref, got_ref, shared_ref)
        uv_ref[2 * (LAYERS - layer) + (name == "v")] = with_columns(base, slabs[slab], at, width_of(layer))


def assemble_w(
    uvw_ref, other_ref, got_ref, shared_ref, same_ref, cross_ref, corner_ref, w_ref, plain, slabs
):
    c = core()

    def unfolded(ref):
        value = ref[pl.ds(384 + FOLDED, 64), :]
        return jnp.concatenate([value, pltpu.roll(value, 64, 1)], axis=0)

    here = pl.ds(88, 8)
    corner = corner_ref[here, :]
    corner = pltpu.roll(corner, 64 * seam(), 1)
    slab_plane(plain.at[0], unfolded(same_ref), unfolded(cross_ref), corner)
    slabs[0] = plain_to_plane(plain.at[0])
    for layer in range(1, STEPS):
        base = full_plane(plain.at[layer % 2], "w", layer, uvw_ref, other_ref, got_ref, shared_ref)
        w_ref[layer] = with_columns(base, slabs[0], RADIUS * (layer - 1), RADIUS)
    row = lax.broadcasted_iota(jnp.int32, (PLANE, 128), 0)
    col = lax.broadcasted_iota(jnp.int32, (PLANE, 128), 1)
    a = seam()
    row = jnp.where((a == 1) & (row >= 256), row - PLANE, row) + 256 * a
    width = jnp.where(c == 0, 108, 20)
    col = jnp.where((c == 0) & (col >= width), col - 128, jnp.where((c == 1) & (col < width), col + 128, col))
    col = col + 128 * lax.axis_index("gx")
    rows, cols = 128 * lax.axis_size("gy"), 128 * lax.axis_size("gx")
    norm = norm_of(row, rows) * norm_of(col, cols) * norm_of(0 * a, LAYERS * lax.axis_size("gz"))
    inside = (row >= 0) & (row < rows) & (col >= 0) & (col < cols)
    plain[0] = jnp.where(inside, 1.0 / jnp.where(inside, norm, 1.0), 0.0)
    w_ref[0] = plain_to_plane(plain.at[0])


def step_down(values, u_ref, v_ref, out_ref):
    new = []
    for t, value in enumerate(values):
        before = values[t - 1] if t > 0 else pltpu.roll(values[-1], 1, 0)
        behind = values[t + 1] if t < VECTORS - 1 else pltpu.roll(values[0], 7, 0)
        total = (value + before) + (behind + pltpu.roll(value, 1, 1)) + pltpu.roll(value, 127, 1)
        here = pl.ds(8 * t, 8)
        new.append(u_ref[here, :] + v_ref[here, :] * total)
        out_ref[here, :] = new[-1]
    return new


def set_carry(carry, main_ref, other_ref, outer_ref, halo_ref, halo_other_ref, halo_outer_ref):
    c = core()
    lane = lanes(64)
    mine = (lane >> 6) == c
    inside = one_if(jnp.logical_not(outside()))
    for i in range(4):
        rows = pl.ds(64 * (i % 2), 64)
        own, other = main_ref[rows, :], other_ref[rows, :]
        if i < 2:
            value = jnp.where(mine, own, other)
        else:
            value = pltpu.roll(jnp.where(mine, other, own), 64, 1)
        outer = pltpu.roll(outer_ref[...], (128 - 32 * i) % 128, 1) if i else outer_ref[...]
        outer = outer * inside
        begin = (1 - c) * (128 - REACH)
        value = jnp.where((lane >= begin) & (lane < begin + REACH), outer, value)
        carry[pl.ds(64 * i, 64), :] = value
    lane = lanes(24)
    value = jnp.where((lane >> 6) == c, halo_ref[...], halo_other_ref[...])
    begin = (1 - c) * (128 - REACH)
    value = jnp.where((lane >= begin) & (lane < begin + REACH), halo_outer_ref[...] * inside, value)
    carry[pl.ds(256, 32), :] = jnp.zeros((32, 128), F32)
    carry[pl.ds(aligned(256 + 8 * seam(), 8), 24), :] = value


def section(active, *refs):
    uv_ref, refs = refs[0], refs[1:]
    pieces, before_ref = (), None
    if active is not None and len(refs) > 5:
        pieces, before_ref, refs = refs[:6], refs[6], refs[7:]
    if len(refs) == 5:
        layers_ref, main_ref, outer_ref, halo_ref, carry = refs
    else:
        layers_ref, carry = refs
        main_ref = None

    @pl.when(lax.axis_index("gz") == active)
    def _():
        if pieces:
            set_carry(carry, *pieces)
            values = [carry[pl.ds(t, 8, stride=VECTORS), :] for t in range(VECTORS)]
        else:
            values = [jnp.zeros((8, 128), F32)] * VECTORS
        for layer in range(LAYERS, 0, -1):
            at = 2 * (LAYERS - layer)
            values = step_down(values, uv_ref.at[at], uv_ref.at[at + 1], layers_ref.at[layer])
        step_down(values, uv_ref.at[2 * LAYERS], uv_ref.at[2 * LAYERS + 1], layers_ref.at[0])
        if main_ref is None:
            return
        c = core()
        lane = lanes(128)
        for t in range(VECTORS):
            carry[pl.ds(t, 8, stride=VECTORS), :] = values[t]
        bottom = carry
        mine = (lane >> 6) == c
        main_ref[...] = jnp.where(mine, bottom[pl.ds(0, 128), :], pltpu.roll(bottom[pl.ds(128, 128), :], 64, 1))
        lane = lanes(64)
        slab = jnp.zeros((64, 128), F32)
        for i in range(4):
            rolled = bottom[pl.ds(64 * i, 64), :]
            rolled = pltpu.roll(rolled, 32 * i, 1) if i else rolled
            begin = (32 * i + 128 - c * 32) & 127
            slab = jnp.where(((lane - begin) & 127) < 32, rolled, slab)
        outer_ref[...] = slab
        halo_ref[...] = bottom[pl.ds(aligned((1 - seam()) * 232, 8), 24), :]

    if before_ref is not None:
        @pl.when(lax.axis_index("gz") != active)
        def _():
            layers_ref[...] = before_ref[...]


def box(values):
    two = [values[i] + values[i + 1] for i in range(len(values) - 1)]
    four = [two[i] + two[i + 2] for i in range(len(two) - 2)]
    return [four[i] + values[i + 4] for i in range(len(values) - 4)]


def smooth(layers_ref, w_ref, kept_ref, give_ref, plains, others, tent):
    c = core()
    mine = (lanes(128) >> 6) == c
    row = lax.broadcasted_iota(jnp.int32, (256, 128), 0)
    col = lax.broadcasted_iota(jnp.int32, (256, 128), 1)
    distance = (row - col + RADIUS) & 127
    weight = jnp.where(distance <= 2 * RADIUS, RADIUS + 1 - jnp.abs(distance - RADIUS), 0)
    tent[...] = weight.astype(F32).astype(jnp.bfloat16)

    def layer(k, plain):
        values = [layers_ref[k, pl.ds(8 * t, 8), :] * w_ref[k, pl.ds(8 * t, 8), :] for t in range(VECTORS)]
        first = [pltpu.roll(value, 1, 0) for value in values[VECTORS - RADIUS:]]
        last = [pltpu.roll(value, 7, 0) for value in values[:RADIUS]]
        total = jnp.concatenate(box(box(first + values + last)), axis=0)
        high = total.astype(jnp.bfloat16)
        rest = total - high.astype(F32)
        middle = rest.astype(jnp.bfloat16)
        small = (rest - middle.astype(F32)).astype(jnp.bfloat16)
        value = jnp.dot(jnp.concatenate([high, middle], axis=1), tent[...], preferred_element_type=F32)
        value = value + jnp.dot(small, tent[pl.ds(0, 128), :], preferred_element_type=F32)
        plane_to_plain(value, plain)
        kept_ref[k] = plain[pl.ds(aligned(c * 128, 128), 128), :]
        others[k] = plain[pl.ds(aligned((1 - c) * 128, 128), 128), :]

    for k in range(STEPS):
        layer(k, plains.at[k % 4])
    count = give_ref.shape[0]
    for k in range(count):
        second = others[k + count] if k + count < STEPS else jnp.zeros((128, 128), F32)
        give_ref[k] = jnp.where(mine, others[k], pltpu.roll(second, 64, 1))


def ends(kept_ref, got_ref, out_ref, top_ref, bottom_ref):
    mine = (lanes(128) >> 6) == core()
    count = got_ref.shape[0]
    for k in range(STEPS):
        other = got_ref[k] if k < count else pltpu.roll(got_ref[k - count], 64, 1)
        out_ref[k] = jnp.where(mine, kept_ref[k], other)
    top_ref[...] = out_ref[pl.ds(STEPS - RADIUS - 1, RADIUS + 1)]
    bottom_ref[...] = out_ref[pl.ds(1, RADIUS - 1)]


def finish(tile_ref, below_ref, above_ref, passive_ref, out_ref):
    gz = lax.axis_index("gz")
    has_below, has_above = one_if(gz > 0), one_if(gz < lax.axis_size("gz") - 1)

    def layer(k):
        if k < 0:
            return below_ref[k + RADIUS] * has_below
        if k == 0:
            return jnp.where(gz == 0, tile_ref[0], below_ref[RADIUS])
        if k > LAYERS:
            return above_ref[k - STEPS] * has_above
        return tile_ref[k]

    for k in range(LAYERS):
        total = layer(k) * 5.0
        for offset in range(1, RADIUS + 1):
            total = total + (layer(k - offset) + layer(k + offset)) * (5.0 - offset)
        out_ref[k] = jnp.where(passive_ref[k] > 0, 0.0, total)


def to_other(value):
    return moved(value, lambda z, y, x: (z, y ^ 1, x))


def after(value, *others):
    return lax.optimization_barrier((value,) + others)[0]


def per_device(filtered, printed, sensitivity, passive):
    sizes = tuple(lax.axis_size(axis) for axis in AXES)
    depth = sizes[0]
    plane = shape(128, 128)
    edge = shape(16, 128)

    def across(z, y, x):
        return (z, y ^ 3, x) if y in (1, 2) else None

    def beside(z, y, x):
        return (z, y ^ 1, x + (1 if y & 1 else -1))

    def same(z, y, x):
        return (z, y, x + (-1 if y & 1 else 1))

    lowest_planes = jnp.stack([printed[0], filtered[0], sensitivity[0]])
    above = moved(lowest_planes, lambda z, y, x: (z - 1, y, x))
    inner, outer, left, right = call(edges, [edge] * 4, printed, scratch=[pltpu.VMEM((128, 128), F32)])
    from_left = moved(right, lambda z, y, x: (z, y, x + 1))
    from_right = moved(left, lambda z, y, x: (z, y, x - 1))
    outer = moved(outer, lambda z, y, x: (z, y ^ 3, x))
    inner = to_other(inner)
    uvw = call(
        functools.partial(all_terms, sizes), shape(3 * STEPS, 128, 128),
        printed, filtered, sensitivity, above, inner, outer, from_left, from_right,
        scratch=[pltpu.VMEM((144, 128), F32), pltpu.VMEM((128, 128), F32)],
    )
    slab, corner = shape(SLAB_ROWS, 128), shape(CORNER_ROWS, 128)
    rows = call(pack_rows, shape(ROW_TOTAL, 128), uvw)
    got = moved(rows, across)
    to_same, to_cross, keep, give = call(pack, [slab, slab, corner, corner], after(uvw, rows))
    from_same = moved(to_same, same)
    from_cross = moved(to_cross, beside)
    corner = call(pick_corner, corner, keep, to_other(give))
    corner = moved(corner, lambda z, y, x: (z, 3 - y, x + (1 if y & 1 else -1)))
    other = to_other(uvw)
    shared = to_other(after(got, from_same, from_cross, corner))
    parts = (uvw, other, got, shared, from_same, from_cross, corner)
    stack = shape(STEPS, PLANE, 128)
    work = [pltpu.VMEM((2, PLANE, 128), F32), pltpu.VMEM((4, PLANE, 128), F32)]
    uvs = call(assemble, shape(2 * STEPS, PLANE, 128), *parts, scratch=work)
    ws = None
    pieces, before = (), ()
    for active in range(depth - 1, -1, -1):
        outs = [stack]
        if active > 0:
            outs = outs + [plane, shape(64, 128), shape(24, 128)]
        layers, *sent = call(
            functools.partial(section, active), outs, uvs, *pieces, *before, scratch=[pltpu.VMEM((PLANE, 128), F32)]
        )
        before = (layers,)
        if active > 0:
            main, side, strip = sent

            def down(where):
                def to(z, y, x):
                    _, ty, tx = where(z, y, x)
                    return (z - 1, ty, tx)
                return to

            def only(where):
                return lambda z, y, x: where(z, y, x) if z == active else None

            def over(z, y, x):
                return (z, y ^ 2, x)

            def corner_of(z, y, x):
                _, ty, tx = beside(z, y, x)
                return (z, ty ^ 2, tx)

            main = moved(main, down(lambda z, y, x: (z, y, x)))
            halo = moved(strip, down(over))
            side = moved(side, down(beside))
            edge_piece = moved(strip, only(down(corner_of)))
            main, halo, side, edge_piece = lax.optimization_barrier((main, halo, side, edge_piece))
            pieces = (main, to_other(main), side, halo, to_other(halo), edge_piece)
            if ws is None:
                ws = call(assemble_w, stack, after(uvw, side), *parts[1:], scratch=work)
    count = STEPS // 2 + 1
    kept, given = call(
        smooth,
        [shape(STEPS, 128, 128), shape(count, 128, 128)],
        layers, ws,
        scratch=[
            pltpu.VMEM((4, PLANE, 128), F32), pltpu.VMEM((STEPS, 128, 128), F32), pltpu.VMEM((256, 128), jnp.bfloat16)
        ],
    )
    given = to_other(given)
    tile, top, bottom = call(
        ends, [shape(STEPS, 128, 128), shape(RADIUS + 1, 128, 128), shape(RADIUS - 1, 128, 128)], kept, given
    )
    below = moved(top, lambda z, y, x: (z + 1, y, x))
    over = moved(bottom, lambda z, y, x: (z - 1, y, x))
    return call(finish, shape(LAYERS, 128, 128), tile, below, over, passive)


def solution(mesh):
    spec = P(*AXES)
    return jax.shard_map(
        per_device, mesh=mesh, in_specs=(spec,) * 4, out_specs=spec, check_vma=False
    )
```

```python
import functools
import math

import jax
import jax.numpy as jnp
from jax import lax
from jax.experimental import pallas as pl
from jax.experimental.pallas import tpu as pltpu
from jax.sharding import PartitionSpec as P

RADIUS = 4
PENALTY = 40.0
EXPONENT = PENALTY + math.log(5.0) / math.log(0.5)
SMOOTH = 0.001
AXES = ("gz", "gy", "gx")
F32 = jnp.float32

LAYERS = 16
STEPS = LAYERS + 1
PLANE = 288
VECTORS = PLANE // 8
REACH = RADIUS + STEPS
SLABS = ((16, 15, 14, 3), (13, 12, 11, 8, 0), (10, 9, 7, 6, 5, 2), (4, 1))
FOLDED = 32
SLAB_ROWS = 3 * 128 + FOLDED + 64
CORNER_ROWS = 3 * 24 + 16 + 8


def width_of(layer):
    return RADIUS + layer


def rows_of(layer):
    return -(-width_of(layer) // 8) * 8


MICROSECONDS = {"all_terms": 2.5, "assemble": 2.5, "section": 2.6, "smooth": 4.0, "finish": 3.0, "ends": 1.0}


def strips():
    out = []
    for slab, layers in enumerate(SLABS):
        at = 0
        for layer in layers:
            for name in ("u", "v"):
                out.append((name, layer, slab, at))
                at += width_of(layer)
        assert at <= (128 if slab < 3 else FOLDED)
    return out


def row_places():
    places, at = {}, 0
    for layer in range(STEPS):
        for name in ("u", "v", "w"):
            if (name, layer) == ("w", 0):
                continue
            rows = 8 if name == "w" else rows_of(layer)
            places[name, layer] = (at, rows)
            at += rows
    return places, at


ROW_PLACES, ROW_TOTAL = row_places()


def moved(value, where):
    sizes = tuple(lax.axis_size(axis) for axis in AXES)
    pairs = []
    for z in range(sizes[0]):
        for y in range(sizes[1]):
            for x in range(sizes[2]):
                to = where(z, y, x)
                if to is not None:
                    tz, ty, tx = to[0] % sizes[0], to[1], to[2] % sizes[2]
                    pairs.append(((z * sizes[1] + y) * sizes[2] + x, (tz * sizes[1] + ty) * sizes[2] + tx))
    return lax.ppermute(value, AXES, pairs)


def shape(*dims):
    return jax.ShapeDtypeStruct(dims, F32)


def call(kernel, outs, *args, scratch=(), in_specs=None, **more):
    name = kernel.func.__name__ if isinstance(kernel, functools.partial) else kernel.__name__
    if in_specs is not None:
        more["in_specs"] = in_specs
    return pl.pallas_call(
        kernel,
        out_shape=outs,
        scratch_shapes=list(scratch),
        compiler_params=pltpu.CompilerParams(vmem_limit_bytes=40 * 1024 * 1024),
        cost_estimate=pl.CostEstimate(flops=0, bytes_accessed=int(MICROSECONDS.get(name, 0.5) * 3e6), transcendentals=0),
        name=name,
        **more,
    )(*args)


def lanes(rows):
    return lax.broadcasted_iota(jnp.int32, (rows, 128), 1)


def core():
    return lax.axis_index("gy") & 1


def seam():
    return lax.axis_index("gy") >> 1


def one_if(condition):
    return jnp.where(condition, 1.0, 0.0)


def outside():
    x, c = lax.axis_index("gx"), core()
    return ((c == 0) & (x == 0)) | ((c == 1) & (x == lax.axis_size("gx") - 1))


def plain_to_plane(ref):
    return jnp.concatenate([ref[pl.ds(t, 8, stride=VECTORS), :] for t in range(VECTORS)], axis=0)


def plane_to_plain(value, ref):
    for t in range(VECTORS):
        ref[pl.ds(t, 8, stride=VECTORS), :] = value[8 * t:8 * t + 8]


def aligned(value, to):
    return pl.multiple_of(value, to)


def power40(p):
    x = p + p
    x2 = x * x
    x4 = x2 * x2
    x8 = x4 * x4
    x32 = x8 * x8
    x32 = x32 * x32
    return x32 * x8


def power39(p):
    x = p + p
    x2 = x * x
    x4 = x2 * x2
    x8 = x4 * x4
    x32 = x8 * x8
    x32 = x32 * x32
    return x32 * (x4 * (x2 * x))


def edges(p_ref, f_ref, s_ref, lowest_ref, inner_ref, outer_ref, left_ref, right_ref, turned, sems):
    copies = [pltpu.make_async_copy(ref.at[0], lowest_ref.at[i + 1], sems.at[i]) for i, ref in enumerate((f_ref, s_ref))]
    for copy in copies:
        copy.start()
    lowest_ref[0] = p_ref[0]
    lane = lanes(128)
    c = core()
    packed = jnp.zeros((128, 128), F32)
    for layer in range(LAYERS):
        inner_ref[pl.ds(layer, 1), :] = p_ref[layer, pl.ds(127 * (1 - c), 1), :]
        outer_ref[pl.ds(layer, 1), :] = p_ref[layer, pl.ds(127 * c, 1), :]
        rolled = pltpu.roll(p_ref[layer], 2 * layer + 1, 1)
        packed = jnp.where((lane >> 1) == layer, rolled, packed)
    turned[...] = packed.T
    right_ref[...] = turned[pl.ds(0, 16, stride=2), :]
    left_ref[...] = turned[pl.ds(1, 16, stride=2), :]
    for copy in copies:
        copy.wait()


def norm_of(position, extent):
    def missing(k):
        k = jnp.maximum(k, 0)
        return (k * (k + 1)) >> 1

    return ((RADIUS + 1) ** 2 - missing(RADIUS - position) - missing(RADIUS - (extent - 1 - position))).astype(F32)


def terms(total, density, sens, p39):
    total = jnp.maximum(total, 1e-30)
    offset = PENALTY * math.log(2.0) / EXPONENT
    smax = jnp.exp(jnp.log(total) * (1.0 / EXPONENT) - offset)
    gap = density - smax
    half = 0.5 * gap * lax.rsqrt(gap * gap + SMOOTH)
    low = 0.5 - half
    top = (0.5 + half) * (2.0 * PENALTY / EXPONENT) * smax
    h = top / total
    return h * sens, h * p39, low, total / top


def plane_norms(sizes):
    row0 = lax.axis_index("gy") * 128
    col0 = lax.axis_index("gx") * 128
    rows = lax.broadcasted_iota(jnp.int32, (128, 128), 0) + row0
    cols = lax.broadcasted_iota(jnp.int32, (128, 128), 1) + col0
    return norm_of(rows, sizes[1] * 128) * norm_of(cols, sizes[2] * 128)


def neighbours(p, layer, inner_ref, outer_ref, beside, powers):
    c = core()
    lane = lanes(128)
    own = power40(p)
    powers[pl.ds(8, 128), :] = own
    y = lax.axis_index("gy")
    there = one_if((y == 1) | (y == 2))
    powers[pl.ds(7 + 129 * (1 - c), 1), :] = power40(inner_ref[pl.ds(layer, 1), :])
    powers[pl.ds(7 + 129 * c, 1), :] = power40(outer_ref[pl.ds(layer, 1), :]) * there
    side = pltpu.roll(beside, (128 - (2 * layer + 1)) % 128, 1)
    right = jnp.where(lane == 127, side, pltpu.roll(own, 127, 1))
    left = jnp.where(lane == 0, side, pltpu.roll(own, 1, 1))
    return (own + right) + left + (powers[pl.ds(7, 128), :] + powers[pl.ds(9, 128), :])


def columns_beside(left_ref, right_ref, turned):
    x = lax.axis_index("gx")
    turned[...] = jnp.zeros((128, 128), F32)
    turned[pl.ds(0, 16, stride=2), :] = right_ref[...] * one_if(x < lax.axis_size("gx") - 1)
    turned[pl.ds(1, 16, stride=2), :] = left_ref[...] * one_if(x > 0)
    return power40(turned[...].T)


def all_terms(
    sizes, p_ref, f_hbm, s_hbm, above_ref, inner_ref, outer_ref, left_ref, right_ref,
    uvw_ref, powers, turned, f_ref, s_ref, sems,
):
    def fetch(part):
        here = pl.ds(4 * part, 4)
        return [
            pltpu.make_async_copy(hbm.at[here], ref.at[here], sems.at[i, part])
            for i, (hbm, ref) in enumerate(((f_hbm, f_ref), (s_hbm, s_ref)))
        ]

    for part in range(LAYERS // 4):
        for copy in fetch(part):
            copy.start()
    beside = columns_beside(left_ref, right_ref, turned)
    norms = 1.0 / plane_norms(sizes)
    gz = lax.axis_index("gz")
    layer0 = gz * LAYERS
    for copy in fetch(0):
        copy.wait()
    uvw_ref[0] = s_ref[0]
    uvw_ref[STEPS] = power39(p_ref[0])
    uvw_ref[2 * STEPS] = norms * (1.0 / norm_of(0 * layer0, sizes[0] * LAYERS))
    for layer in range(1, STEPS):
        if layer % 4 == 0 and layer < LAYERS:
            for copy in fetch(layer // 4):
                copy.wait()
        total = neighbours(p_ref[layer - 1], layer - 1, inner_ref, outer_ref, beside, powers)
        if layer < LAYERS:
            p, f, s = p_ref[layer], f_ref[layer], s_ref[layer]
        else:
            p, f, s = above_ref[0], above_ref[1], above_ref[2]
        u, v, low, inverse = terms(total, f, s, power39(p))
        if layer == LAYERS:
            there = one_if(gz < sizes[0] - 1)
            u, v = u * there, v * there
        norm_z = norm_of(layer0 + layer, sizes[0] * LAYERS)
        uvw_ref[layer] = u
        uvw_ref[STEPS + layer] = v
        uvw_ref[2 * STEPS + layer] = low * inverse * (norms * (1.0 / norm_z))


def plane_of(uvw_ref, name, layer):
    return uvw_ref.at[STEPS * "uvw".index(name) + layer]


def pack_rows(uvw_ref, rows_ref):
    c = core()
    for (name, layer), (at, rows) in ROW_PLACES.items():
        start = aligned(c * (128 - rows), 8)
        rows_ref[pl.ds(at, rows), :] = plane_of(uvw_ref, name, layer)[pl.ds(start, rows), :]


def pack(uvw_ref, same_ref, cross_ref, keep_ref, give_ref):
    c = core()

    def put(at, left, right):
        count = left.shape[0]
        same_ref[pl.ds(at, count), :] = jnp.where(c == 0, right, left)
        cross_ref[pl.ds(at, count), :] = jnp.where(c == 0, left, right)

    def put_corner(at, rows, left, right):
        first, last = slice(0, rows), slice(left.shape[0] - rows, left.shape[0])
        keep_ref[pl.ds(at, rows), :] = jnp.where(c == 0, left[first], right[last])
        give_ref[pl.ds(at, rows), :] = jnp.where(c == 0, right[first], left[last])

    lane = lanes(128)
    for slab in range(4):
        left = right = jnp.zeros((128, 128), F32)
        for name, layer, where, at in strips():
            if where == slab:
                width = width_of(layer)
                plane = plane_of(uvw_ref, name, layer)[...]
                inside = (lane >= at) & (lane < at + width)
                left = jnp.where(inside, pltpu.roll(plane, at, 1) if at else plane, left)
                right = jnp.where(inside, pltpu.roll(plane, (at + width) % 128, 1), right)
        if slab < 3:
            put(128 * slab, left, right)
            put_corner(24 * slab, 24, left, right)
            continue
        put_corner(72, 16, left, right)
        folded = []
        for value in (left, right):
            total = value[:FOLDED]
            for i in range(1, 4):
                total = total + pltpu.roll(value[FOLDED * i:FOLDED * (i + 1)], FOLDED * i, 1)
            folded.append(total)
        put(384, *folded)
    lane = lanes(64)
    left = right = jnp.zeros((64, 128), F32)
    for layer in range(1, STEPS):
        ref = plane_of(uvw_ref, "w", layer)
        for half in range(2):
            plane = ref[pl.ds(64 * half, 64), :]
            at = 64 * half + RADIUS * (layer - 1)
            inside = (lane >= at) & (lane < at + RADIUS)
            left = jnp.where(inside, pltpu.roll(plane, at, 1) if at else plane, left)
            right = jnp.where(inside, pltpu.roll(plane, (at + RADIUS) % 128, 1), right)
    put(384 + FOLDED, left, right)
    put_corner(88, 8, left, right)


def pick_corner(keep_ref, got_ref, corner_ref):
    corner_ref[...] = jnp.where((core() ^ seam()) == 1, keep_ref[...], got_ref[...])


def slab_plane(plain, same, cross, corner):
    c = core()
    inside = one_if(jnp.logical_not(outside()))
    plain[pl.ds(256, 32), :] = jnp.zeros((32, 128), F32)
    plain[pl.ds(aligned(c * 128, 128), 128), :] = same * inside
    plain[pl.ds(aligned((1 - c) * 128, 128), 128), :] = cross * inside
    rows = corner.shape[0]
    plain[pl.ds(aligned(256 + seam() * (32 - rows), 8), rows), :] = corner * inside


def full_plane(plain, name, layer, uvw_ref, other_ref, got_ref, shared_ref):
    c = core()
    plain[pl.ds(aligned(c * 128, 128), 128), :] = plane_of(uvw_ref, name, layer)[...]
    plain[pl.ds(aligned((1 - c) * 128, 128), 128), :] = plane_of(other_ref, name, layer)[...]
    plain[pl.ds(256, 32), :] = jnp.zeros((32, 128), F32)
    start, rows = ROW_PLACES[name, layer]
    here = pl.ds(start, rows)
    to = aligned(256 + seam() * (32 - rows), 8)
    plain[pl.ds(to, rows), :] = jnp.where((c ^ seam()) == 1, got_ref[here, :], shared_ref[here, :])
    return plain_to_plane(plain)


def with_columns(base, columns, at, width):
    c = core()
    lane = lanes(PLANE)
    columns = pltpu.roll(columns, (128 - at - (1 - c) * width) & 127, 1)
    begin = (1 - c) * (128 - width)
    return jnp.where((lane >= begin) & (lane < begin + width), columns, base)


def assemble(
    uvw_ref, other_ref, got_ref, shared_ref, same_ref, cross_ref, corner_ref, uv_ref, plain, slabs
):
    c = core()
    for slab in range(4):
        if slab < 3:
            here = pl.ds(128 * slab, 128)
            same, cross = same_ref[here, :], cross_ref[here, :]
            here = pl.ds(24 * slab, 24)
        else:
            here = pl.ds(384, FOLDED)
            same, cross = (
                jnp.concatenate([value] + [pltpu.roll(value, 128 - FOLDED * i, 1) for i in range(1, 4)], axis=0)
                for value in (same_ref[here, :], cross_ref[here, :])
            )
            here = pl.ds(72, 16)
        corner = corner_ref[here, :]
        slot = plain.at[slab % 2]
        slab_plane(slot, same, cross, corner)
        slabs[slab] = plain_to_plane(slot)
    for place, (name, layer, slab, at) in enumerate(strips()):
        base = full_plane(plain.at[place % 2], name, layer, uvw_ref, other_ref, got_ref, shared_ref)
        uv_ref[2 * (LAYERS - layer) + (name == "v")] = with_columns(base, slabs[slab], at, width_of(layer))


def assemble_w(
    uvw_ref, other_ref, got_ref, shared_ref, same_ref, cross_ref, corner_ref, w_ref, plain, slabs
):
    c = core()

    def unfolded(ref):
        value = ref[pl.ds(384 + FOLDED, 64), :]
        return jnp.concatenate([value, pltpu.roll(value, 64, 1)], axis=0)

    here = pl.ds(88, 8)
    corner = corner_ref[here, :]
    corner = pltpu.roll(corner, 64 * seam(), 1)
    slab_plane(plain.at[0], unfolded(same_ref), unfolded(cross_ref), corner)
    slabs[0] = plain_to_plane(plain.at[0])
    for layer in range(1, STEPS):
        base = full_plane(plain.at[layer % 2], "w", layer, uvw_ref, other_ref, got_ref, shared_ref)
        w_ref[layer] = with_columns(base, slabs[0], RADIUS * (layer - 1), RADIUS)
    row = lax.broadcasted_iota(jnp.int32, (PLANE, 128), 0)
    col = lax.broadcasted_iota(jnp.int32, (PLANE, 128), 1)
    a = seam()
    row = jnp.where((a == 1) & (row >= 256), row - PLANE, row) + 256 * a
    width = jnp.where(c == 0, 108, 20)
    col = jnp.where((c == 0) & (col >= width), col - 128, jnp.where((c == 1) & (col < width), col + 128, col))
    col = col + 128 * lax.axis_index("gx")
    rows, cols = 128 * lax.axis_size("gy"), 128 * lax.axis_size("gx")
    norm = norm_of(row, rows) * norm_of(col, cols) * norm_of(0 * a, LAYERS * lax.axis_size("gz"))
    inside = (row >= 0) & (row < rows) & (col >= 0) & (col < cols)
    plain[0] = jnp.where(inside, 1.0 / jnp.where(inside, norm, 1.0), 0.0)
    w_ref[0] = plain_to_plane(plain.at[0])


def step_down(values, u_ref, v_ref, out_ref):
    new = []
    for t, value in enumerate(values):
        before = values[t - 1] if t > 0 else pltpu.roll(values[-1], 1, 0)
        behind = values[t + 1] if t < VECTORS - 1 else pltpu.roll(values[0], 7, 0)
        total = (value + before) + (behind + pltpu.roll(value, 1, 1)) + pltpu.roll(value, 127, 1)
        here = pl.ds(8 * t, 8)
        new.append(u_ref[here, :] + v_ref[here, :] * total)
        out_ref[here, :] = new[-1]
    return new


def set_carry(carry, main_ref, outer_ref, halo_ref, halo_outer_ref):
    c = core()
    lane = lanes(64)
    mine = (lane >> 6) == c
    inside = one_if(jnp.logical_not(outside()))
    begin = (1 - c) * (128 - REACH)
    beyond = (lane >= begin) & (lane < begin + REACH)
    for i in range(4):
        value = main_ref[pl.ds(64 * (i % 2), 64), :]
        if i >= 2:
            value = pltpu.roll(value, 64, 1)
        inner = pltpu.roll(main_ref[pl.ds(128, 64), :], (32 * (2 - c) - 32 * i) & 127, 1)
        value = jnp.where(mine, value, inner)
        outer = pltpu.roll(outer_ref[...], (128 - 32 * i) % 128, 1) if i else outer_ref[...]
        carry[pl.ds(64 * i, 64), :] = jnp.where(beyond, outer * inside, value)
    lane = lanes(24)
    beyond = (lane >= begin) & (lane < begin + REACH)
    carry[pl.ds(256, 32), :] = jnp.zeros((32, 128), F32)
    carry[pl.ds(aligned(256 + 8 * seam(), 8), 24), :] = jnp.where(beyond, halo_outer_ref[...] * inside, halo_ref[...])


def merge(main_ref, give_ref, got_ref, down_ref, halo_ref):
    down_ref[pl.ds(0, 128), :] = main_ref[...]
    down_ref[pl.ds(128, 64), :] = got_ref[pl.ds(0, 64), :]
    rows = pl.ds(64, 24)
    halo_ref[...] = jnp.where((lanes(24) >> 6) == core(), give_ref[rows, :], got_ref[rows, :])


def section(active, *refs):
    uv_ref, refs = refs[0], refs[1:]
    pieces, before_ref = (), None
    if len(refs) > 6 or len(refs) == 5 + 2:
        pieces, before_ref, refs = refs[:4], refs[4], refs[5:]
    if len(refs) == 6:
        layers_ref, main_ref, outer_ref, give_ref, strip_ref, carry = refs
    else:
        layers_ref, carry = refs
        main_ref = None

    @pl.when(lax.axis_index("gz") == active)
    def _():
        if pieces:
            set_carry(carry, *pieces)
            values = [carry[pl.ds(t, 8, stride=VECTORS), :] for t in range(VECTORS)]
        else:
            values = [jnp.zeros((8, 128), F32)] * VECTORS
        for layer in range(LAYERS, 0, -1):
            at = 2 * (LAYERS - layer)
            values = step_down(values, uv_ref.at[at], uv_ref.at[at + 1], layers_ref.at[layer])
        step_down(values, uv_ref.at[2 * LAYERS], uv_ref.at[2 * LAYERS + 1], layers_ref.at[0])
        if main_ref is None:
            return
        c = core()
        lane = lanes(128)
        for t in range(VECTORS):
            carry[pl.ds(t, 8, stride=VECTORS), :] = values[t]
        bottom = carry
        mine = (lane >> 6) == c
        main_ref[...] = jnp.where(mine, bottom[pl.ds(0, 128), :], pltpu.roll(bottom[pl.ds(128, 128), :], 64, 1))
        lane = lanes(64)
        slab = inner = jnp.zeros((64, 128), F32)
        for i in range(4):
            block = bottom[pl.ds(64 * i, 64), :]
            rolled = pltpu.roll(block, 32 * i, 1) if i else block
            begin = (32 * i + 128 - c * 32) & 127
            slab = jnp.where(((lane - begin) & 127) < 32, rolled, slab)
            inner = jnp.where((lane >> 5) == i, pltpu.roll(block, (32 * i - 32 * (1 + c)) & 127, 1), inner)
        outer_ref[...] = slab
        give_ref[pl.ds(0, 64), :] = inner
        strip = bottom[pl.ds(aligned((1 - seam()) * 232, 8), 24), :]
        give_ref[pl.ds(64, 24), :] = strip
        strip_ref[...] = strip

    if before_ref is not None:
        @pl.when(lax.axis_index("gz") != active)
        def _():
            layers_ref[...] = before_ref[...]


def box(values):
    two = [values[i] + values[i + 1] for i in range(len(values) - 1)]
    four = [two[i] + two[i + 2] for i in range(len(two) - 2)]
    return [four[i] + values[i + 4] for i in range(len(values) - 4)]


def smooth(layers_ref, w_ref, kept_ref, give_ref, plains, others, tent):
    c = core()
    mine = (lanes(128) >> 6) == c
    row = lax.broadcasted_iota(jnp.int32, (256, 128), 0)
    col = lax.broadcasted_iota(jnp.int32, (256, 128), 1)
    distance = (row - col + RADIUS) & 127
    weight = jnp.where(distance <= 2 * RADIUS, RADIUS + 1 - jnp.abs(distance - RADIUS), 0)
    tent[...] = weight.astype(F32).astype(jnp.bfloat16)

    def layer(k, plain):
        values = [layers_ref[k, pl.ds(8 * t, 8), :] * w_ref[k, pl.ds(8 * t, 8), :] for t in range(VECTORS)]
        first = [pltpu.roll(value, 1, 0) for value in values[VECTORS - RADIUS:]]
        last = [pltpu.roll(value, 7, 0) for value in values[:RADIUS]]
        total = jnp.concatenate(box(box(first + values + last)), axis=0)
        high = total.astype(jnp.bfloat16)
        rest = total - high.astype(F32)
        middle = rest.astype(jnp.bfloat16)
        small = (rest - middle.astype(F32)).astype(jnp.bfloat16)
        value = jnp.dot(jnp.concatenate([high, middle], axis=1), tent[...], preferred_element_type=F32)
        value = value + jnp.dot(small, tent[pl.ds(0, 128), :], preferred_element_type=F32)
        plane_to_plain(value, plain)
        kept_ref[k] = plain[pl.ds(aligned(c * 128, 128), 128), :]
        others[k] = plain[pl.ds(aligned((1 - c) * 128, 128), 128), :]

    for k in range(STEPS):
        layer(k, plains.at[k % 4])
    count = give_ref.shape[0]
    for k in range(count):
        second = others[k + count] if k + count < STEPS else jnp.zeros((128, 128), F32)
        give_ref[k] = jnp.where(mine, others[k], pltpu.roll(second, 64, 1))


def ends(kept_ref, got_ref, out_ref, top_ref, bottom_ref):
    mine = (lanes(128) >> 6) == core()
    count = got_ref.shape[0]
    for k in range(STEPS):
        other = got_ref[k] if k < count else pltpu.roll(got_ref[k - count], 64, 1)
        out_ref[k] = jnp.where(mine, kept_ref[k], other)
    top_ref[...] = out_ref[pl.ds(STEPS - RADIUS - 1, RADIUS + 1)]
    bottom_ref[...] = out_ref[pl.ds(1, RADIUS - 1)]


def finish(tile_ref, below_ref, above_ref, passive_ref, out_ref):
    gz = lax.axis_index("gz")
    has_below, has_above = one_if(gz > 0), one_if(gz < lax.axis_size("gz") - 1)

    def layer(k):
        if k < 0:
            return below_ref[k + RADIUS] * has_below
        if k == 0:
            return jnp.where(gz == 0, tile_ref[0], below_ref[RADIUS])
        if k > LAYERS:
            return above_ref[k - STEPS] * has_above
        return tile_ref[k]

    for k in range(LAYERS):
        total = layer(k) * 5.0
        for offset in range(1, RADIUS + 1):
            total = total + (layer(k - offset) + layer(k + offset)) * (5.0 - offset)
        out_ref[k] = jnp.where(passive_ref[k] > 0, 0.0, total)


def to_other(value):
    return moved(value, lambda z, y, x: (z, y ^ 1, x))


def after(value, *others):
    return lax.optimization_barrier((value,) + others)[0]


def per_device(filtered, printed, sensitivity, passive):
    sizes = tuple(lax.axis_size(axis) for axis in AXES)
    depth = sizes[0]
    plane = shape(128, 128)
    edge = shape(16, 128)

    def across(z, y, x):
        return (z, y ^ 3, x) if y in (1, 2) else None

    def beside(z, y, x):
        return (z, y ^ 1, x + (1 if y & 1 else -1))

    def same(z, y, x):
        return (z, y, x + (-1 if y & 1 else 1))

    hbm, vmem = pl.BlockSpec(memory_space=pltpu.HBM), pl.BlockSpec(memory_space=pltpu.VMEM)
    lowest_planes, inner, outer, left, right = call(
        edges, [shape(3, 128, 128)] + [edge] * 4, printed, filtered, sensitivity,
        in_specs=[vmem, hbm, hbm],
        scratch=[pltpu.VMEM((128, 128), F32), pltpu.SemaphoreType.DMA((2,))],
    )
    above = moved(lowest_planes, lambda z, y, x: (z - 1, y, x))
    from_left = moved(right, lambda z, y, x: (z, y, x + 1))
    from_right = moved(left, lambda z, y, x: (z, y, x - 1))
    outer = moved(outer, lambda z, y, x: (z, y ^ 3, x))
    inner = to_other(inner)
    uvw = call(
        functools.partial(all_terms, sizes), shape(3 * STEPS, 128, 128),
        printed, filtered, sensitivity, above, inner, outer, from_left, from_right,
        in_specs=[vmem, hbm, hbm] + [vmem] * 5,
        scratch=[
            pltpu.VMEM((144, 128), F32), pltpu.VMEM((128, 128), F32),
            pltpu.VMEM((LAYERS, 128, 128), F32), pltpu.VMEM((LAYERS, 128, 128), F32),
            pltpu.SemaphoreType.DMA((2, LAYERS // 4)),
        ],
    )
    slab, corner = shape(SLAB_ROWS, 128), shape(CORNER_ROWS, 128)
    rows = call(pack_rows, shape(ROW_TOTAL, 128), uvw)
    got = moved(rows, across)
    to_same, to_cross, keep, give = call(pack, [slab, slab, corner, corner], after(uvw, rows))
    from_same = moved(to_same, same)
    from_cross = moved(to_cross, beside)
    corner = call(pick_corner, corner, keep, to_other(give))
    corner = moved(corner, lambda z, y, x: (z, 3 - y, x + (1 if y & 1 else -1)))
    other = to_other(uvw)
    shared = to_other(after(got, from_same, from_cross, corner))
    parts = (uvw, other, got, shared, from_same, from_cross, corner)
    stack = shape(STEPS, PLANE, 128)
    work = [pltpu.VMEM((2, PLANE, 128), F32), pltpu.VMEM((4, PLANE, 128), F32)]
    uvs = call(assemble, shape(2 * STEPS, PLANE, 128), *parts, scratch=work)
    ws = None
    pieces, before = (), ()
    for active in range(depth - 1, -1, -1):
        outs = [stack]
        if active > 0:
            outs = outs + [plane, shape(64, 128), shape(88, 128), shape(24, 128)]
        layers, *sent = call(
            functools.partial(section, active), outs, uvs, *pieces, *before, scratch=[pltpu.VMEM((PLANE, 128), F32)]
        )
        before = (layers,)
        if active > 0:
            main, side, give, strip = sent

            def down(where):
                def to(z, y, x):
                    _, ty, tx = where(z, y, x)
                    return (z - 1, ty, tx) if z == active else None
                return to

            def over(z, y, x):
                return (z, y ^ 2, x)

            def corner_of(z, y, x):
                _, ty, tx = beside(z, y, x)
                return (z, ty ^ 2, tx)

            side = moved(side, down(beside))
            edge_piece = moved(strip, down(corner_of))
            main, halo = call(merge, [shape(192, 128), shape(24, 128)], main, give, to_other(give))
            main = moved(main, down(lambda z, y, x: (z, y, x)))
            halo = moved(halo, down(over))
            pieces = (main, side, halo, edge_piece)
            if ws is None:
                ws = call(assemble_w, stack, after(uvw, side), *parts[1:], scratch=work)
    count = STEPS // 2 + 1
    kept, given = call(
        smooth,
        [shape(STEPS, 128, 128), shape(count, 128, 128)],
        layers, ws,
        scratch=[
            pltpu.VMEM((4, PLANE, 128), F32), pltpu.VMEM((STEPS, 128, 128), F32), pltpu.VMEM((256, 128), jnp.bfloat16)
        ],
    )
    given = to_other(given)
    tile, top, bottom = call(
        ends, [shape(STEPS, 128, 128), shape(RADIUS + 1, 128, 128), shape(RADIUS - 1, 128, 128)], kept, given
    )
    below = moved(top, lambda z, y, x: (z + 1, y, x))
    over = moved(bottom, lambda z, y, x: (z - 1, y, x))
    return call(finish, shape(LAYERS, 128, 128), tile, below, over, passive)


def solution(mesh):
    spec = P(*AXES)
    return jax.shard_map(
        per_device, mesh=mesh, in_specs=(spec,) * 4, out_specs=spec, check_vma=False
    )
```

```python
import functools
import math

import jax
import jax.numpy as jnp
from jax import lax
from jax.experimental import pallas as pl
from jax.experimental.pallas import tpu as pltpu
from jax.sharding import PartitionSpec as P

RADIUS = 4
PENALTY = 40.0
EXPONENT = PENALTY + math.log(5.0) / math.log(0.5)
SMOOTH = 0.001
AXES = ("gz", "gy", "gx")
F32 = jnp.float32

LAYERS = 16
STEPS = LAYERS + 1
PLANE = 288
VECTORS = PLANE // 8
REACH = RADIUS + STEPS
LOW = LAYERS - RADIUS
SLABS = ((16, 15, 14, 3), (13, 12, 11, 8, 0), (10, 9, 7, 6, 5, 2), (4, 1))
FOLDED = 32
SLAB_ROWS = 3 * 128 + FOLDED + 64
CORNER_ROWS = 3 * 24 + 16 + 8


def width_of(layer):
    return RADIUS + layer


def rows_of(layer):
    return -(-width_of(layer) // 8) * 8


MICROSECONDS = {"all_terms": 2.5, "assemble": 2.5, "section": 1.5, "section_rest": 3.0, "smooth_rest": 3.0, "finish": 3.0}
VMEM_LIMIT = {"edges": (64 << 20) - (64 << 10)}


def strips():
    out = []
    for slab, layers in enumerate(SLABS):
        at = 0
        for layer in layers:
            for name in ("u", "v"):
                out.append((name, layer, slab, at))
                at += width_of(layer)
        assert at <= (128 if slab < 3 else FOLDED)
    return out


def row_places():
    places, at = {}, 0
    for layer in range(STEPS):
        for name in ("u", "v", "w"):
            if (name, layer) == ("w", 0):
                continue
            rows = 8 if name == "w" else rows_of(layer)
            places[name, layer] = (at, rows)
            at += rows
    return places, at


ROW_PLACES, ROW_TOTAL = row_places()


def moved(value, where):
    sizes = tuple(lax.axis_size(axis) for axis in AXES)
    pairs = []
    for z in range(sizes[0]):
        for y in range(sizes[1]):
            for x in range(sizes[2]):
                to = where(z, y, x)
                if to is not None:
                    tz, ty, tx = to[0] % sizes[0], to[1], to[2] % sizes[2]
                    pairs.append(((z * sizes[1] + y) * sizes[2] + x, (tz * sizes[1] + ty) * sizes[2] + tx))
    return lax.ppermute(value, AXES, pairs)


def shape(*dims):
    return jax.ShapeDtypeStruct(dims, F32)


def call(kernel, outs, *args, scratch=(), in_specs=None, **more):
    name = kernel.func.__name__ if isinstance(kernel, functools.partial) else kernel.__name__
    if in_specs is not None:
        more["in_specs"] = in_specs
    return pl.pallas_call(
        kernel,
        out_shape=outs,
        scratch_shapes=list(scratch),
        compiler_params=pltpu.CompilerParams(vmem_limit_bytes=VMEM_LIMIT.get(name, 40 << 20)),
        cost_estimate=pl.CostEstimate(flops=0, bytes_accessed=int(MICROSECONDS.get(name, 0.5) * 3e6), transcendentals=0),
        name=name,
        **more,
    )(*args)


def lanes(rows):
    return lax.broadcasted_iota(jnp.int32, (rows, 128), 1)


def core():
    return lax.axis_index("gy") & 1


def seam():
    return lax.axis_index("gy") >> 1


def one_if(condition):
    return jnp.where(condition, 1.0, 0.0)


def outside():
    x, c = lax.axis_index("gx"), core()
    return ((c == 0) & (x == 0)) | ((c == 1) & (x == lax.axis_size("gx") - 1))


def plain_to_plane(ref):
    return jnp.concatenate([ref[pl.ds(t, 8, stride=VECTORS), :] for t in range(VECTORS)], axis=0)


def plane_to_plain(value, ref):
    for t in range(VECTORS):
        ref[pl.ds(t, 8, stride=VECTORS), :] = value[8 * t:8 * t + 8]


def aligned(value, to):
    return pl.multiple_of(value, to)


def power40(p):
    x = p + p
    x2 = x * x
    x4 = x2 * x2
    x8 = x4 * x4
    x32 = x8 * x8
    x32 = x32 * x32
    return x32 * x8


def power39(p):
    x = p + p
    x2 = x * x
    x4 = x2 * x2
    x8 = x4 * x4
    x32 = x8 * x8
    x32 = x32 * x32
    return x32 * (x4 * (x2 * x))


def edges(p_hbm, f_hbm, s_hbm, lowest_ref, inner_ref, outer_ref, left_ref, right_ref, turned, p_ref, sems):
    planes = [pltpu.make_async_copy(p_hbm.at[pl.ds(4 * i, 4)], p_ref.at[pl.ds(4 * i, 4)], sems.at[i]) for i in range(4)]
    copies = [pltpu.make_async_copy(ref.at[0], lowest_ref.at[i + 1], sems.at[4 + i]) for i, ref in enumerate((f_hbm, s_hbm))]
    for copy in planes + copies:
        copy.start()
    lane = lanes(128)
    c = core()
    packed = jnp.zeros((128, 128), F32)
    for layer in range(LAYERS):
        if layer % 4 == 0:
            planes[layer // 4].wait()
        inner_ref[pl.ds(layer, 1), :] = p_ref[layer, pl.ds(127 * (1 - c), 1), :]
        outer_ref[pl.ds(layer, 1), :] = p_ref[layer, pl.ds(127 * c, 1), :]
        rolled = pltpu.roll(p_ref[layer], 2 * layer + 1, 1)
        packed = jnp.where((lane >> 1) == layer, rolled, packed)
    turned[...] = packed.T
    right_ref[...] = turned[pl.ds(0, 16, stride=2), :]
    left_ref[...] = turned[pl.ds(1, 16, stride=2), :]
    lowest_ref[0] = p_ref[0]
    for copy in copies:
        copy.wait()


def early(p_ref, f_ref, s_ref, out_ref):
    out_ref[...] = p_ref[0, pl.ds(0, 8), :] + f_ref[0, pl.ds(0, 8), :] + s_ref[0, pl.ds(0, 8), :]


def norm_of(position, extent):
    def missing(k):
        k = jnp.maximum(k, 0)
        return (k * (k + 1)) >> 1

    return ((RADIUS + 1) ** 2 - missing(RADIUS - position) - missing(RADIUS - (extent - 1 - position))).astype(F32)


def terms(total, density, sens, p39):
    total = jnp.maximum(total, 1e-30)
    offset = PENALTY * math.log(2.0) / EXPONENT
    smax = jnp.exp(jnp.log(total) * (1.0 / EXPONENT) - offset)
    gap = density - smax
    half = 0.5 * gap * lax.rsqrt(gap * gap + SMOOTH)
    low = 0.5 - half
    top = (0.5 + half) * (2.0 * PENALTY / EXPONENT) * smax
    h = top / total
    return h * sens, h * p39, low, total / top


def plane_norms(sizes):
    row0 = lax.axis_index("gy") * 128
    col0 = lax.axis_index("gx") * 128
    rows = lax.broadcasted_iota(jnp.int32, (128, 128), 0) + row0
    cols = lax.broadcasted_iota(jnp.int32, (128, 128), 1) + col0
    return norm_of(rows, sizes[1] * 128) * norm_of(cols, sizes[2] * 128)


def neighbours(p, layer, inner_ref, outer_ref, beside, powers):
    c = core()
    lane = lanes(128)
    own = power40(p)
    powers[pl.ds(8, 128), :] = own
    y = lax.axis_index("gy")
    there = one_if((y == 1) | (y == 2))
    powers[pl.ds(7 + 129 * (1 - c), 1), :] = power40(inner_ref[pl.ds(layer, 1), :])
    powers[pl.ds(7 + 129 * c, 1), :] = power40(outer_ref[pl.ds(layer, 1), :]) * there
    side = pltpu.roll(beside, (128 - (2 * layer + 1)) % 128, 1)
    right = jnp.where(lane == 127, side, pltpu.roll(own, 127, 1))
    left = jnp.where(lane == 0, side, pltpu.roll(own, 1, 1))
    return (own + right) + left + (powers[pl.ds(7, 128), :] + powers[pl.ds(9, 128), :])


def columns_beside(left_ref, right_ref, turned):
    x = lax.axis_index("gx")
    turned[...] = jnp.zeros((128, 128), F32)
    turned[pl.ds(0, 16, stride=2), :] = right_ref[...] * one_if(x < lax.axis_size("gx") - 1)
    turned[pl.ds(1, 16, stride=2), :] = left_ref[...] * one_if(x > 0)
    return power40(turned[...].T)


def all_terms(
    sizes, p_ref, f_ref, s_ref, above_ref, inner_ref, outer_ref, left_ref, right_ref, early_ref, uvw_ref, powers, turned
):
    beside = columns_beside(left_ref, right_ref, turned)
    norms = 1.0 / plane_norms(sizes)
    gz = lax.axis_index("gz")
    layer0 = gz * LAYERS
    uvw_ref[0] = s_ref[0]
    uvw_ref[STEPS] = power39(p_ref[0])
    uvw_ref[2 * STEPS] = norms * (1.0 / norm_of(0 * layer0, sizes[0] * LAYERS))
    for layer in range(1, STEPS):
        total = neighbours(p_ref[layer - 1], layer - 1, inner_ref, outer_ref, beside, powers)
        if layer < LAYERS:
            p, f, s = p_ref[layer], f_ref[layer], s_ref[layer]
        else:
            p, f, s = above_ref[0], above_ref[1], above_ref[2]
        u, v, low, inverse = terms(total, f, s, power39(p))
        if layer == LAYERS:
            there = one_if(gz < sizes[0] - 1)
            u, v = u * there, v * there
        norm_z = norm_of(layer0 + layer, sizes[0] * LAYERS)
        uvw_ref[layer] = u
        uvw_ref[STEPS + layer] = v
        uvw_ref[2 * STEPS + layer] = low * inverse * (norms * (1.0 / norm_z))


def plane_of(uvw_ref, name, layer):
    return uvw_ref.at[STEPS * "uvw".index(name) + layer]


def pack_rows(uvw_ref, rows_ref):
    c = core()
    for (name, layer), (at, rows) in ROW_PLACES.items():
        start = aligned(c * (128 - rows), 8)
        rows_ref[pl.ds(at, rows), :] = plane_of(uvw_ref, name, layer)[pl.ds(start, rows), :]


def pack(uvw_ref, same_ref, cross_ref, keep_ref, give_ref):
    c = core()

    def put(at, left, right):
        count = left.shape[0]
        same_ref[pl.ds(at, count), :] = jnp.where(c == 0, right, left)
        cross_ref[pl.ds(at, count), :] = jnp.where(c == 0, left, right)

    def put_corner(at, rows, left, right):
        first, last = slice(0, rows), slice(left.shape[0] - rows, left.shape[0])
        keep_ref[pl.ds(at, rows), :] = jnp.where(c == 0, left[first], right[last])
        give_ref[pl.ds(at, rows), :] = jnp.where(c == 0, right[first], left[last])

    lane = lanes(128)
    for slab in range(4):
        left = right = jnp.zeros((128, 128), F32)
        for name, layer, where, at in strips():
            if where == slab:
                width = width_of(layer)
                plane = plane_of(uvw_ref, name, layer)[...]
                inside = (lane >= at) & (lane < at + width)
                left = jnp.where(inside, pltpu.roll(plane, at, 1) if at else plane, left)
                right = jnp.where(inside, pltpu.roll(plane, (at + width) % 128, 1), right)
        if slab < 3:
            put(128 * slab, left, right)
            put_corner(24 * slab, 24, left, right)
            continue
        put_corner(72, 16, left, right)
        folded = []
        for value in (left, right):
            total = value[:FOLDED]
            for i in range(1, 4):
                total = total + pltpu.roll(value[FOLDED * i:FOLDED * (i + 1)], FOLDED * i, 1)
            folded.append(total)
        put(384, *folded)
    lane = lanes(64)
    left = right = jnp.zeros((64, 128), F32)
    for layer in range(1, STEPS):
        ref = plane_of(uvw_ref, "w", layer)
        for half in range(2):
            plane = ref[pl.ds(64 * half, 64), :]
            at = 64 * half + RADIUS * (layer - 1)
            inside = (lane >= at) & (lane < at + RADIUS)
            left = jnp.where(inside, pltpu.roll(plane, at, 1) if at else plane, left)
            right = jnp.where(inside, pltpu.roll(plane, (at + RADIUS) % 128, 1), right)
    put(384 + FOLDED, left, right)
    put_corner(88, 8, left, right)


def pick_corner(keep_ref, got_ref, corner_ref):
    corner_ref[...] = jnp.where((core() ^ seam()) == 1, keep_ref[...], got_ref[...])


def slab_plane(plain, same, cross, corner):
    c = core()
    inside = one_if(jnp.logical_not(outside()))
    plain[pl.ds(256, 32), :] = jnp.zeros((32, 128), F32)
    plain[pl.ds(aligned(c * 128, 128), 128), :] = same * inside
    plain[pl.ds(aligned((1 - c) * 128, 128), 128), :] = cross * inside
    rows = corner.shape[0]
    plain[pl.ds(aligned(256 + seam() * (32 - rows), 8), rows), :] = corner * inside


def full_plane(plain, name, layer, uvw_ref, other_ref, got_ref, shared_ref):
    c = core()
    plain[pl.ds(aligned(c * 128, 128), 128), :] = plane_of(uvw_ref, name, layer)[...]
    plain[pl.ds(aligned((1 - c) * 128, 128), 128), :] = plane_of(other_ref, name, layer)[...]
    plain[pl.ds(256, 32), :] = jnp.zeros((32, 128), F32)
    start, rows = ROW_PLACES[name, layer]
    here = pl.ds(start, rows)
    to = aligned(256 + seam() * (32 - rows), 8)
    plain[pl.ds(to, rows), :] = jnp.where((c ^ seam()) == 1, got_ref[here, :], shared_ref[here, :])
    return plain_to_plane(plain)


def with_columns(base, columns, at, width):
    c = core()
    lane = lanes(PLANE)
    columns = pltpu.roll(columns, (128 - at - (1 - c) * width) & 127, 1)
    begin = (1 - c) * (128 - width)
    return jnp.where((lane >= begin) & (lane < begin + width), columns, base)


def assemble(
    uvw_ref, other_ref, got_ref, shared_ref, same_ref, cross_ref, corner_ref, uv_ref, plain, slabs
):
    c = core()
    for slab in range(4):
        if slab < 3:
            here = pl.ds(128 * slab, 128)
            same, cross = same_ref[here, :], cross_ref[here, :]
            here = pl.ds(24 * slab, 24)
        else:
            here = pl.ds(384, FOLDED)
            same, cross = (
                jnp.concatenate([value] + [pltpu.roll(value, 128 - FOLDED * i, 1) for i in range(1, 4)], axis=0)
                for value in (same_ref[here, :], cross_ref[here, :])
            )
            here = pl.ds(72, 16)
        corner = corner_ref[here, :]
        slot = plain.at[slab % 2]
        slab_plane(slot, same, cross, corner)
        slabs[slab] = plain_to_plane(slot)
    for place, (name, layer, slab, at) in enumerate(strips()):
        base = full_plane(plain.at[place % 2], name, layer, uvw_ref, other_ref, got_ref, shared_ref)
        uv_ref[2 * (LAYERS - layer) + (name == "v")] = with_columns(base, slabs[slab], at, width_of(layer))


def assemble_w(
    uvw_ref, other_ref, got_ref, shared_ref, same_ref, cross_ref, corner_ref, w_ref, plain, slabs
):
    c = core()

    def unfolded(ref):
        value = ref[pl.ds(384 + FOLDED, 64), :]
        return jnp.concatenate([value, pltpu.roll(value, 64, 1)], axis=0)

    here = pl.ds(88, 8)
    corner = corner_ref[here, :]
    corner = pltpu.roll(corner, 64 * seam(), 1)
    slab_plane(plain.at[0], unfolded(same_ref), unfolded(cross_ref), corner)
    slabs[0] = plain_to_plane(plain.at[0])
    for layer in range(1, STEPS):
        base = full_plane(plain.at[layer % 2], "w", layer, uvw_ref, other_ref, got_ref, shared_ref)
        w_ref[layer] = with_columns(base, slabs[0], RADIUS * (layer - 1), RADIUS)
    row = lax.broadcasted_iota(jnp.int32, (PLANE, 128), 0)
    col = lax.broadcasted_iota(jnp.int32, (PLANE, 128), 1)
    a = seam()
    row = jnp.where((a == 1) & (row >= 256), row - PLANE, row) + 256 * a
    width = jnp.where(c == 0, 108, 20)
    col = jnp.where((c == 0) & (col >= width), col - 128, jnp.where((c == 1) & (col < width), col + 128, col))
    col = col + 128 * lax.axis_index("gx")
    rows, cols = 128 * lax.axis_size("gy"), 128 * lax.axis_size("gx")
    norm = norm_of(row, rows) * norm_of(col, cols) * norm_of(0 * a, LAYERS * lax.axis_size("gz"))
    inside = (row >= 0) & (row < rows) & (col >= 0) & (col < cols)
    plain[0] = jnp.where(inside, 1.0 / jnp.where(inside, norm, 1.0), 0.0)
    w_ref[0] = plain_to_plane(plain.at[0])


def step_down(values, u_ref, v_ref, out_ref):
    new = []
    for t, value in enumerate(values):
        before = values[t - 1] if t > 0 else pltpu.roll(values[-1], 1, 0)
        behind = values[t + 1] if t < VECTORS - 1 else pltpu.roll(values[0], 7, 0)
        total = (value + before) + (behind + pltpu.roll(value, 1, 1)) + pltpu.roll(value, 127, 1)
        here = pl.ds(8 * t, 8)
        new.append(u_ref[here, :] + v_ref[here, :] * total)
        out_ref[here, :] = new[-1]
    return new


def set_carry(carry, main_ref, outer_ref, halo_ref, halo_outer_ref):
    c = core()
    lane = lanes(64)
    mine = (lane >> 6) == c
    inside = one_if(jnp.logical_not(outside()))
    begin = (1 - c) * (128 - REACH)
    beyond = (lane >= begin) & (lane < begin + REACH)
    for i in range(4):
        if main_ref.shape[0] == 256:
            value = main_ref[pl.ds(64 * i, 64), :]
        else:
            value = main_ref[pl.ds(64 * (i % 2), 64), :]
            if i >= 2:
                value = pltpu.roll(value, 64, 1)
            inner = pltpu.roll(main_ref[pl.ds(128, 64), :], (32 * (2 - c) - 32 * i) & 127, 1)
            value = jnp.where(mine, value, inner)
        outer = pltpu.roll(outer_ref[...], (128 - 32 * i) % 128, 1) if i else outer_ref[...]
        carry[pl.ds(64 * i, 64), :] = jnp.where(beyond, outer * inside, value)
    lane = lanes(24)
    beyond = (lane >= begin) & (lane < begin + REACH)
    carry[pl.ds(256, 32), :] = jnp.zeros((32, 128), F32)
    carry[pl.ds(aligned(256 + 8 * seam(), 8), 24), :] = jnp.where(beyond, halo_outer_ref[...] * inside, halo_ref[...])


def merge(give_ref, got_ref, down_ref, halo_ref):
    mine = (lanes(128) >> 6) == core()
    rows = pl.ds(0, 128)
    own, other = give_ref[rows, :], got_ref[rows, :]
    down_ref[rows, :] = jnp.where(mine, own, other)
    down_ref[pl.ds(128, 128), :] = pltpu.roll(jnp.where(mine, other, own), 64, 1)
    rows = pl.ds(128, 24)
    halo_ref[...] = jnp.where(mine[:24], give_ref[rows, :], got_ref[rows, :])


def load_carry(pieces, carry):
    set_carry(carry, *pieces)
    return [carry[pl.ds(t, 8, stride=VECTORS), :] for t in range(VECTORS)]


def run_down(values, uv_ref, layers_ref, first, last, base=0):
    for layer in range(first, last - 1, -1):
        at = 2 * (LAYERS - layer)
        values = step_down(values, uv_ref.at[at], uv_ref.at[at + 1], layers_ref.at[layer - base])
    return values


def section(active, shared, *refs):
    uv_ref, refs = refs[0], refs[1:]
    pieces, before_ref = (), None
    if len(refs) > 5:
        pieces, before_ref, refs = refs[:4], refs[4], refs[5:]
    layers_ref, down_ref, outer_ref, strip_ref, carry = refs

    @pl.when(lax.axis_index("gz") == active)
    def _():
        values = load_carry(pieces, carry) if pieces else [jnp.zeros((8, 128), F32)] * VECTORS
        values = run_down(values, uv_ref, layers_ref, LAYERS, 1)
        layers_ref[0] = layers_ref[1]
        for t in range(VECTORS):
            carry[pl.ds(t, 8, stride=VECTORS), :] = values[t]
        c = core()
        mine = (lanes(128) >> 6) == c
        down_ref[pl.ds(0, 128), :] = jnp.where(
            mine, carry[pl.ds(0, 128), :], pltpu.roll(carry[pl.ds(128, 128), :], 64, 1)
        )
        lane = lanes(64)
        slab = inner = jnp.zeros((64, 128), F32)
        for i in range(4):
            block = carry[pl.ds(64 * i, 64), :]
            rolled = pltpu.roll(block, 32 * i, 1) if i else block
            begin = (32 * i + 128 - c * 32) & 127
            slab = jnp.where(((lane - begin) & 127) < 32, rolled, slab)
            if not shared:
                inner = jnp.where((lane >> 5) == i, pltpu.roll(block, (32 * i - 32 * (2 - c)) & 127, 1), inner)
        outer_ref[...] = slab
        strip = carry[pl.ds(aligned((1 - seam()) * 232, 8), 24), :]
        strip_ref[...] = strip
        if shared:
            down_ref[pl.ds(128, 24), :] = strip
        else:
            down_ref[pl.ds(128, 64), :] = inner

    if before_ref is not None:
        @pl.when(lax.axis_index("gz") != active)
        def _():
            layers_ref[...] = before_ref[...]


def section_top(uv_ref, main_ref, outer_ref, halo_ref, halo_outer_ref, before_ref, top_ref, carry):
    @pl.when(lax.axis_index("gz") == 0)
    def _():
        values = load_carry((main_ref, outer_ref, halo_ref, halo_outer_ref), carry)
        run_down(values, uv_ref, top_ref, LAYERS, LOW, LOW)

    @pl.when(lax.axis_index("gz") != 0)
    def _():
        top_ref[...] = before_ref[pl.ds(LOW, STEPS - LOW)]


def section_rest(uv_ref, top_ref, before_ref, layers_ref):
    @pl.when(lax.axis_index("gz") == 0)
    def _():
        values = [top_ref[0, pl.ds(8 * t, 8), :] for t in range(VECTORS)]
        run_down(values, uv_ref, layers_ref, LOW - 1, 0)

    @pl.when(lax.axis_index("gz") != 0)
    def _():
        layers_ref[...] = before_ref[pl.ds(0, LOW)]


def box(values):
    two = [values[i] + values[i + 1] for i in range(len(values) - 1)]
    four = [two[i] + two[i + 2] for i in range(len(two) - 2)]
    return [four[i] + values[i + 4] for i in range(len(values) - 4)]


def smooth(layers, kept_ref, plains, others, tent):
    c = core()
    row = lax.broadcasted_iota(jnp.int32, (256, 128), 0)
    col = lax.broadcasted_iota(jnp.int32, (256, 128), 1)
    distance = (row - col + RADIUS) & 127
    weight = jnp.where(distance <= 2 * RADIUS, RADIUS + 1 - jnp.abs(distance - RADIUS), 0)
    tent[...] = weight.astype(F32).astype(jnp.bfloat16)
    for k, (layer_ref, w_ref) in enumerate(layers):
        plain = plains.at[k % 4]
        values = [layer_ref[pl.ds(8 * t, 8), :] * w_ref[pl.ds(8 * t, 8), :] for t in range(VECTORS)]
        first = [pltpu.roll(value, 1, 0) for value in values[VECTORS - RADIUS:]]
        last = [pltpu.roll(value, 7, 0) for value in values[:RADIUS]]
        total = jnp.concatenate(box(box(first + values + last)), axis=0)
        high = total.astype(jnp.bfloat16)
        rest = total - high.astype(F32)
        middle = rest.astype(jnp.bfloat16)
        small = (rest - middle.astype(F32)).astype(jnp.bfloat16)
        value = jnp.dot(jnp.concatenate([high, middle], axis=1), tent[...], preferred_element_type=F32)
        value = value + jnp.dot(small, tent[pl.ds(0, 128), :], preferred_element_type=F32)
        plane_to_plain(value, plain)
        kept_ref[k] = plain[pl.ds(aligned(c * 128, 128), 128), :]
        others[k] = plain[pl.ds(aligned((1 - c) * 128, 128), 128), :]


def pair_up(others, first, count, give_ref):
    mine = (lanes(128) >> 6) == core()
    for k in range(count):
        give_ref[k] = jnp.where(mine, others[first + k], pltpu.roll(others[first + count + k], 64, 1))


def smooth_first(top_ref, before_ref, w_ref, kept_ref, give_ref, plains, others, tent):
    layers = [(top_ref.at[k], w_ref.at[LOW + k]) for k in range(STEPS - LOW)]
    layers += [(before_ref.at[k], w_ref.at[k]) for k in range(1, RADIUS)]
    smooth(layers, kept_ref, plains, others, tent)
    pair_up(others, 0, 4, give_ref)


def smooth_rest(layers_ref, w_ref, kept_ref, give_ref, give_more_ref, plains, others, tent):
    smooth([(layers_ref.at[k], w_ref.at[k]) for k in range(LOW)], kept_ref, plains, others, tent)
    pair_up(others, 0, 3, give_ref)
    pair_up(others, 6, 3, give_more_ref)


def whole(kept, got, second):
    mine = (lanes(128) >> 6) == core()
    return jnp.where(mine, kept, pltpu.roll(got, 64, 1) if second else got)


def ends(kept_ref, got_ref, top_ref, bottom_ref):
    for k in range(8):
        value = whole(kept_ref[k], got_ref[k % 4], k >= 4)
        if k < STEPS - LOW:
            top_ref[k] = value
        else:
            bottom_ref[k - (STEPS - LOW)] = value


def finish(kept_ref, got_ref, got_more_ref, top_ref, below_ref, above_ref, passive_ref, out_ref, tile):
    gz = lax.axis_index("gz")
    for k in range(LOW):
        got = got_ref if k < 6 else got_more_ref
        tile[k] = whole(kept_ref[k], got[k % 3], k % 6 >= 3)

    def layer(k):
        if k < 0:
            return jnp.where(gz > 0, below_ref[k + RADIUS], 0.0)
        if k == 0:
            return jnp.where(gz == 0, tile[0], below_ref[RADIUS])
        if k > LAYERS:
            return jnp.where(gz < lax.axis_size("gz") - 1, above_ref[k - STEPS], 0.0)
        return tile[k] if k < LOW else top_ref[k - LOW]

    for k in range(LAYERS):
        total = layer(k) * 5.0
        for offset in range(1, RADIUS + 1):
            total = total + (layer(k - offset) + layer(k + offset)) * (5.0 - offset)
        out_ref[k] = jnp.where(passive_ref[k] > 0, 0.0, total)


def to_other(value):
    return moved(value, lambda z, y, x: (z, y ^ 1, x))


def after(value, *others):
    return lax.optimization_barrier((value,) + others)[0]


def per_device(filtered, printed, sensitivity, passive):
    sizes = tuple(lax.axis_size(axis) for axis in AXES)
    depth = sizes[0]
    plane = shape(128, 128)
    edge = shape(16, 128)

    def across(z, y, x):
        return (z, y ^ 3, x) if y in (1, 2) else None

    def beside(z, y, x):
        return (z, y ^ 1, x + (1 if y & 1 else -1))

    def same(z, y, x):
        return (z, y, x + (-1 if y & 1 else 1))

    hbm = pl.BlockSpec(memory_space=pltpu.HBM)
    lowest_planes, inner, outer, left, right = call(
        edges, [shape(3, 128, 128)] + [edge] * 4, printed, filtered, sensitivity,
        in_specs=[hbm] * 3,
        scratch=[pltpu.VMEM((128, 128), F32), pltpu.VMEM((LAYERS, 128, 128), F32), pltpu.SemaphoreType.DMA((6,))],
    )
    above = moved(lowest_planes, lambda z, y, x: (z - 1, y, x))
    from_left = moved(right, lambda z, y, x: (z, y, x + 1))
    from_right = moved(left, lambda z, y, x: (z, y, x - 1))
    outer = moved(outer, lambda z, y, x: (z, y ^ 3, x))
    inner = to_other(inner)
    ready = call(early, shape(8, 128), printed, filtered, after(sensitivity, left))
    uvw = call(
        functools.partial(all_terms, sizes), shape(3 * STEPS, 128, 128),
        printed, filtered, sensitivity, above, inner, outer, from_left, from_right, ready,
        scratch=[
            pltpu.VMEM((144, 128), F32), pltpu.VMEM((128, 128), F32),
        ],
    )
    slab, corner = shape(SLAB_ROWS, 128), shape(CORNER_ROWS, 128)
    rows = call(pack_rows, shape(ROW_TOTAL, 128), uvw)
    got = moved(rows, across)
    to_same, to_cross, keep, give = call(pack, [slab, slab, corner, corner], after(uvw, rows))
    from_same = moved(to_same, same)
    from_cross = moved(to_cross, beside)
    corner = call(pick_corner, corner, keep, to_other(give))
    corner = moved(corner, lambda z, y, x: (z, 3 - y, x + (1 if y & 1 else -1)))
    other = to_other(uvw)
    shared = to_other(after(got, from_same, from_cross, corner))
    parts = (uvw, other, got, shared, from_same, from_cross, corner)
    stack = shape(STEPS, PLANE, 128)
    work = [pltpu.VMEM((2, PLANE, 128), F32), pltpu.VMEM((4, PLANE, 128), F32)]
    uvs = call(assemble, shape(2 * STEPS, PLANE, 128), *parts, scratch=work)
    ws = None
    pieces, before = (), ()
    whole_stack = [pltpu.VMEM((PLANE, 128), F32)]
    for active in range(depth - 1, 0, -1):
        swap = (depth - 1 - active) % 2 == 1
        layers, main, side, strip = call(
            functools.partial(section, active, swap),
            [stack, shape(152 if swap else 192, 128), shape(64, 128), shape(24, 128)],
            uvs, *pieces, *before, scratch=whole_stack,
        )
        before = (layers,)

        def down(where):
            def to(z, y, x):
                _, ty, tx = where(z, y, x)
                return (z - 1, ty, tx) if z == active else None
            return to

        def over(z, y, x):
            return (z, y ^ 2, x)

        def corner_of(z, y, x):
            _, ty, tx = beside(z, y, x)
            return (z, ty ^ 2, tx)

        side = moved(side, down(beside))
        edge_piece = moved(strip, down(corner_of))
        halo = strip
        if swap:
            main, halo = call(merge, [shape(256, 128), shape(24, 128)], main, to_other(main))
        main = moved(main, down(lambda z, y, x: (z, y, x)))
        halo = moved(halo, down(over))
        pieces = (main, side, halo, edge_piece)
        if ws is None:
            ws = call(assemble_w, stack, after(uvw, side), *parts[1:], scratch=work)
    top_layers = call(
        section_top, shape(STEPS - LOW, PLANE, 128), uvs, *pieces, layers, scratch=whole_stack
    )

    def work_for(count):
        return [
            pltpu.VMEM((4, PLANE, 128), F32), pltpu.VMEM((count, 128, 128), F32), pltpu.VMEM((256, 128), jnp.bfloat16)
        ]

    kept, given = call(
        smooth_first, [shape(8, 128, 128), shape(4, 128, 128)], top_layers, layers, ws, scratch=work_for(8)
    )
    top, bottom = call(ends, [shape(RADIUS + 1, 128, 128), shape(RADIUS - 1, 128, 128)], kept, to_other(given))
    below = moved(top, lambda z, y, x: (z + 1, y, x))
    over = moved(bottom, lambda z, y, x: (z - 1, y, x))
    rest = call(section_rest, shape(LOW, PLANE, 128), uvs, after(top_layers, top), layers)
    third = shape(3, 128, 128)
    kept, given, given_more = call(
        smooth_rest, [shape(LOW, 128, 128), third, third], rest, ws, scratch=work_for(LOW)
    )
    return call(
        finish, shape(LAYERS, 128, 128),
        kept, to_other(given), to_other(given_more), top, below, over, passive,
        scratch=[pltpu.VMEM((LOW, 128, 128), F32)],
    )


def solution(mesh):
    spec = P(*AXES)
    return jax.shard_map(
        per_device, mesh=mesh, in_specs=(spec,) * 4, out_specs=spec, check_vma=False
    )
```

```python
import functools
import math

import jax
import jax.numpy as jnp
from jax import lax
from jax.experimental import pallas as pl
from jax.experimental.pallas import tpu as pltpu
from jax.sharding import PartitionSpec as P

RADIUS = 4
PENALTY = 40.0
EXPONENT = PENALTY + math.log(5.0) / math.log(0.5)
SMOOTH = 0.001
AXES = ("gz", "gy", "gx")
F32 = jnp.float32

LAYERS = 16
STEPS = LAYERS + 1
PLANE = 288
VECTORS = PLANE // 8
REACH = RADIUS + STEPS
LOW = LAYERS - RADIUS
SLABS = ((16, 15, 14, 3), (13, 12, 11, 8, 0), (10, 9, 7, 6, 5, 2), (4, 1))
FOLDED = 32
SLAB_ROWS = 3 * 128 + FOLDED + 64
CORNERS = ((0, 24), (24, 24), (48, 16), (64, 8), (72, 8))
CORNER_ROWS = 80


def width_of(layer):
    return RADIUS + layer


def rows_of(layer):
    return -(-width_of(layer) // 8) * 8


MICROSECONDS = {"all_terms": 2.5, "assemble": 2.5, "section": 1.5, "section_rest": 3.0, "smooth_rest": 3.0, "finish": 3.0}
VMEM_LIMIT = {"edges": 52 << 20}


def strips():
    out = []
    for slab, layers in enumerate(SLABS):
        at = 0
        for layer in layers:
            for name in ("u", "v"):
                out.append((name, layer, slab, at))
                at += width_of(layer)
        assert at <= (128 if slab < 3 else FOLDED)
    return out


def row_places():
    places, at = {}, 0
    for layer in range(STEPS):
        for name in ("u", "v", "w"):
            if (name, layer) == ("w", 0):
                continue
            rows = 8 if name == "w" else rows_of(layer)
            places[name, layer] = (at, rows)
            at += rows
    return places, at


ROW_PLACES, ROW_TOTAL = row_places()


def moved(value, where):
    sizes = tuple(lax.axis_size(axis) for axis in AXES)
    pairs = []
    for z in range(sizes[0]):
        for y in range(sizes[1]):
            for x in range(sizes[2]):
                to = where(z, y, x)
                if to is not None:
                    tz, ty, tx = to[0] % sizes[0], to[1], to[2] % sizes[2]
                    pairs.append(((z * sizes[1] + y) * sizes[2] + x, (tz * sizes[1] + ty) * sizes[2] + tx))
    return lax.ppermute(value, AXES, pairs)


def shape(*dims):
    return jax.ShapeDtypeStruct(dims, F32)


def call(kernel, outs, *args, scratch=(), in_specs=None, **more):
    name = kernel.func.__name__ if isinstance(kernel, functools.partial) else kernel.__name__
    if in_specs is not None:
        more["in_specs"] = in_specs
    return pl.pallas_call(
        kernel,
        out_shape=outs,
        scratch_shapes=list(scratch),
        compiler_params=pltpu.CompilerParams(vmem_limit_bytes=VMEM_LIMIT.get(name, 40 << 20)),
        cost_estimate=pl.CostEstimate(flops=0, bytes_accessed=int(MICROSECONDS.get(name, 0.5) * 3e6), transcendentals=0),
        name=name,
        **more,
    )(*args)


def lanes(rows):
    return lax.broadcasted_iota(jnp.int32, (rows, 128), 1)


def core():
    return lax.axis_index("gy") & 1


def seam():
    return lax.axis_index("gy") >> 1


def one_if(condition):
    return jnp.where(condition, 1.0, 0.0)


def outside():
    x, c = lax.axis_index("gx"), core()
    return ((c == 0) & (x == 0)) | ((c == 1) & (x == lax.axis_size("gx") - 1))


def plain_to_plane(ref):
    return jnp.concatenate([ref[pl.ds(t, 8, stride=VECTORS), :] for t in range(VECTORS)], axis=0)


def plane_to_plain(value, ref):
    for t in range(VECTORS):
        ref[pl.ds(t, 8, stride=VECTORS), :] = value[8 * t:8 * t + 8]


def aligned(value, to):
    return pl.multiple_of(value, to)


def power40(p):
    x = p + p
    x2 = x * x
    x4 = x2 * x2
    x8 = x4 * x4
    x32 = x8 * x8
    x32 = x32 * x32
    return x32 * x8


def power39(p):
    x = p + p
    x2 = x * x
    x4 = x2 * x2
    x8 = x4 * x4
    x32 = x8 * x8
    x32 = x32 * x32
    return x32 * (x4 * (x2 * x))


def edges(p_hbm, f_hbm, s_hbm, lowest_ref, inner_ref, outer_ref, left_ref, right_ref, turned, p_ref, sems):
    planes = [pltpu.make_async_copy(p_hbm.at[pl.ds(4 * i, 4)], p_ref.at[pl.ds(4 * i, 4)], sems.at[i]) for i in range(4)]
    copies = [pltpu.make_async_copy(ref.at[0], lowest_ref.at[i + 1], sems.at[4 + i]) for i, ref in enumerate((f_hbm, s_hbm))]
    for copy in planes + copies:
        copy.start()
    lane = lanes(128)
    c = core()
    packed = jnp.zeros((128, 128), F32)
    for layer in range(LAYERS):
        if layer % 4 == 0:
            planes[layer // 4].wait()
        inner_ref[pl.ds(layer, 1), :] = p_ref[layer, pl.ds(127 * (1 - c), 1), :]
        outer_ref[pl.ds(layer, 1), :] = p_ref[layer, pl.ds(127 * c, 1), :]
        rolled = pltpu.roll(p_ref[layer], 2 * layer + 1, 1)
        packed = jnp.where((lane >> 1) == layer, rolled, packed)
    turned[...] = packed.T
    right_ref[...] = turned[pl.ds(0, 16, stride=2), :]
    left_ref[...] = turned[pl.ds(1, 16, stride=2), :]
    lowest_ref[0] = p_ref[0]
    for copy in copies:
        copy.wait()


def early(p_ref, f_ref, s_ref, out_ref):
    out_ref[...] = p_ref[0, pl.ds(0, 8), :] + f_ref[0, pl.ds(0, 8), :] + s_ref[0, pl.ds(0, 8), :]


def norm_of(position, extent):
    def missing(k):
        k = jnp.maximum(k, 0)
        return (k * (k + 1)) >> 1

    return ((RADIUS + 1) ** 2 - missing(RADIUS - position) - missing(RADIUS - (extent - 1 - position))).astype(F32)


def terms(total, density, sens, p39):
    total = jnp.maximum(total, 1e-30)
    offset = PENALTY * math.log(2.0) / EXPONENT
    smax = jnp.exp(jnp.log(total) * (1.0 / EXPONENT) - offset)
    gap = density - smax
    half = 0.5 * gap * lax.rsqrt(gap * gap + SMOOTH)
    low = 0.5 - half
    top = (0.5 + half) * (2.0 * PENALTY / EXPONENT) * smax
    h = top / total
    return h * sens, h * p39, low, total / top


def plane_norms(sizes):
    row0 = lax.axis_index("gy") * 128
    col0 = lax.axis_index("gx") * 128
    rows = lax.broadcasted_iota(jnp.int32, (128, 128), 0) + row0
    cols = lax.broadcasted_iota(jnp.int32, (128, 128), 1) + col0
    return norm_of(rows, sizes[1] * 128) * norm_of(cols, sizes[2] * 128)


def neighbours(p, layer, inner_ref, outer_ref, beside, powers):
    c = core()
    lane = lanes(128)
    own = power40(p)
    powers[pl.ds(8, 128), :] = own
    y = lax.axis_index("gy")
    there = one_if((y == 1) | (y == 2))
    powers[pl.ds(7 + 129 * (1 - c), 1), :] = power40(inner_ref[pl.ds(layer, 1), :])
    powers[pl.ds(7 + 129 * c, 1), :] = power40(outer_ref[pl.ds(layer, 1), :]) * there
    side = pltpu.roll(beside, (128 - (2 * layer + 1)) % 128, 1)
    right = jnp.where(lane == 127, side, pltpu.roll(own, 127, 1))
    left = jnp.where(lane == 0, side, pltpu.roll(own, 1, 1))
    return (own + right) + left + (powers[pl.ds(7, 128), :] + powers[pl.ds(9, 128), :])


def columns_beside(left_ref, right_ref, turned):
    x = lax.axis_index("gx")
    turned[...] = jnp.zeros((128, 128), F32)
    turned[pl.ds(0, 16, stride=2), :] = right_ref[...] * one_if(x < lax.axis_size("gx") - 1)
    turned[pl.ds(1, 16, stride=2), :] = left_ref[...] * one_if(x > 0)
    return power40(turned[...].T)


def all_terms(
    sizes, p_ref, f_ref, s_ref, above_ref, inner_ref, outer_ref, left_ref, right_ref, early_ref,
    uvw_ref, rows_ref, same_ref, cross_ref, keep_ref, give_ref, powers, turned, w_slabs,
):
    c = core()
    beside = columns_beside(left_ref, right_ref, turned)
    norms = 1.0 / plane_norms(sizes)
    gz = lax.axis_index("gz")
    layer0 = gz * LAYERS
    lane = lanes(128)
    half_lane = lanes(64)

    def put(slab, at, left, right):
        count = left.shape[0]
        same_ref[pl.ds(at, count), :] = jnp.where(c == 0, right, left)
        cross_ref[pl.ds(at, count), :] = jnp.where(c == 0, left, right)

    def put_corner(slab, left, right):
        at, rows = CORNERS[slab]
        first, last = slice(0, rows), slice(left.shape[0] - rows, left.shape[0])
        keep_ref[pl.ds(at, rows), :] = jnp.where(c == 0, left[first], right[last])
        give_ref[pl.ds(at, rows), :] = jnp.where(c == 0, right[first], left[last])

    def terms_of(layer, slot):
        if layer == 0:
            return s_ref[0], power39(p_ref[0]), norms * (1.0 / norm_of(0 * layer0, sizes[0] * LAYERS))
        total = neighbours(p_ref[layer - 1], layer - 1, inner_ref, outer_ref, beside, powers.at[slot])
        if layer < LAYERS:
            p, f, s = p_ref[layer], f_ref[layer], s_ref[layer]
        else:
            p, f, s = above_ref[0], above_ref[1], above_ref[2]
        u, v, low, inverse = terms(total, f, s, power39(p))
        if layer == LAYERS:
            there = one_if(gz < sizes[0] - 1)
            u, v = u * there, v * there
        return u, v, low * inverse * (norms * (1.0 / norm_of(layer0 + layer, sizes[0] * LAYERS)))

    w_slabs[...] = jnp.zeros(w_slabs.shape, F32)
    count = 0
    for slab, layers in enumerate(SLABS):
        left = right = jnp.zeros((128, 128), F32)
        at = 0
        for layer in layers:
            u, v, w = terms_of(layer, count % 2)
            count += 1
            uvw_ref[layer] = u
            uvw_ref[STEPS + layer] = v
            uvw_ref[2 * STEPS + layer] = w
            width = width_of(layer)
            for plane in (u, v):
                inside = (lane >= at) & (lane < at + width)
                left = jnp.where(inside, pltpu.roll(plane, at, 1) if at else plane, left)
                right = jnp.where(inside, pltpu.roll(plane, (at + width) % 128, 1), right)
                at += width
            if layer == 0:
                continue
            for half in range(2):
                plane = w[64 * half:64 * half + 64]
                begin = 64 * half + RADIUS * (layer - 1)
                inside = (half_lane >= begin) & (half_lane < begin + RADIUS)
                moved_left = pltpu.roll(plane, begin, 1) if begin else plane
                w_slabs[0] = jnp.where(inside, moved_left, w_slabs[0])
                w_slabs[1] = jnp.where(inside, pltpu.roll(plane, (begin + RADIUS) % 128, 1), w_slabs[1])
        put_corner(slab, left, right)
        if slab < 3:
            put(slab, 128 * slab, left, right)
            continue
        folded = []
        for value in (left, right):
            total = value[:FOLDED]
            for i in range(1, 4):
                total = total + pltpu.roll(value[FOLDED * i:FOLDED * (i + 1)], FOLDED * i, 1)
            folded.append(total)
        put(slab, 384, *folded)
    put(4, 384 + FOLDED, w_slabs[0], w_slabs[1])
    put_corner(4, w_slabs[0], w_slabs[1])
    for (name, layer), (at, rows) in ROW_PLACES.items():
        start = aligned(c * (128 - rows), 8)
        rows_ref[pl.ds(at, rows), :] = plane_of(uvw_ref, name, layer)[pl.ds(start, rows), :]


def plane_of(uvw_ref, name, layer):
    return uvw_ref.at[STEPS * "uvw".index(name) + layer]


def pick_corner(keep_ref, got_ref, corner_ref):
    corner_ref[...] = jnp.where((core() ^ seam()) == 1, keep_ref[...], got_ref[...])


def slab_plane(plain, same, cross, corner):
    c = core()
    inside = one_if(jnp.logical_not(outside()))
    plain[pl.ds(256, 32), :] = jnp.zeros((32, 128), F32)
    plain[pl.ds(aligned(c * 128, 128), 128), :] = same * inside
    plain[pl.ds(aligned((1 - c) * 128, 128), 128), :] = cross * inside
    rows = corner.shape[0]
    plain[pl.ds(aligned(256 + seam() * (32 - rows), 8), rows), :] = corner * inside


def full_plane(plain, name, layer, uvw_ref, other_ref, got_ref, shared_ref):
    c = core()
    plain[pl.ds(aligned(c * 128, 128), 128), :] = plane_of(uvw_ref, name, layer)[...]
    plain[pl.ds(aligned((1 - c) * 128, 128), 128), :] = plane_of(other_ref, name, layer)[...]
    plain[pl.ds(256, 32), :] = jnp.zeros((32, 128), F32)
    start, rows = ROW_PLACES[name, layer]
    here = pl.ds(start, rows)
    to = aligned(256 + seam() * (32 - rows), 8)
    plain[pl.ds(to, rows), :] = jnp.where((c ^ seam()) == 1, got_ref[here, :], shared_ref[here, :])
    return plain_to_plane(plain)


def with_columns(base, columns, at, width):
    c = core()
    lane = lanes(PLANE)
    columns = pltpu.roll(columns, (128 - at - (1 - c) * width) & 127, 1)
    begin = (1 - c) * (128 - width)
    return jnp.where((lane >= begin) & (lane < begin + width), columns, base)


def assemble(
    uvw_ref, other_ref, got_ref, shared_ref, same_ref, cross_ref, corner_ref, uv_ref, plain, slabs
):
    c = core()
    for slab in range(4):
        if slab < 3:
            here = pl.ds(128 * slab, 128)
            same, cross = same_ref[here, :], cross_ref[here, :]
            here = pl.ds(*CORNERS[slab])
        else:
            here = pl.ds(384, FOLDED)
            same, cross = (
                jnp.concatenate([value] + [pltpu.roll(value, 128 - FOLDED * i, 1) for i in range(1, 4)], axis=0)
                for value in (same_ref[here, :], cross_ref[here, :])
            )
            here = pl.ds(*CORNERS[3])
        corner = corner_ref[here, :]
        slot = plain.at[slab % 2]
        slab_plane(slot, same, cross, corner)
        slabs[slab] = plain_to_plane(slot)
    for place, (name, layer, slab, at) in enumerate(strips()):
        base = full_plane(plain.at[place % 2], name, layer, uvw_ref, other_ref, got_ref, shared_ref)
        uv_ref[2 * (LAYERS - layer) + (name == "v")] = with_columns(base, slabs[slab], at, width_of(layer))


def assemble_w(
    uvw_ref, other_ref, got_ref, shared_ref, same_ref, cross_ref, corner_ref, w_ref, plain, slabs
):
    c = core()

    def unfolded(ref):
        value = ref[pl.ds(384 + FOLDED, 64), :]
        return jnp.concatenate([value, pltpu.roll(value, 64, 1)], axis=0)

    here = pl.ds(*CORNERS[4])
    corner = corner_ref[here, :]
    corner = pltpu.roll(corner, 64 * seam(), 1)
    slab_plane(plain.at[0], unfolded(same_ref), unfolded(cross_ref), corner)
    slabs[0] = plain_to_plane(plain.at[0])
    for layer in range(1, STEPS):
        base = full_plane(plain.at[layer % 2], "w", layer, uvw_ref, other_ref, got_ref, shared_ref)
        w_ref[layer] = with_columns(base, slabs[0], RADIUS * (layer - 1), RADIUS)
    row = lax.broadcasted_iota(jnp.int32, (PLANE, 128), 0)
    col = lax.broadcasted_iota(jnp.int32, (PLANE, 128), 1)
    a = seam()
    row = jnp.where((a == 1) & (row >= 256), row - PLANE, row) + 256 * a
    width = jnp.where(c == 0, 108, 20)
    col = jnp.where((c == 0) & (col >= width), col - 128, jnp.where((c == 1) & (col < width), col + 128, col))
    col = col + 128 * lax.axis_index("gx")
    rows, cols = 128 * lax.axis_size("gy"), 128 * lax.axis_size("gx")
    norm = norm_of(row, rows) * norm_of(col, cols) * norm_of(0 * a, LAYERS * lax.axis_size("gz"))
    inside = (row >= 0) & (row < rows) & (col >= 0) & (col < cols)
    plain[0] = jnp.where(inside, 1.0 / jnp.where(inside, norm, 1.0), 0.0)
    w_ref[0] = plain_to_plane(plain.at[0])


def step_down(values, u_ref, v_ref, out_ref):
    new = []
    for t, value in enumerate(values):
        before = values[t - 1] if t > 0 else pltpu.roll(values[-1], 1, 0)
        behind = values[t + 1] if t < VECTORS - 1 else pltpu.roll(values[0], 7, 0)
        total = (value + before) + (behind + pltpu.roll(value, 1, 1)) + pltpu.roll(value, 127, 1)
        here = pl.ds(8 * t, 8)
        new.append(u_ref[here, :] + v_ref[here, :] * total)
        out_ref[here, :] = new[-1]
    return new


def set_carry(carry, main_ref, outer_ref, halo_ref, halo_outer_ref):
    c = core()
    lane = lanes(64)
    mine = (lane >> 6) == c
    inside = one_if(jnp.logical_not(outside()))
    begin = (1 - c) * (128 - REACH)
    beyond = (lane >= begin) & (lane < begin + REACH)
    for i in range(4):
        if main_ref.shape[0] == 256:
            value = main_ref[pl.ds(64 * i, 64), :]
        else:
            value = main_ref[pl.ds(64 * (i % 2), 64), :]
            if i >= 2:
                value = pltpu.roll(value, 64, 1)
            inner = pltpu.roll(main_ref[pl.ds(128, 64), :], (32 * (2 - c) - 32 * i) & 127, 1)
            value = jnp.where(mine, value, inner)
        outer = pltpu.roll(outer_ref[...], (128 - 32 * i) % 128, 1) if i else outer_ref[...]
        carry[pl.ds(64 * i, 64), :] = jnp.where(beyond, outer * inside, value)
    lane = lanes(24)
    beyond = (lane >= begin) & (lane < begin + REACH)
    carry[pl.ds(256, 32), :] = jnp.zeros((32, 128), F32)
    carry[pl.ds(aligned(256 + 8 * seam(), 8), 24), :] = jnp.where(beyond, halo_outer_ref[...] * inside, halo_ref[...])


def merge(give_ref, got_ref, down_ref, halo_ref):
    mine = (lanes(128) >> 6) == core()
    rows = pl.ds(0, 128)
    own, other = give_ref[rows, :], got_ref[rows, :]
    down_ref[rows, :] = jnp.where(mine, own, other)
    down_ref[pl.ds(128, 128), :] = pltpu.roll(jnp.where(mine, other, own), 64, 1)
    rows = pl.ds(128, 24)
    halo_ref[...] = jnp.where(mine[:24], give_ref[rows, :], got_ref[rows, :])


def load_carry(pieces, carry):
    set_carry(carry, *pieces)
    return [carry[pl.ds(t, 8, stride=VECTORS), :] for t in range(VECTORS)]


def run_down(values, uv_ref, layers_ref, first, last, base=0):
    for layer in range(first, last - 1, -1):
        at = 2 * (LAYERS - layer)
        values = step_down(values, uv_ref.at[at], uv_ref.at[at + 1], layers_ref.at[layer - base])
    return values


def section(active, shared, *refs):
    uv_ref, refs = refs[0], refs[1:]
    pieces, before_ref = (), None
    if len(refs) > 5:
        pieces, before_ref, refs = refs[:4], refs[4], refs[5:]
    layers_ref, down_ref, outer_ref, strip_ref, carry = refs

    @pl.when(lax.axis_index("gz") == active)
    def _():
        values = load_carry(pieces, carry) if pieces else [jnp.zeros((8, 128), F32)] * VECTORS
        values = run_down(values, uv_ref, layers_ref, LAYERS, 1)
        layers_ref[0] = layers_ref[1]
        for t in range(VECTORS):
            carry[pl.ds(t, 8, stride=VECTORS), :] = values[t]
        c = core()
        mine = (lanes(128) >> 6) == c
        down_ref[pl.ds(0, 128), :] = jnp.where(
            mine, carry[pl.ds(0, 128), :], pltpu.roll(carry[pl.ds(128, 128), :], 64, 1)
        )
        lane = lanes(64)
        slab = inner = jnp.zeros((64, 128), F32)
        for i in range(4):
            block = carry[pl.ds(64 * i, 64), :]
            rolled = pltpu.roll(block, 32 * i, 1) if i else block
            begin = (32 * i + 128 - c * 32) & 127
            slab = jnp.where(((lane - begin) & 127) < 32, rolled, slab)
            if not shared:
                inner = jnp.where((lane >> 5) == i, pltpu.roll(block, (32 * i - 32 * (2 - c)) & 127, 1), inner)
        outer_ref[...] = slab
        strip = carry[pl.ds(aligned((1 - seam()) * 232, 8), 24), :]
        strip_ref[...] = strip
        if shared:
            down_ref[pl.ds(128, 24), :] = strip
        else:
            down_ref[pl.ds(128, 64), :] = inner

    if before_ref is not None:
        @pl.when(lax.axis_index("gz") != active)
        def _():
            layers_ref[...] = before_ref[...]


def section_top(uv_ref, main_ref, outer_ref, halo_ref, halo_outer_ref, before_ref, top_ref, carry):
    @pl.when(lax.axis_index("gz") == 0)
    def _():
        values = load_carry((main_ref, outer_ref, halo_ref, halo_outer_ref), carry)
        run_down(values, uv_ref, top_ref, LAYERS, LOW, LOW)

    @pl.when(lax.axis_index("gz") != 0)
    def _():
        top_ref[...] = before_ref[pl.ds(LOW, STEPS - LOW)]


def section_rest(uv_ref, top_ref, before_ref, layers_ref):
    @pl.when(lax.axis_index("gz") == 0)
    def _():
        values = [top_ref[0, pl.ds(8 * t, 8), :] for t in range(VECTORS)]
        run_down(values, uv_ref, layers_ref, LOW - 1, 0)

    @pl.when(lax.axis_index("gz") != 0)
    def _():
        layers_ref[...] = before_ref[pl.ds(0, LOW)]


def box(values):
    two = [values[i] + values[i + 1] for i in range(len(values) - 1)]
    four = [two[i] + two[i + 2] for i in range(len(two) - 2)]
    return [four[i] + values[i + 4] for i in range(len(values) - 4)]


def smooth(layers, kept_ref, plains, others, tent):
    c = core()
    row = lax.broadcasted_iota(jnp.int32, (256, 128), 0)
    col = lax.broadcasted_iota(jnp.int32, (256, 128), 1)
    distance = (row - col + RADIUS) & 127
    weight = jnp.where(distance <= 2 * RADIUS, RADIUS + 1 - jnp.abs(distance - RADIUS), 0)
    tent[...] = weight.astype(F32).astype(jnp.bfloat16)
    for k, (layer_ref, w_ref) in enumerate(layers):
        plain = plains.at[k % 4]
        values = [layer_ref[pl.ds(8 * t, 8), :] * w_ref[pl.ds(8 * t, 8), :] for t in range(VECTORS)]
        first = [pltpu.roll(value, 1, 0) for value in values[VECTORS - RADIUS:]]
        last = [pltpu.roll(value, 7, 0) for value in values[:RADIUS]]
        total = jnp.concatenate(box(box(first + values + last)), axis=0)
        high = total.astype(jnp.bfloat16)
        rest = total - high.astype(F32)
        middle = rest.astype(jnp.bfloat16)
        small = (rest - middle.astype(F32)).astype(jnp.bfloat16)
        value = jnp.dot(jnp.concatenate([high, middle], axis=1), tent[...], preferred_element_type=F32)
        value = value + jnp.dot(small, tent[pl.ds(0, 128), :], preferred_element_type=F32)
        plane_to_plain(value, plain)
        kept_ref[k] = plain[pl.ds(aligned(c * 128, 128), 128), :]
        others[k] = plain[pl.ds(aligned((1 - c) * 128, 128), 128), :]


def pair_up(others, first, count, give_ref):
    mine = (lanes(128) >> 6) == core()
    for k in range(count):
        give_ref[k] = jnp.where(mine, others[first + k], pltpu.roll(others[first + count + k], 64, 1))


def smooth_first(top_ref, before_ref, w_ref, kept_ref, give_ref, plains, others, tent):
    layers = [(top_ref.at[k], w_ref.at[LOW + k]) for k in range(STEPS - LOW)]
    layers += [(before_ref.at[k], w_ref.at[k]) for k in range(1, RADIUS)]
    smooth(layers, kept_ref, plains, others, tent)
    pair_up(others, 0, 4, give_ref)


def smooth_rest(layers_ref, w_ref, kept_ref, give_ref, give_more_ref, plains, others, tent):
    smooth([(layers_ref.at[k], w_ref.at[k]) for k in range(LOW)], kept_ref, plains, others, tent)
    pair_up(others, 0, 3, give_ref)
    pair_up(others, 6, 3, give_more_ref)


def whole(kept, got, second):
    mine = (lanes(128) >> 6) == core()
    return jnp.where(mine, kept, pltpu.roll(got, 64, 1) if second else got)


def ends(kept_ref, got_ref, top_ref, bottom_ref):
    for k in range(8):
        value = whole(kept_ref[k], got_ref[k % 4], k >= 4)
        if k < STEPS - LOW:
            top_ref[k] = value
        else:
            bottom_ref[k - (STEPS - LOW)] = value


def finish(kept_ref, got_ref, got_more_ref, top_ref, below_ref, above_ref, passive_ref, out_ref, tile):
    gz = lax.axis_index("gz")
    for k in range(LOW):
        got = got_ref if k < 6 else got_more_ref
        tile[k] = whole(kept_ref[k], got[k % 3], k % 6 >= 3)

    def layer(k):
        if k < 0:
            return jnp.where(gz > 0, below_ref[k + RADIUS], 0.0)
        if k == 0:
            return jnp.where(gz == 0, tile[0], below_ref[RADIUS])
        if k > LAYERS:
            return jnp.where(gz < lax.axis_size("gz") - 1, above_ref[k - STEPS], 0.0)
        return tile[k] if k < LOW else top_ref[k - LOW]

    for k in range(LAYERS):
        total = layer(k) * 5.0
        for offset in range(1, RADIUS + 1):
            total = total + (layer(k - offset) + layer(k + offset)) * (5.0 - offset)
        out_ref[k] = jnp.where(passive_ref[k] > 0, 0.0, total)


def to_other(value):
    return moved(value, lambda z, y, x: (z, y ^ 1, x))


def after(value, *others):
    return lax.optimization_barrier((value,) + others)[0]


def per_device(filtered, printed, sensitivity, passive):
    sizes = tuple(lax.axis_size(axis) for axis in AXES)
    depth = sizes[0]
    plane = shape(128, 128)
    edge = shape(16, 128)

    def across(z, y, x):
        return (z, y ^ 3, x) if y in (1, 2) else None

    def beside(z, y, x):
        return (z, y ^ 1, x + (1 if y & 1 else -1))

    def same(z, y, x):
        return (z, y, x + (-1 if y & 1 else 1))

    hbm = pl.BlockSpec(memory_space=pltpu.HBM)
    lowest_planes, inner, outer, left, right = call(
        edges, [shape(3, 128, 128)] + [edge] * 4, printed, filtered, sensitivity,
        in_specs=[hbm] * 3,
        scratch=[pltpu.VMEM((128, 128), F32), pltpu.VMEM((LAYERS, 128, 128), F32), pltpu.SemaphoreType.DMA((6,))],
    )
    above = moved(lowest_planes, lambda z, y, x: (z - 1, y, x))
    from_left = moved(right, lambda z, y, x: (z, y, x + 1))
    from_right = moved(left, lambda z, y, x: (z, y, x - 1))
    outer = moved(outer, lambda z, y, x: (z, y ^ 3, x))
    inner = to_other(inner)
    ready = call(early, shape(8, 128), printed, filtered, after(sensitivity, left))
    slab, corner = shape(SLAB_ROWS, 128), shape(CORNER_ROWS, 128)
    uvw, rows, to_same, to_cross, keep, give = call(
        functools.partial(all_terms, sizes),
        [shape(3 * STEPS, 128, 128), shape(ROW_TOTAL, 128), slab, slab, corner, corner],
        printed, filtered, sensitivity, above, inner, outer, from_left, from_right, ready,
        scratch=[pltpu.VMEM((2, 144, 128), F32), pltpu.VMEM((128, 128), F32), pltpu.VMEM((2, 64, 128), F32)],
    )
    got = moved(rows, across)
    from_same = moved(to_same, same)
    from_cross = moved(to_cross, beside)
    corner = call(pick_corner, corner, keep, to_other(give))
    corner = moved(corner, lambda z, y, x: (z, 3 - y, x + (1 if y & 1 else -1)))
    other = to_other(uvw)
    shared = to_other(after(got, from_same, from_cross, corner))
    parts = (uvw, other, got, shared, from_same, from_cross, corner)
    stack = shape(STEPS, PLANE, 128)
    work = [pltpu.VMEM((2, PLANE, 128), F32), pltpu.VMEM((4, PLANE, 128), F32)]
    uvs = call(assemble, shape(2 * STEPS, PLANE, 128), *parts, scratch=work)
    ws = None
    pieces, before = (), ()
    whole_stack = [pltpu.VMEM((PLANE, 128), F32)]
    for active in range(depth - 1, 0, -1):
        swap = (depth - 1 - active) % 2 == 1
        layers, main, side, strip = call(
            functools.partial(section, active, swap),
            [stack, shape(152 if swap else 192, 128), shape(64, 128), shape(24, 128)],
            uvs, *pieces, *before, scratch=whole_stack,
        )
        before = (layers,)

        def down(where):
            def to(z, y, x):
                _, ty, tx = where(z, y, x)
                return (z - 1, ty, tx) if z == active else None
            return to

        def over(z, y, x):
            return (z, y ^ 2, x)

        def corner_of(z, y, x):
            _, ty, tx = beside(z, y, x)
            return (z, ty ^ 2, tx)

        side = moved(side, down(beside))
        edge_piece = moved(strip, down(corner_of))
        halo = strip
        if swap:
            main, halo = call(merge, [shape(256, 128), shape(24, 128)], main, to_other(main))
        main = moved(main, down(lambda z, y, x: (z, y, x)))
        halo = moved(halo, down(over))
        pieces = (main, side, halo, edge_piece)
        if ws is None:
            ws = call(assemble_w, stack, after(uvw, side), *parts[1:], scratch=work)
    top_layers = call(
        section_top, shape(STEPS - LOW, PLANE, 128), uvs, *pieces, layers, scratch=whole_stack
    )

    def work_for(count):
        return [
            pltpu.VMEM((4, PLANE, 128), F32), pltpu.VMEM((count, 128, 128), F32), pltpu.VMEM((256, 128), jnp.bfloat16)
        ]

    kept, given = call(
        smooth_first, [shape(8, 128, 128), shape(4, 128, 128)], top_layers, layers, ws, scratch=work_for(8)
    )
    top, bottom = call(ends, [shape(RADIUS + 1, 128, 128), shape(RADIUS - 1, 128, 128)], kept, to_other(given))
    below = moved(top, lambda z, y, x: (z + 1, y, x))
    over = moved(bottom, lambda z, y, x: (z - 1, y, x))
    rest = call(section_rest, shape(LOW, PLANE, 128), uvs, after(top_layers, top), layers)
    third = shape(3, 128, 128)
    kept, given, given_more = call(
        smooth_rest, [shape(LOW, 128, 128), third, third], rest, ws, scratch=work_for(LOW)
    )
    return call(
        finish, shape(LAYERS, 128, 128),
        kept, to_other(given), to_other(given_more), top, below, over, passive,
        scratch=[pltpu.VMEM((LOW, 128, 128), F32)],
    )


def solution(mesh):
    spec = P(*AXES)
    return jax.shard_map(
        per_device, mesh=mesh, in_specs=(spec,) * 4, out_specs=spec, check_vma=False
    )
```

```python
import functools
import math

import jax
import jax.numpy as jnp
from jax import lax
from jax.experimental import pallas as pl
from jax.experimental.pallas import tpu as pltpu
from jax.sharding import PartitionSpec as P

RADIUS = 4
PENALTY = 40.0
EXPONENT = PENALTY + math.log(5.0) / math.log(0.5)
SMOOTH = 0.001
AXES = ("gz", "gy", "gx")
F32 = jnp.float32

LAYERS = 16
STEPS = LAYERS + 1
PLANE = 288
VECTORS = PLANE // 8
REACH = RADIUS + STEPS
LOW = LAYERS - RADIUS
SLABS = ((16, 15, 14, 3), (13, 12, 11, 8, 0), (10, 9, 7, 6, 5, 2), (4, 1))
FOLDED = 32
SLAB_ROWS = 3 * 128 + FOLDED + 64
CORNERS = ((0, 24), (24, 24), (48, 16), (64, 8), (72, 8))
CORNER_ROWS = 80


def width_of(layer):
    return RADIUS + layer


def rows_of(layer):
    return -(-width_of(layer) // 8) * 8


MICROSECONDS = {"all_terms": 2.5, "assemble": 2.5, "section": 1.5, "section_rest": 3.0, "smooth_rest": 3.0, "finish": 3.0}
VMEM_LIMIT = {"edges": 52 << 20}


def strips():
    out = []
    for slab, layers in enumerate(SLABS):
        at = 0
        for layer in layers:
            for name in ("u", "v"):
                out.append((name, layer, slab, at))
                at += width_of(layer)
        assert at <= (128 if slab < 3 else FOLDED)
    return out


def row_places():
    places, at = {}, 0
    for layer in range(STEPS):
        for name in ("u", "v", "w"):
            if (name, layer) == ("w", 0):
                continue
            rows = 8 if name == "w" else rows_of(layer)
            places[name, layer] = (at, rows)
            at += rows
    return places, at


ROW_PLACES, ROW_TOTAL = row_places()


def moved(value, where):
    sizes = tuple(lax.axis_size(axis) for axis in AXES)
    pairs = []
    for z in range(sizes[0]):
        for y in range(sizes[1]):
            for x in range(sizes[2]):
                to = where(z, y, x)
                if to is not None:
                    tz, ty, tx = to[0] % sizes[0], to[1], to[2] % sizes[2]
                    pairs.append(((z * sizes[1] + y) * sizes[2] + x, (tz * sizes[1] + ty) * sizes[2] + tx))
    return lax.ppermute(value, AXES, pairs)


def shape(*dims):
    return jax.ShapeDtypeStruct(dims, F32)


def call(kernel, outs, *args, scratch=(), in_specs=None, **more):
    name = kernel.func.__name__ if isinstance(kernel, functools.partial) else kernel.__name__
    if in_specs is not None:
        more["in_specs"] = in_specs
    return pl.pallas_call(
        kernel,
        out_shape=outs,
        scratch_shapes=list(scratch),
        compiler_params=pltpu.CompilerParams(vmem_limit_bytes=VMEM_LIMIT.get(name, 40 << 20)),
        cost_estimate=pl.CostEstimate(flops=0, bytes_accessed=int(MICROSECONDS.get(name, 0.5) * 3e6), transcendentals=0),
        name=name,
        **more,
    )(*args)


def lanes(rows):
    return lax.broadcasted_iota(jnp.int32, (rows, 128), 1)


def core():
    return lax.axis_index("gy") & 1


def seam():
    return lax.axis_index("gy") >> 1


def one_if(condition):
    return jnp.where(condition, 1.0, 0.0)


def outside():
    x, c = lax.axis_index("gx"), core()
    return ((c == 0) & (x == 0)) | ((c == 1) & (x == lax.axis_size("gx") - 1))


def plain_to_plane(ref):
    return jnp.concatenate([ref[pl.ds(t, 8, stride=VECTORS), :] for t in range(VECTORS)], axis=0)


def plane_to_plain(value, ref):
    for t in range(VECTORS):
        ref[pl.ds(t, 8, stride=VECTORS), :] = value[8 * t:8 * t + 8]


def aligned(value, to):
    return pl.multiple_of(value, to)


def power40(p):
    x = p + p
    x2 = x * x
    x4 = x2 * x2
    x8 = x4 * x4
    x32 = x8 * x8
    x32 = x32 * x32
    return x32 * x8


def power39(p):
    x = p + p
    x2 = x * x
    x4 = x2 * x2
    x8 = x4 * x4
    x32 = x8 * x8
    x32 = x32 * x32
    return x32 * (x4 * (x2 * x))


def edges(p_hbm, f_hbm, s_hbm, lowest_ref, inner_ref, outer_ref, left_ref, right_ref, turned, p_ref, sems):
    planes = [pltpu.make_async_copy(p_hbm.at[pl.ds(4 * i, 4)], p_ref.at[pl.ds(4 * i, 4)], sems.at[i]) for i in range(4)]
    copies = [pltpu.make_async_copy(ref.at[0], lowest_ref.at[i + 1], sems.at[4 + i]) for i, ref in enumerate((f_hbm, s_hbm))]
    for copy in planes + copies:
        copy.start()
    lane = lanes(128)
    c = core()
    packed = jnp.zeros((128, 128), F32)
    for layer in range(LAYERS):
        if layer % 4 == 0:
            planes[layer // 4].wait()
        inner_ref[pl.ds(layer, 1), :] = p_ref[layer, pl.ds(127 * (1 - c), 1), :]
        outer_ref[pl.ds(layer, 1), :] = p_ref[layer, pl.ds(127 * c, 1), :]
        rolled = pltpu.roll(p_ref[layer], 2 * layer + 1, 1)
        packed = jnp.where((lane >> 1) == layer, rolled, packed)
    turned[...] = packed.T
    right_ref[...] = turned[pl.ds(0, 16, stride=2), :]
    left_ref[...] = turned[pl.ds(1, 16, stride=2), :]
    lowest_ref[0] = p_ref[0]
    for copy in copies:
        copy.wait()


def early(p_ref, f_ref, s_ref, out_ref):
    out_ref[...] = p_ref[0, pl.ds(0, 8), :] + f_ref[0, pl.ds(0, 8), :] + s_ref[0, pl.ds(0, 8), :]


def norm_of(position, extent):
    def missing(k):
        k = jnp.maximum(k, 0)
        return (k * (k + 1)) >> 1

    return ((RADIUS + 1) ** 2 - missing(RADIUS - position) - missing(RADIUS - (extent - 1 - position))).astype(F32)


def terms(total, density, sens, p39):
    total = jnp.maximum(total, 1e-30)
    offset = PENALTY * math.log(2.0) / EXPONENT
    smax = jnp.exp(jnp.log(total) * (1.0 / EXPONENT) - offset)
    gap = density - smax
    half = 0.5 * gap * lax.rsqrt(gap * gap + SMOOTH)
    low = 0.5 - half
    top = (0.5 + half) * (2.0 * PENALTY / EXPONENT) * smax
    h = top / total
    return h * sens, h * p39, low, total / top


def plane_norms(sizes):
    row0 = lax.axis_index("gy") * 128
    col0 = lax.axis_index("gx") * 128
    rows = lax.broadcasted_iota(jnp.int32, (128, 128), 0) + row0
    cols = lax.broadcasted_iota(jnp.int32, (128, 128), 1) + col0
    return norm_of(rows, sizes[1] * 128) * norm_of(cols, sizes[2] * 128)


def neighbours(p, layer, inner_ref, outer_ref, beside, powers):
    c = core()
    lane = lanes(128)
    own = power40(p)
    powers[pl.ds(8, 128), :] = own
    y = lax.axis_index("gy")
    there = one_if((y == 1) | (y == 2))
    powers[pl.ds(7 + 129 * (1 - c), 1), :] = power40(inner_ref[pl.ds(layer, 1), :])
    powers[pl.ds(7 + 129 * c, 1), :] = power40(outer_ref[pl.ds(layer, 1), :]) * there
    side = pltpu.roll(beside, (128 - (2 * layer + 1)) % 128, 1)
    right = jnp.where(lane == 127, side, pltpu.roll(own, 127, 1))
    left = jnp.where(lane == 0, side, pltpu.roll(own, 1, 1))
    return (own + right) + left + (powers[pl.ds(7, 128), :] + powers[pl.ds(9, 128), :])


def columns_beside(left_ref, right_ref, turned):
    x = lax.axis_index("gx")
    turned[...] = jnp.zeros((128, 128), F32)
    turned[pl.ds(0, 16, stride=2), :] = right_ref[...] * one_if(x < lax.axis_size("gx") - 1)
    turned[pl.ds(1, 16, stride=2), :] = left_ref[...] * one_if(x > 0)
    return power40(turned[...].T)


def all_terms(
    sizes, p_ref, f_ref, s_ref, above_ref, inner_ref, outer_ref, left_ref, right_ref, early_ref, uvw_ref, powers, turned
):
    beside = columns_beside(left_ref, right_ref, turned)
    norms = 1.0 / plane_norms(sizes)
    gz = lax.axis_index("gz")
    layer0 = gz * LAYERS
    uvw_ref[0] = s_ref[0]
    uvw_ref[STEPS] = power39(p_ref[0])
    uvw_ref[2 * STEPS] = norms * (1.0 / norm_of(0 * layer0, sizes[0] * LAYERS))
    for layer in range(1, STEPS):
        total = neighbours(p_ref[layer - 1], layer - 1, inner_ref, outer_ref, beside, powers)
        if layer < LAYERS:
            p, f, s = p_ref[layer], f_ref[layer], s_ref[layer]
        else:
            p, f, s = above_ref[0], above_ref[1], above_ref[2]
        u, v, low, inverse = terms(total, f, s, power39(p))
        if layer == LAYERS:
            there = one_if(gz < sizes[0] - 1)
            u, v = u * there, v * there
        norm_z = norm_of(layer0 + layer, sizes[0] * LAYERS)
        uvw_ref[layer] = u
        uvw_ref[STEPS + layer] = v
        uvw_ref[2 * STEPS + layer] = low * inverse * (norms * (1.0 / norm_z))


def plane_of(uvw_ref, name, layer):
    return uvw_ref.at[STEPS * "uvw".index(name) + layer]


def pack_rows(uvw_ref, rows_ref):
    c = core()
    for (name, layer), (at, rows) in ROW_PLACES.items():
        start = aligned(c * (128 - rows), 8)
        rows_ref[pl.ds(at, rows), :] = plane_of(uvw_ref, name, layer)[pl.ds(start, rows), :]


def pack(uvw_ref, same_ref, cross_ref, keep_ref, give_ref):
    c = core()

    def put(at, left, right):
        count = left.shape[0]
        same_ref[pl.ds(at, count), :] = jnp.where(c == 0, right, left)
        cross_ref[pl.ds(at, count), :] = jnp.where(c == 0, left, right)

    def put_corner(slab, left, right):
        at, rows = CORNERS[slab]
        first, last = slice(0, rows), slice(left.shape[0] - rows, left.shape[0])
        keep_ref[pl.ds(at, rows), :] = jnp.where(c == 0, left[first], right[last])
        give_ref[pl.ds(at, rows), :] = jnp.where(c == 0, right[first], left[last])

    lane = lanes(128)
    for slab in range(4):
        left = right = jnp.zeros((128, 128), F32)
        for name, layer, where, at in strips():
            if where == slab:
                width = width_of(layer)
                plane = plane_of(uvw_ref, name, layer)[...]
                inside = (lane >= at) & (lane < at + width)
                left = jnp.where(inside, pltpu.roll(plane, at, 1) if at else plane, left)
                right = jnp.where(inside, pltpu.roll(plane, (at + width) % 128, 1), right)
        if slab < 3:
            put(128 * slab, left, right)
            put_corner(slab, left, right)
            continue
        put_corner(slab, left, right)
        folded = []
        for value in (left, right):
            total = value[:FOLDED]
            for i in range(1, 4):
                total = total + pltpu.roll(value[FOLDED * i:FOLDED * (i + 1)], FOLDED * i, 1)
            folded.append(total)
        put(384, *folded)
    lane = lanes(64)
    left = right = jnp.zeros((64, 128), F32)
    for layer in range(1, STEPS):
        ref = plane_of(uvw_ref, "w", layer)
        for half in range(2):
            plane = ref[pl.ds(64 * half, 64), :]
            at = 64 * half + RADIUS * (layer - 1)
            inside = (lane >= at) & (lane < at + RADIUS)
            left = jnp.where(inside, pltpu.roll(plane, at, 1) if at else plane, left)
            right = jnp.where(inside, pltpu.roll(plane, (at + RADIUS) % 128, 1), right)
    put(384 + FOLDED, left, right)
    put_corner(4, left, right)


def join(own_ref, other_ref, out_ref):
    out_ref[pl.ds(0, SLAB_ROWS), :] = own_ref[...]
    out_ref[pl.ds(SLAB_ROWS, SLAB_ROWS), :] = other_ref[...]


def pick_corner(keep_ref, got_ref, corner_ref):
    corner_ref[...] = jnp.where((core() ^ seam()) == 1, keep_ref[...], got_ref[...])


def slab_plane(plain, same, cross, corner):
    c = core()
    inside = one_if(jnp.logical_not(outside()))
    plain[pl.ds(256, 32), :] = jnp.zeros((32, 128), F32)
    plain[pl.ds(aligned(c * 128, 128), 128), :] = same * inside
    plain[pl.ds(aligned((1 - c) * 128, 128), 128), :] = cross * inside
    rows = corner.shape[0]
    plain[pl.ds(aligned(256 + seam() * (32 - rows), 8), rows), :] = corner * inside


def full_plane(plain, name, layer, uvw_ref, other_ref, got_ref, shared_ref):
    c = core()
    plain[pl.ds(aligned(c * 128, 128), 128), :] = plane_of(uvw_ref, name, layer)[...]
    plain[pl.ds(aligned((1 - c) * 128, 128), 128), :] = plane_of(other_ref, name, layer)[...]
    plain[pl.ds(256, 32), :] = jnp.zeros((32, 128), F32)
    start, rows = ROW_PLACES[name, layer]
    here = pl.ds(start, rows)
    to = aligned(256 + seam() * (32 - rows), 8)
    plain[pl.ds(to, rows), :] = jnp.where((c ^ seam()) == 1, got_ref[here, :], shared_ref[here, :])
    return plain_to_plane(plain)


def with_columns(base, columns, at, width):
    c = core()
    lane = lanes(PLANE)
    columns = pltpu.roll(columns, (128 - at - (1 - c) * width) & 127, 1)
    begin = (1 - c) * (128 - width)
    return jnp.where((lane >= begin) & (lane < begin + width), columns, base)


def assemble(
    uvw_ref, other_ref, got_ref, shared_ref, came_ref, corner_ref, uv_ref, plain, slabs
):
    c = core()
    cross_ref, same_ref = (came_ref.at[pl.ds(SLAB_ROWS * i, SLAB_ROWS)] for i in range(2))
    for slab in range(4):
        if slab < 3:
            here = pl.ds(128 * slab, 128)
            same, cross = same_ref[here, :], cross_ref[here, :]
            here = pl.ds(*CORNERS[slab])
        else:
            here = pl.ds(384, FOLDED)
            same, cross = (
                jnp.concatenate([value] + [pltpu.roll(value, 128 - FOLDED * i, 1) for i in range(1, 4)], axis=0)
                for value in (same_ref[here, :], cross_ref[here, :])
            )
            here = pl.ds(*CORNERS[3])
        corner = corner_ref[here, :]
        slot = plain.at[slab % 2]
        slab_plane(slot, same, cross, corner)
        slabs[slab] = plain_to_plane(slot)
    for place, (name, layer, slab, at) in enumerate(strips()):
        base = full_plane(plain.at[place % 2], name, layer, uvw_ref, other_ref, got_ref, shared_ref)
        uv_ref[2 * (LAYERS - layer) + (name == "v")] = with_columns(base, slabs[slab], at, width_of(layer))


def assemble_w(
    uvw_ref, other_ref, got_ref, shared_ref, came_ref, corner_ref, w_ref, plain, slabs
):
    c = core()
    cross_ref, same_ref = (came_ref.at[pl.ds(SLAB_ROWS * i, SLAB_ROWS)] for i in range(2))

    def unfolded(ref):
        value = ref[pl.ds(384 + FOLDED, 64), :]
        return jnp.concatenate([value, pltpu.roll(value, 64, 1)], axis=0)

    here = pl.ds(*CORNERS[4])
    corner = corner_ref[here, :]
    corner = pltpu.roll(corner, 64 * seam(), 1)
    slab_plane(plain.at[0], unfolded(same_ref), unfolded(cross_ref), corner)
    slabs[0] = plain_to_plane(plain.at[0])
    for layer in range(1, STEPS):
        base = full_plane(plain.at[layer % 2], "w", layer, uvw_ref, other_ref, got_ref, shared_ref)
        w_ref[layer] = with_columns(base, slabs[0], RADIUS * (layer - 1), RADIUS)
    row = lax.broadcasted_iota(jnp.int32, (PLANE, 128), 0)
    col = lax.broadcasted_iota(jnp.int32, (PLANE, 128), 1)
    a = seam()
    row = jnp.where((a == 1) & (row >= 256), row - PLANE, row) + 256 * a
    width = jnp.where(c == 0, 108, 20)
    col = jnp.where((c == 0) & (col >= width), col - 128, jnp.where((c == 1) & (col < width), col + 128, col))
    col = col + 128 * lax.axis_index("gx")
    rows, cols = 128 * lax.axis_size("gy"), 128 * lax.axis_size("gx")
    norm = norm_of(row, rows) * norm_of(col, cols) * norm_of(0 * a, LAYERS * lax.axis_size("gz"))
    inside = (row >= 0) & (row < rows) & (col >= 0) & (col < cols)
    plain[0] = jnp.where(inside, 1.0 / jnp.where(inside, norm, 1.0), 0.0)
    w_ref[0] = plain_to_plane(plain.at[0])


def step_down(values, u_ref, v_ref, out_ref):
    new = []
    for t, value in enumerate(values):
        before = values[t - 1] if t > 0 else pltpu.roll(values[-1], 1, 0)
        behind = values[t + 1] if t < VECTORS - 1 else pltpu.roll(values[0], 7, 0)
        total = (value + before) + (behind + pltpu.roll(value, 1, 1)) + pltpu.roll(value, 127, 1)
        here = pl.ds(8 * t, 8)
        new.append(u_ref[here, :] + v_ref[here, :] * total)
        out_ref[here, :] = new[-1]
    return new


def set_carry(carry, main_ref, outer_ref, halo_ref, halo_outer_ref):
    c = core()
    lane = lanes(64)
    mine = (lane >> 6) == c
    inside = one_if(jnp.logical_not(outside()))
    begin = (1 - c) * (128 - REACH)
    beyond = (lane >= begin) & (lane < begin + REACH)
    for i in range(4):
        if main_ref.shape[0] == 256:
            value = main_ref[pl.ds(64 * i, 64), :]
        else:
            value = main_ref[pl.ds(64 * (i % 2), 64), :]
            if i >= 2:
                value = pltpu.roll(value, 64, 1)
            inner = pltpu.roll(main_ref[pl.ds(128, 64), :], (32 * (2 - c) - 32 * i) & 127, 1)
            value = jnp.where(mine, value, inner)
        outer = pltpu.roll(outer_ref[...], (128 - 32 * i) % 128, 1) if i else outer_ref[...]
        carry[pl.ds(64 * i, 64), :] = jnp.where(beyond, outer * inside, value)
    lane = lanes(24)
    beyond = (lane >= begin) & (lane < begin + REACH)
    carry[pl.ds(256, 32), :] = jnp.zeros((32, 128), F32)
    carry[pl.ds(aligned(256 + 8 * seam(), 8), 24), :] = jnp.where(beyond, halo_outer_ref[...] * inside, halo_ref[...])


def merge(give_ref, got_ref, down_ref, halo_ref):
    mine = (lanes(128) >> 6) == core()
    rows = pl.ds(0, 128)
    own, other = give_ref[rows, :], got_ref[rows, :]
    down_ref[rows, :] = jnp.where(mine, own, other)
    down_ref[pl.ds(128, 128), :] = pltpu.roll(jnp.where(mine, other, own), 64, 1)
    rows = pl.ds(128, 24)
    halo_ref[...] = jnp.where(mine[:24], give_ref[rows, :], got_ref[rows, :])


def load_carry(pieces, carry):
    set_carry(carry, *pieces)
    return [carry[pl.ds(t, 8, stride=VECTORS), :] for t in range(VECTORS)]


def run_down(values, uv_ref, layers_ref, first, last, base=0):
    for layer in range(first, last - 1, -1):
        at = 2 * (LAYERS - layer)
        values = step_down(values, uv_ref.at[at], uv_ref.at[at + 1], layers_ref.at[layer - base])
    return values


def section(active, shared, *refs):
    uv_ref, refs = refs[0], refs[1:]
    pieces, before_ref = (), None
    if len(refs) > 5:
        pieces, before_ref, refs = refs[:4], refs[4], refs[5:]
    layers_ref, down_ref, outer_ref, strip_ref, carry = refs

    @pl.when(lax.axis_index("gz") == active)
    def _():
        values = load_carry(pieces, carry) if pieces else [jnp.zeros((8, 128), F32)] * VECTORS
        values = run_down(values, uv_ref, layers_ref, LAYERS, 1)
        layers_ref[0] = layers_ref[1]
        for t in range(VECTORS):
            carry[pl.ds(t, 8, stride=VECTORS), :] = values[t]
        c = core()
        mine = (lanes(128) >> 6) == c
        down_ref[pl.ds(0, 128), :] = jnp.where(
            mine, carry[pl.ds(0, 128), :], pltpu.roll(carry[pl.ds(128, 128), :], 64, 1)
        )
        lane = lanes(64)
        slab = inner = jnp.zeros((64, 128), F32)
        for i in range(4):
            block = carry[pl.ds(64 * i, 64), :]
            rolled = pltpu.roll(block, 32 * i, 1) if i else block
            begin = (32 * i + 128 - c * 32) & 127
            slab = jnp.where(((lane - begin) & 127) < 32, rolled, slab)
            if not shared:
                inner = jnp.where((lane >> 5) == i, pltpu.roll(block, (32 * i - 32 * (2 - c)) & 127, 1), inner)
        outer_ref[...] = slab
        strip = carry[pl.ds(aligned((1 - seam()) * 232, 8), 24), :]
        strip_ref[...] = strip
        if shared:
            down_ref[pl.ds(128, 24), :] = strip
        else:
            down_ref[pl.ds(128, 64), :] = inner

    if before_ref is not None:
        @pl.when(lax.axis_index("gz") != active)
        def _():
            layers_ref[...] = before_ref[...]


def section_top(uv_ref, main_ref, outer_ref, halo_ref, halo_outer_ref, before_ref, top_ref, carry):
    @pl.when(lax.axis_index("gz") == 0)
    def _():
        values = load_carry((main_ref, outer_ref, halo_ref, halo_outer_ref), carry)
        run_down(values, uv_ref, top_ref, LAYERS, LOW, LOW)

    @pl.when(lax.axis_index("gz") != 0)
    def _():
        top_ref[...] = before_ref[pl.ds(LOW, STEPS - LOW)]


def section_rest(uv_ref, top_ref, before_ref, layers_ref):
    @pl.when(lax.axis_index("gz") == 0)
    def _():
        values = [top_ref[0, pl.ds(8 * t, 8), :] for t in range(VECTORS)]
        run_down(values, uv_ref, layers_ref, LOW - 1, 0)

    @pl.when(lax.axis_index("gz") != 0)
    def _():
        layers_ref[...] = before_ref[pl.ds(0, LOW)]


def box(values):
    two = [values[i] + values[i + 1] for i in range(len(values) - 1)]
    four = [two[i] + two[i + 2] for i in range(len(two) - 2)]
    return [four[i] + values[i + 4] for i in range(len(values) - 4)]


def smooth(layers, kept_ref, plains, others, tent):
    c = core()
    row = lax.broadcasted_iota(jnp.int32, (256, 128), 0)
    col = lax.broadcasted_iota(jnp.int32, (256, 128), 1)
    distance = (row - col + RADIUS) & 127
    weight = jnp.where(distance <= 2 * RADIUS, RADIUS + 1 - jnp.abs(distance - RADIUS), 0)
    tent[...] = weight.astype(F32).astype(jnp.bfloat16)
    for k, (layer_ref, w_ref) in enumerate(layers):
        plain = plains.at[k % 4]
        values = [layer_ref[pl.ds(8 * t, 8), :] * w_ref[pl.ds(8 * t, 8), :] for t in range(VECTORS)]
        first = [pltpu.roll(value, 1, 0) for value in values[VECTORS - RADIUS:]]
        last = [pltpu.roll(value, 7, 0) for value in values[:RADIUS]]
        total = jnp.concatenate(box(box(first + values + last)), axis=0)
        high = total.astype(jnp.bfloat16)
        rest = total - high.astype(F32)
        middle = rest.astype(jnp.bfloat16)
        small = (rest - middle.astype(F32)).astype(jnp.bfloat16)
        value = jnp.dot(jnp.concatenate([high, middle], axis=1), tent[...], preferred_element_type=F32)
        value = value + jnp.dot(small, tent[pl.ds(0, 128), :], preferred_element_type=F32)
        plane_to_plain(value, plain)
        kept_ref[k] = plain[pl.ds(aligned(c * 128, 128), 128), :]
        others[k] = plain[pl.ds(aligned((1 - c) * 128, 128), 128), :]


def pair_up(others, first, count, give_ref):
    mine = (lanes(128) >> 6) == core()
    for k in range(count):
        give_ref[k] = jnp.where(mine, others[first + k], pltpu.roll(others[first + count + k], 64, 1))


def smooth_first(top_ref, before_ref, w_ref, kept_ref, give_ref, plains, others, tent):
    layers = [(top_ref.at[k], w_ref.at[LOW + k]) for k in range(STEPS - LOW)]
    layers += [(before_ref.at[k], w_ref.at[k]) for k in range(1, RADIUS)]
    smooth(layers, kept_ref, plains, others, tent)
    pair_up(others, 0, 4, give_ref)


def smooth_rest(layers_ref, w_ref, kept_ref, give_ref, give_more_ref, plains, others, tent):
    smooth([(layers_ref.at[k], w_ref.at[k]) for k in range(LOW)], kept_ref, plains, others, tent)
    pair_up(others, 0, 3, give_ref)
    pair_up(others, 6, 3, give_more_ref)


def whole(kept, got, second):
    mine = (lanes(128) >> 6) == core()
    return jnp.where(mine, kept, pltpu.roll(got, 64, 1) if second else got)


def ends(kept_ref, got_ref, top_ref, bottom_ref):
    for k in range(8):
        value = whole(kept_ref[k], got_ref[k % 4], k >= 4)
        if k < STEPS - LOW:
            top_ref[k] = value
        else:
            bottom_ref[k - (STEPS - LOW)] = value


def finish(kept_ref, got_ref, got_more_ref, top_ref, below_ref, above_ref, passive_ref, out_ref, tile):
    gz = lax.axis_index("gz")
    for k in range(LOW):
        got = got_ref if k < 6 else got_more_ref
        tile[k] = whole(kept_ref[k], got[k % 3], k % 6 >= 3)

    def layer(k):
        if k < 0:
            return jnp.where(gz > 0, below_ref[k + RADIUS], 0.0)
        if k == 0:
            return jnp.where(gz == 0, tile[0], below_ref[RADIUS])
        if k > LAYERS:
            return jnp.where(gz < lax.axis_size("gz") - 1, above_ref[k - STEPS], 0.0)
        return tile[k] if k < LOW else top_ref[k - LOW]

    for k in range(LAYERS):
        total = layer(k) * 5.0
        for offset in range(1, RADIUS + 1):
            total = total + (layer(k - offset) + layer(k + offset)) * (5.0 - offset)
        out_ref[k] = jnp.where(passive_ref[k] > 0, 0.0, total)


def to_other(value):
    return moved(value, lambda z, y, x: (z, y ^ 1, x))


def after(value, *others):
    return lax.optimization_barrier((value,) + others)[0]


def per_device(filtered, printed, sensitivity, passive):
    sizes = tuple(lax.axis_size(axis) for axis in AXES)
    depth = sizes[0]
    plane = shape(128, 128)
    edge = shape(16, 128)

    def across(z, y, x):
        return (z, y ^ 3, x) if y in (1, 2) else None

    def beside(z, y, x):
        return (z, y ^ 1, x + (1 if y & 1 else -1))

    hbm = pl.BlockSpec(memory_space=pltpu.HBM)
    lowest_planes, inner, outer, left, right = call(
        edges, [shape(3, 128, 128)] + [edge] * 4, printed, filtered, sensitivity,
        in_specs=[hbm] * 3,
        scratch=[pltpu.VMEM((128, 128), F32), pltpu.VMEM((LAYERS, 128, 128), F32), pltpu.SemaphoreType.DMA((6,))],
    )
    above = moved(lowest_planes, lambda z, y, x: (z - 1, y, x))
    from_left = moved(right, lambda z, y, x: (z, y, x + 1))
    from_right = moved(left, lambda z, y, x: (z, y, x - 1))
    outer = moved(outer, lambda z, y, x: (z, y ^ 3, x))
    inner = to_other(inner)
    ready = call(early, shape(8, 128), printed, filtered, after(sensitivity, left))
    uvw = call(
        functools.partial(all_terms, sizes), shape(3 * STEPS, 128, 128),
        printed, filtered, sensitivity, above, inner, outer, from_left, from_right, ready,
        scratch=[
            pltpu.VMEM((144, 128), F32), pltpu.VMEM((128, 128), F32),
        ],
    )
    slab, corner = shape(SLAB_ROWS, 128), shape(CORNER_ROWS, 128)
    rows = call(pack_rows, shape(ROW_TOTAL, 128), uvw)
    got = moved(rows, across)
    to_same, to_cross, keep, give = call(pack, [slab, slab, corner, corner], after(uvw, rows))
    came = moved(call(join, shape(2 * SLAB_ROWS, 128), to_cross, to_other(to_same)), beside)
    corner = call(pick_corner, corner, keep, to_other(give))
    corner = moved(corner, lambda z, y, x: (z, 3 - y, x + (1 if y & 1 else -1)))
    other = to_other(uvw)
    shared = to_other(after(got, came, corner))
    parts = (uvw, other, got, shared, came, corner)
    stack = shape(STEPS, PLANE, 128)
    work = [pltpu.VMEM((2, PLANE, 128), F32), pltpu.VMEM((4, PLANE, 128), F32)]
    uvs = call(assemble, shape(2 * STEPS, PLANE, 128), *parts, scratch=work)
    ws = None
    pieces, before = (), ()
    whole_stack = [pltpu.VMEM((PLANE, 128), F32)]
    for active in range(depth - 1, 0, -1):
        swap = (depth - 1 - active) % 2 == 1
        layers, main, side, strip = call(
            functools.partial(section, active, swap),
            [stack, shape(152 if swap else 192, 128), shape(64, 128), shape(24, 128)],
            uvs, *pieces, *before, scratch=whole_stack,
        )
        before = (layers,)

        def down(where):
            def to(z, y, x):
                _, ty, tx = where(z, y, x)
                return (z - 1, ty, tx) if z == active else None
            return to

        def over(z, y, x):
            return (z, y ^ 2, x)

        def corner_of(z, y, x):
            _, ty, tx = beside(z, y, x)
            return (z, ty ^ 2, tx)

        side = moved(side, down(beside))
        edge_piece = moved(strip, down(corner_of))
        halo = strip
        if swap:
            main, halo = call(merge, [shape(256, 128), shape(24, 128)], main, to_other(main))
        main = moved(main, down(lambda z, y, x: (z, y, x)))
        halo = moved(halo, down(over))
        pieces = (main, side, halo, edge_piece)
        if ws is None:
            ws = call(assemble_w, stack, after(uvw, side), *parts[1:], scratch=work)
    top_layers = call(
        section_top, shape(STEPS - LOW, PLANE, 128), uvs, *pieces, layers, scratch=whole_stack
    )

    def work_for(count):
        return [
            pltpu.VMEM((4, PLANE, 128), F32), pltpu.VMEM((count, 128, 128), F32), pltpu.VMEM((256, 128), jnp.bfloat16)
        ]

    kept, given = call(
        smooth_first, [shape(8, 128, 128), shape(4, 128, 128)], top_layers, layers, ws, scratch=work_for(8)
    )
    top, bottom = call(ends, [shape(RADIUS + 1, 128, 128), shape(RADIUS - 1, 128, 128)], kept, to_other(given))
    below = moved(top, lambda z, y, x: (z + 1, y, x))
    over = moved(bottom, lambda z, y, x: (z - 1, y, x))
    rest = call(section_rest, shape(LOW, PLANE, 128), uvs, after(top_layers, top), layers)
    third = shape(3, 128, 128)
    kept, given, given_more = call(
        smooth_rest, [shape(LOW, 128, 128), third, third], rest, ws, scratch=work_for(LOW)
    )
    return call(
        finish, shape(LAYERS, 128, 128),
        kept, to_other(given), to_other(given_more), top, below, over, passive,
        scratch=[pltpu.VMEM((LOW, 128, 128), F32)],
    )


def solution(mesh):
    spec = P(*AXES)
    return jax.shard_map(
        per_device, mesh=mesh, in_specs=(spec,) * 4, out_specs=spec, check_vma=False
    )
```

```python
import functools
import math

import jax
import jax.numpy as jnp
from jax import lax
from jax.experimental import pallas as pl
from jax.experimental.pallas import tpu as pltpu
from jax.sharding import PartitionSpec as P

RADIUS = 4
PENALTY = 40.0
EXPONENT = PENALTY + math.log(5.0) / math.log(0.5)
SMOOTH = 0.001
AXES = ("gz", "gy", "gx")
F32 = jnp.float32

LAYERS = 16
STEPS = LAYERS + 1
PLANE = 288
VECTORS = PLANE // 8
REACH = RADIUS + STEPS
LOW = LAYERS - RADIUS
SLABS = ((16, 15, 14, 3), (13, 12, 11, 8, 0), (10, 9, 7, 6, 5, 2), (4, 1))
FOLDED = 32
SLAB_ROWS = 3 * 128 + FOLDED + 64
CORNERS = ((0, 24), (24, 24), (48, 16), (64, 8), (72, 8))
CORNER_ROWS = 80


def width_of(layer):
    return RADIUS + layer


def rows_of(layer):
    return -(-width_of(layer) // 8) * 8


MICROSECONDS = {"all_terms": 2.5, "assemble": 2.5, "section": 1.5, "section_rest": 3.0, "smooth_rest": 3.0, "finish": 3.0}
VMEM_LIMIT = {"edges": 52 << 20}


def strips():
    out = []
    for slab, layers in enumerate(SLABS):
        at = 0
        for layer in layers:
            for name in ("u", "v"):
                out.append((name, layer, slab, at))
                at += width_of(layer)
        assert at <= (128 if slab < 3 else FOLDED)
    return out


def row_places():
    places, at = {}, 0
    for layer in range(STEPS):
        for name in ("u", "v", "w"):
            if (name, layer) == ("w", 0):
                continue
            rows = 8 if name == "w" else rows_of(layer)
            places[name, layer] = (at, rows)
            at += rows
    return places, at


ROW_PLACES, ROW_TOTAL = row_places()


def moved(value, where):
    sizes = tuple(lax.axis_size(axis) for axis in AXES)
    pairs = []
    for z in range(sizes[0]):
        for y in range(sizes[1]):
            for x in range(sizes[2]):
                to = where(z, y, x)
                if to is not None:
                    tz, ty, tx = to[0] % sizes[0], to[1], to[2] % sizes[2]
                    pairs.append(((z * sizes[1] + y) * sizes[2] + x, (tz * sizes[1] + ty) * sizes[2] + tx))
    return lax.ppermute(value, AXES, pairs)


def shape(*dims):
    return jax.ShapeDtypeStruct(dims, F32)


def call(kernel, outs, *args, scratch=(), in_specs=None, **more):
    name = kernel.func.__name__ if isinstance(kernel, functools.partial) else kernel.__name__
    if in_specs is not None:
        more["in_specs"] = in_specs
    return pl.pallas_call(
        kernel,
        out_shape=outs,
        scratch_shapes=list(scratch),
        compiler_params=pltpu.CompilerParams(vmem_limit_bytes=VMEM_LIMIT.get(name, 40 << 20)),
        cost_estimate=pl.CostEstimate(flops=0, bytes_accessed=int(MICROSECONDS.get(name, 0.5) * 3e6), transcendentals=0),
        name=name,
        **more,
    )(*args)


def lanes(rows):
    return lax.broadcasted_iota(jnp.int32, (rows, 128), 1)


def core():
    return lax.axis_index("gy") & 1


def seam():
    return lax.axis_index("gy") >> 1


def one_if(condition):
    return jnp.where(condition, 1.0, 0.0)


def outside():
    x, c = lax.axis_index("gx"), core()
    return ((c == 0) & (x == 0)) | ((c == 1) & (x == lax.axis_size("gx") - 1))


def plain_to_plane(ref):
    return jnp.concatenate([ref[pl.ds(t, 8, stride=VECTORS), :] for t in range(VECTORS)], axis=0)


def plane_to_plain(value, ref):
    for t in range(VECTORS):
        ref[pl.ds(t, 8, stride=VECTORS), :] = value[8 * t:8 * t + 8]


def aligned(value, to):
    return pl.multiple_of(value, to)


def power40(p):
    x = p + p
    x2 = x * x
    x4 = x2 * x2
    x8 = x4 * x4
    x32 = x8 * x8
    x32 = x32 * x32
    return x32 * x8


def power39(p):
    x = p + p
    x2 = x * x
    x4 = x2 * x2
    x8 = x4 * x4
    x32 = x8 * x8
    x32 = x32 * x32
    return x32 * (x4 * (x2 * x))


def edges(p_hbm, f_hbm, s_hbm, lowest_ref, inner_ref, outer_ref, along_ref, back_ref, turned, p_ref, sems):
    planes = [pltpu.make_async_copy(p_hbm.at[pl.ds(4 * i, 4)], p_ref.at[pl.ds(4 * i, 4)], sems.at[i]) for i in range(4)]
    copies = [pltpu.make_async_copy(ref.at[0], lowest_ref.at[i + 1], sems.at[4 + i]) for i, ref in enumerate((f_hbm, s_hbm))]
    for copy in planes + copies:
        copy.start()
    lane = lanes(128)
    c = core()
    packed = jnp.zeros((128, 128), F32)
    for layer in range(LAYERS):
        if layer % 4 == 0:
            planes[layer // 4].wait()
        inner_ref[pl.ds(layer, 1), :] = p_ref[layer, pl.ds(127 * (1 - c), 1), :]
        outer_ref[pl.ds(layer, 1), :] = p_ref[layer, pl.ds(127 * c, 1), :]
        rolled = pltpu.roll(p_ref[layer], 2 * layer + 1, 1)
        packed = jnp.where((lane >> 1) == layer, rolled, packed)
    turned[...] = packed.T
    right, left = turned[pl.ds(0, 16, stride=2), :], turned[pl.ds(1, 16, stride=2), :]
    along_ref[...] = jnp.where(c == 0, right, left)
    back_ref[...] = jnp.where(c == 0, left, right)
    lowest_ref[0] = p_ref[0]
    for copy in copies:
        copy.wait()


def early(p_ref, f_ref, s_ref, out_ref):
    out_ref[...] = p_ref[0, pl.ds(0, 8), :] + f_ref[0, pl.ds(0, 8), :] + s_ref[0, pl.ds(0, 8), :]


def norm_of(position, extent):
    def missing(k):
        k = jnp.maximum(k, 0)
        return (k * (k + 1)) >> 1

    return ((RADIUS + 1) ** 2 - missing(RADIUS - position) - missing(RADIUS - (extent - 1 - position))).astype(F32)


def terms(total, density, sens, p39):
    total = jnp.maximum(total, 1e-30)
    offset = PENALTY * math.log(2.0) / EXPONENT
    smax = jnp.exp(jnp.log(total) * (1.0 / EXPONENT) - offset)
    gap = density - smax
    half = 0.5 * gap * lax.rsqrt(gap * gap + SMOOTH)
    low = 0.5 - half
    top = (0.5 + half) * (2.0 * PENALTY / EXPONENT) * smax
    h = top / total
    return h * sens, h * p39, low, total / top


def plane_norms(sizes):
    row0 = lax.axis_index("gy") * 128
    col0 = lax.axis_index("gx") * 128
    rows = lax.broadcasted_iota(jnp.int32, (128, 128), 0) + row0
    cols = lax.broadcasted_iota(jnp.int32, (128, 128), 1) + col0
    return norm_of(rows, sizes[1] * 128) * norm_of(cols, sizes[2] * 128)


def neighbours(p, layer, inner_ref, outer_ref, beside, powers):
    c = core()
    lane = lanes(128)
    own = power40(p)
    powers[pl.ds(8, 128), :] = own
    y = lax.axis_index("gy")
    there = one_if((y == 1) | (y == 2))
    powers[pl.ds(7 + 129 * (1 - c), 1), :] = power40(inner_ref[pl.ds(layer, 1), :])
    powers[pl.ds(7 + 129 * c, 1), :] = power40(outer_ref[pl.ds(layer, 1), :]) * there
    side = pltpu.roll(beside, (128 - (2 * layer + 1)) % 128, 1)
    right = jnp.where(lane == 127, side, pltpu.roll(own, 127, 1))
    left = jnp.where(lane == 0, side, pltpu.roll(own, 1, 1))
    return (own + right) + left + (powers[pl.ds(7, 128), :] + powers[pl.ds(9, 128), :])


def columns_beside(along_ref, back_ref, turned):
    x = lax.axis_index("gx")
    turned[...] = jnp.zeros((128, 128), F32)
    first = core() == 0
    right = jnp.where(first, back_ref[...], along_ref[...])
    left = jnp.where(first, along_ref[...], back_ref[...])
    turned[pl.ds(0, 16, stride=2), :] = right * one_if(x < lax.axis_size("gx") - 1)
    turned[pl.ds(1, 16, stride=2), :] = left * one_if(x > 0)
    return power40(turned[...].T)


def all_terms(
    sizes, p_ref, f_ref, s_ref, above_ref, inner_ref, outer_ref, along_ref, back_ref, early_ref, uvw_ref, powers, turned
):
    beside = columns_beside(along_ref, back_ref, turned)
    norms = 1.0 / plane_norms(sizes)
    gz = lax.axis_index("gz")
    layer0 = gz * LAYERS
    uvw_ref[0] = s_ref[0]
    uvw_ref[STEPS] = power39(p_ref[0])
    uvw_ref[2 * STEPS] = norms * (1.0 / norm_of(0 * layer0, sizes[0] * LAYERS))
    for layer in range(1, STEPS):
        total = neighbours(p_ref[layer - 1], layer - 1, inner_ref, outer_ref, beside, powers)
        if layer < LAYERS:
            p, f, s = p_ref[layer], f_ref[layer], s_ref[layer]
        else:
            p, f, s = above_ref[0], above_ref[1], above_ref[2]
        u, v, low, inverse = terms(total, f, s, power39(p))
        if layer == LAYERS:
            there = one_if(gz < sizes[0] - 1)
            u, v = u * there, v * there
        norm_z = norm_of(layer0 + layer, sizes[0] * LAYERS)
        uvw_ref[layer] = u
        uvw_ref[STEPS + layer] = v
        uvw_ref[2 * STEPS + layer] = low * inverse * (norms * (1.0 / norm_z))


def plane_of(uvw_ref, name, layer):
    return uvw_ref.at[STEPS * "uvw".index(name) + layer]


def pack_rows(uvw_ref, rows_ref):
    c = core()
    for (name, layer), (at, rows) in ROW_PLACES.items():
        start = aligned(c * (128 - rows), 8)
        rows_ref[pl.ds(at, rows), :] = plane_of(uvw_ref, name, layer)[pl.ds(start, rows), :]


def pack(uvw_ref, same_ref, cross_ref, keep_ref, give_ref):
    c = core()

    def put(at, left, right):
        count = left.shape[0]
        same_ref[pl.ds(at, count), :] = jnp.where(c == 0, right, left)
        cross_ref[pl.ds(at, count), :] = jnp.where(c == 0, left, right)

    def put_corner(slab, left, right):
        at, rows = CORNERS[slab]
        first, last = slice(0, rows), slice(left.shape[0] - rows, left.shape[0])
        keep_ref[pl.ds(at, rows), :] = jnp.where(c == 0, left[first], right[last])
        give_ref[pl.ds(at, rows), :] = jnp.where(c == 0, right[first], left[last])

    lane = lanes(128)
    for slab in range(4):
        left = right = jnp.zeros((128, 128), F32)
        for name, layer, where, at in strips():
            if where == slab:
                width = width_of(layer)
                plane = plane_of(uvw_ref, name, layer)[...]
                inside = (lane >= at) & (lane < at + width)
                left = jnp.where(inside, pltpu.roll(plane, at, 1) if at else plane, left)
                right = jnp.where(inside, pltpu.roll(plane, (at + width) % 128, 1), right)
        if slab < 3:
            put(128 * slab, left, right)
            put_corner(slab, left, right)
            continue
        put_corner(slab, left, right)
        folded = []
        for value in (left, right):
            total = value[:FOLDED]
            for i in range(1, 4):
                total = total + pltpu.roll(value[FOLDED * i:FOLDED * (i + 1)], FOLDED * i, 1)
            folded.append(total)
        put(384, *folded)
    lane = lanes(64)
    left = right = jnp.zeros((64, 128), F32)
    for layer in range(1, STEPS):
        ref = plane_of(uvw_ref, "w", layer)
        for half in range(2):
            plane = ref[pl.ds(64 * half, 64), :]
            at = 64 * half + RADIUS * (layer - 1)
            inside = (lane >= at) & (lane < at + RADIUS)
            left = jnp.where(inside, pltpu.roll(plane, at, 1) if at else plane, left)
            right = jnp.where(inside, pltpu.roll(plane, (at + RADIUS) % 128, 1), right)
    put(384 + FOLDED, left, right)
    put_corner(4, left, right)


def pick_corner(keep_ref, got_ref, corner_ref):
    corner_ref[...] = jnp.where((core() ^ seam()) == 1, keep_ref[...], got_ref[...])


def slab_plane(plain, same, cross, corner):
    c = core()
    inside = one_if(jnp.logical_not(outside()))
    plain[pl.ds(256, 32), :] = jnp.zeros((32, 128), F32)
    plain[pl.ds(aligned(c * 128, 128), 128), :] = same * inside
    plain[pl.ds(aligned((1 - c) * 128, 128), 128), :] = cross * inside
    rows = corner.shape[0]
    plain[pl.ds(aligned(256 + seam() * (32 - rows), 8), rows), :] = corner * inside


def full_plane(plain, name, layer, uvw_ref, other_ref, got_ref, shared_ref):
    c = core()
    plain[pl.ds(aligned(c * 128, 128), 128), :] = plane_of(uvw_ref, name, layer)[...]
    plain[pl.ds(aligned((1 - c) * 128, 128), 128), :] = plane_of(other_ref, name, layer)[...]
    plain[pl.ds(256, 32), :] = jnp.zeros((32, 128), F32)
    start, rows = ROW_PLACES[name, layer]
    here = pl.ds(start, rows)
    to = aligned(256 + seam() * (32 - rows), 8)
    plain[pl.ds(to, rows), :] = jnp.where((c ^ seam()) == 1, got_ref[here, :], shared_ref[here, :])
    return plain_to_plane(plain)


def with_columns(base, columns, at, width):
    c = core()
    lane = lanes(PLANE)
    columns = pltpu.roll(columns, (128 - at - (1 - c) * width) & 127, 1)
    begin = (1 - c) * (128 - width)
    return jnp.where((lane >= begin) & (lane < begin + width), columns, base)


def assemble(
    uvw_ref, other_ref, got_ref, shared_ref, same_ref, cross_ref, corner_ref, uv_ref, plain, slabs
):
    c = core()
    for slab in range(4):
        if slab < 3:
            here = pl.ds(128 * slab, 128)
            same, cross = same_ref[here, :], cross_ref[here, :]
            here = pl.ds(*CORNERS[slab])
        else:
            here = pl.ds(384, FOLDED)
            same, cross = (
                jnp.concatenate([value] + [pltpu.roll(value, 128 - FOLDED * i, 1) for i in range(1, 4)], axis=0)
                for value in (same_ref[here, :], cross_ref[here, :])
            )
            here = pl.ds(*CORNERS[3])
        corner = corner_ref[here, :]
        slot = plain.at[slab % 2]
        slab_plane(slot, same, cross, corner)
        slabs[slab] = plain_to_plane(slot)
    for place, (name, layer, slab, at) in enumerate(strips()):
        base = full_plane(plain.at[place % 2], name, layer, uvw_ref, other_ref, got_ref, shared_ref)
        uv_ref[2 * (LAYERS - layer) + (name == "v")] = with_columns(base, slabs[slab], at, width_of(layer))


def assemble_w(
    uvw_ref, other_ref, got_ref, shared_ref, same_ref, cross_ref, corner_ref, w_ref, plain, slabs
):
    c = core()

    def unfolded(ref):
        value = ref[pl.ds(384 + FOLDED, 64), :]
        return jnp.concatenate([value, pltpu.roll(value, 64, 1)], axis=0)

    here = pl.ds(*CORNERS[4])
    corner = corner_ref[here, :]
    corner = pltpu.roll(corner, 64 * seam(), 1)
    slab_plane(plain.at[0], unfolded(same_ref), unfolded(cross_ref), corner)
    slabs[0] = plain_to_plane(plain.at[0])
    for layer in range(1, STEPS):
        base = full_plane(plain.at[layer % 2], "w", layer, uvw_ref, other_ref, got_ref, shared_ref)
        w_ref[layer] = with_columns(base, slabs[0], RADIUS * (layer - 1), RADIUS)
    row = lax.broadcasted_iota(jnp.int32, (PLANE, 128), 0)
    col = lax.broadcasted_iota(jnp.int32, (PLANE, 128), 1)
    a = seam()
    row = jnp.where((a == 1) & (row >= 256), row - PLANE, row) + 256 * a
    width = jnp.where(c == 0, 108, 20)
    col = jnp.where((c == 0) & (col >= width), col - 128, jnp.where((c == 1) & (col < width), col + 128, col))
    col = col + 128 * lax.axis_index("gx")
    rows, cols = 128 * lax.axis_size("gy"), 128 * lax.axis_size("gx")
    norm = norm_of(row, rows) * norm_of(col, cols) * norm_of(0 * a, LAYERS * lax.axis_size("gz"))
    inside = (row >= 0) & (row < rows) & (col >= 0) & (col < cols)
    plain[0] = jnp.where(inside, 1.0 / jnp.where(inside, norm, 1.0), 0.0)
    w_ref[0] = plain_to_plane(plain.at[0])


def step_down(values, u_ref, v_ref, out_ref):
    new = []
    for t, value in enumerate(values):
        before = values[t - 1] if t > 0 else pltpu.roll(values[-1], 1, 0)
        behind = values[t + 1] if t < VECTORS - 1 else pltpu.roll(values[0], 7, 0)
        total = (value + before) + (behind + pltpu.roll(value, 1, 1)) + pltpu.roll(value, 127, 1)
        here = pl.ds(8 * t, 8)
        new.append(u_ref[here, :] + v_ref[here, :] * total)
        out_ref[here, :] = new[-1]
    return new


def set_carry(carry, main_ref, outer_ref, halo_ref, halo_outer_ref):
    c = core()
    lane = lanes(64)
    mine = (lane >> 6) == c
    inside = one_if(jnp.logical_not(outside()))
    begin = (1 - c) * (128 - REACH)
    beyond = (lane >= begin) & (lane < begin + REACH)
    for i in range(4):
        if main_ref.shape[0] == 256:
            value = main_ref[pl.ds(64 * i, 64), :]
        else:
            value = main_ref[pl.ds(64 * (i % 2), 64), :]
            if i >= 2:
                value = pltpu.roll(value, 64, 1)
            inner = pltpu.roll(main_ref[pl.ds(128, 64), :], (32 * (2 - c) - 32 * i) & 127, 1)
            value = jnp.where(mine, value, inner)
        outer = pltpu.roll(outer_ref[...], (128 - 32 * i) % 128, 1) if i else outer_ref[...]
        carry[pl.ds(64 * i, 64), :] = jnp.where(beyond, outer * inside, value)
    lane = lanes(24)
    beyond = (lane >= begin) & (lane < begin + REACH)
    carry[pl.ds(256, 32), :] = jnp.zeros((32, 128), F32)
    carry[pl.ds(aligned(256 + 8 * seam(), 8), 24), :] = jnp.where(beyond, halo_outer_ref[...] * inside, halo_ref[...])


def merge(give_ref, got_ref, down_ref, halo_ref):
    mine = (lanes(128) >> 6) == core()
    rows = pl.ds(0, 128)
    own, other = give_ref[rows, :], got_ref[rows, :]
    down_ref[rows, :] = jnp.where(mine, own, other)
    down_ref[pl.ds(128, 128), :] = pltpu.roll(jnp.where(mine, other, own), 64, 1)
    rows = pl.ds(128, 24)
    halo_ref[...] = jnp.where(mine[:24], give_ref[rows, :], got_ref[rows, :])


def load_carry(pieces, carry):
    set_carry(carry, *pieces)
    return [carry[pl.ds(t, 8, stride=VECTORS), :] for t in range(VECTORS)]


def run_down(values, uv_ref, layers_ref, first, last, base=0):
    for layer in range(first, last - 1, -1):
        at = 2 * (LAYERS - layer)
        values = step_down(values, uv_ref.at[at], uv_ref.at[at + 1], layers_ref.at[layer - base])
    return values


def section(active, shared, *refs):
    uv_ref, refs = refs[0], refs[1:]
    pieces, before_ref = (), None
    if len(refs) > 5:
        pieces, before_ref, refs = refs[:4], refs[4], refs[5:]
    layers_ref, down_ref, outer_ref, strip_ref, carry = refs

    @pl.when(lax.axis_index("gz") == active)
    def _():
        values = load_carry(pieces, carry) if pieces else [jnp.zeros((8, 128), F32)] * VECTORS
        values = run_down(values, uv_ref, layers_ref, LAYERS, 1)
        layers_ref[0] = layers_ref[1]
        for t in range(VECTORS):
            carry[pl.ds(t, 8, stride=VECTORS), :] = values[t]
        c = core()
        mine = (lanes(128) >> 6) == c
        down_ref[pl.ds(0, 128), :] = jnp.where(
            mine, carry[pl.ds(0, 128), :], pltpu.roll(carry[pl.ds(128, 128), :], 64, 1)
        )
        lane = lanes(64)
        slab = inner = jnp.zeros((64, 128), F32)
        for i in range(4):
            block = carry[pl.ds(64 * i, 64), :]
            rolled = pltpu.roll(block, 32 * i, 1) if i else block
            begin = (32 * i + 128 - c * 32) & 127
            slab = jnp.where(((lane - begin) & 127) < 32, rolled, slab)
            if not shared:
                inner = jnp.where((lane >> 5) == i, pltpu.roll(block, (32 * i - 32 * (2 - c)) & 127, 1), inner)
        outer_ref[...] = slab
        strip = carry[pl.ds(aligned((1 - seam()) * 232, 8), 24), :]
        strip_ref[...] = strip
        if shared:
            down_ref[pl.ds(128, 24), :] = strip
        else:
            down_ref[pl.ds(128, 64), :] = inner

    if before_ref is not None:
        @pl.when(lax.axis_index("gz") != active)
        def _():
            layers_ref[...] = before_ref[...]


def section_top(uv_ref, main_ref, outer_ref, halo_ref, halo_outer_ref, before_ref, top_ref, carry):
    @pl.when(lax.axis_index("gz") == 0)
    def _():
        values = load_carry((main_ref, outer_ref, halo_ref, halo_outer_ref), carry)
        run_down(values, uv_ref, top_ref, LAYERS, LOW, LOW)

    @pl.when(lax.axis_index("gz") != 0)
    def _():
        top_ref[...] = before_ref[pl.ds(LOW, STEPS - LOW)]


def section_rest(uv_ref, top_ref, before_ref, layers_ref):
    @pl.when(lax.axis_index("gz") == 0)
    def _():
        values = [top_ref[0, pl.ds(8 * t, 8), :] for t in range(VECTORS)]
        run_down(values, uv_ref, layers_ref, LOW - 1, 0)

    @pl.when(lax.axis_index("gz") != 0)
    def _():
        layers_ref[...] = before_ref[pl.ds(0, LOW)]


def box(values):
    two = [values[i] + values[i + 1] for i in range(len(values) - 1)]
    four = [two[i] + two[i + 2] for i in range(len(two) - 2)]
    return [four[i] + values[i + 4] for i in range(len(values) - 4)]


def smooth(layers, kept_ref, plains, others, tent):
    c = core()
    row = lax.broadcasted_iota(jnp.int32, (256, 128), 0)
    col = lax.broadcasted_iota(jnp.int32, (256, 128), 1)
    distance = (row - col + RADIUS) & 127
    weight = jnp.where(distance <= 2 * RADIUS, RADIUS + 1 - jnp.abs(distance - RADIUS), 0)
    tent[...] = weight.astype(F32).astype(jnp.bfloat16)
    for k, (layer_ref, w_ref) in enumerate(layers):
        plain = plains.at[k % 4]
        values = [layer_ref[pl.ds(8 * t, 8), :] * w_ref[pl.ds(8 * t, 8), :] for t in range(VECTORS)]
        first = [pltpu.roll(value, 1, 0) for value in values[VECTORS - RADIUS:]]
        last = [pltpu.roll(value, 7, 0) for value in values[:RADIUS]]
        total = jnp.concatenate(box(box(first + values + last)), axis=0)
        high = total.astype(jnp.bfloat16)
        rest = total - high.astype(F32)
        middle = rest.astype(jnp.bfloat16)
        small = (rest - middle.astype(F32)).astype(jnp.bfloat16)
        value = jnp.dot(jnp.concatenate([high, middle], axis=1), tent[...], preferred_element_type=F32)
        value = value + jnp.dot(small, tent[pl.ds(0, 128), :], preferred_element_type=F32)
        plane_to_plain(value, plain)
        kept_ref[k] = plain[pl.ds(aligned(c * 128, 128), 128), :]
        others[k] = plain[pl.ds(aligned((1 - c) * 128, 128), 128), :]


def pair_up(others, first, count, give_ref):
    mine = (lanes(128) >> 6) == core()
    for k in range(count):
        give_ref[k] = jnp.where(mine, others[first + k], pltpu.roll(others[first + count + k], 64, 1))


def smooth_first(top_ref, before_ref, w_ref, kept_ref, give_ref, plains, others, tent):
    layers = [(top_ref.at[k], w_ref.at[LOW + k]) for k in range(STEPS - LOW)]
    layers += [(before_ref.at[k], w_ref.at[k]) for k in range(1, RADIUS)]
    smooth(layers, kept_ref, plains, others, tent)
    pair_up(others, 0, 4, give_ref)


def smooth_rest(layers_ref, w_ref, kept_ref, give_ref, give_more_ref, plains, others, tent):
    smooth([(layers_ref.at[k], w_ref.at[k]) for k in range(LOW)], kept_ref, plains, others, tent)
    pair_up(others, 0, 3, give_ref)
    pair_up(others, 6, 3, give_more_ref)


def whole(kept, got, second):
    mine = (lanes(128) >> 6) == core()
    return jnp.where(mine, kept, pltpu.roll(got, 64, 1) if second else got)


def ends(kept_ref, got_ref, top_ref, bottom_ref):
    for k in range(8):
        value = whole(kept_ref[k], got_ref[k % 4], k >= 4)
        if k < STEPS - LOW:
            top_ref[k] = value
        else:
            bottom_ref[k - (STEPS - LOW)] = value


def finish(kept_ref, got_ref, got_more_ref, top_ref, below_ref, above_ref, passive_ref, out_ref, tile):
    gz = lax.axis_index("gz")
    for k in range(LOW):
        got = got_ref if k < 6 else got_more_ref
        tile[k] = whole(kept_ref[k], got[k % 3], k % 6 >= 3)

    def layer(k):
        if k < 0:
            return jnp.where(gz > 0, below_ref[k + RADIUS], 0.0)
        if k == 0:
            return jnp.where(gz == 0, tile[0], below_ref[RADIUS])
        if k > LAYERS:
            return jnp.where(gz < lax.axis_size("gz") - 1, above_ref[k - STEPS], 0.0)
        return tile[k] if k < LOW else top_ref[k - LOW]

    for k in range(LAYERS):
        total = layer(k) * 5.0
        for offset in range(1, RADIUS + 1):
            total = total + (layer(k - offset) + layer(k + offset)) * (5.0 - offset)
        out_ref[k] = jnp.where(passive_ref[k] > 0, 0.0, total)


def to_other(value):
    return moved(value, lambda z, y, x: (z, y ^ 1, x))


def after(value, *others):
    return lax.optimization_barrier((value,) + others)[0]


def per_device(filtered, printed, sensitivity, passive):
    sizes = tuple(lax.axis_size(axis) for axis in AXES)
    depth = sizes[0]
    plane = shape(128, 128)
    edge = shape(16, 128)

    def across(z, y, x):
        return (z, y ^ 3, x) if y in (1, 2) else None

    def on_grid(x):
        return 0 <= x < sizes[2]

    def beside(z, y, x):
        to = x + (1 if y & 1 else -1)
        return (z, y ^ 1, to) if on_grid(to) else (z, y ^ 2, x)

    def same(z, y, x):
        to = x + (-1 if y & 1 else 1)
        return (z, y, to) if on_grid(to) else (z, y ^ 1, x)

    def opposite(z, y, x):
        to = x + (1 if y & 1 else -1)
        return (z, y, to) if on_grid(to) else (z, y ^ 1, x)

    def across_beside(z, y, x):
        to = x + (1 if y & 1 else -1)
        return (z, 3 - y, to) if on_grid(to) else (z, y ^ 2, x)

    hbm = pl.BlockSpec(memory_space=pltpu.HBM)
    lowest_planes, inner, outer, along, back = call(
        edges, [shape(3, 128, 128)] + [edge] * 4, printed, filtered, sensitivity,
        in_specs=[hbm] * 3,
        scratch=[pltpu.VMEM((128, 128), F32), pltpu.VMEM((LAYERS, 128, 128), F32), pltpu.SemaphoreType.DMA((6,))],
    )
    above = moved(lowest_planes, lambda z, y, x: (z - 1, y, x))
    along, back = moved(along, same), moved(back, opposite)
    outer = moved(outer, lambda z, y, x: (z, y ^ 3, x))
    inner = to_other(inner)
    ready = call(early, shape(8, 128), printed, filtered, after(sensitivity, inner))
    uvw = call(
        functools.partial(all_terms, sizes), shape(3 * STEPS, 128, 128),
        printed, filtered, sensitivity, above, inner, outer, along, back, ready,
        scratch=[
            pltpu.VMEM((144, 128), F32), pltpu.VMEM((128, 128), F32),
        ],
    )
    slab, corner = shape(SLAB_ROWS, 128), shape(CORNER_ROWS, 128)
    rows = call(pack_rows, shape(ROW_TOTAL, 128), uvw)
    got = moved(rows, across)
    to_same, to_cross, keep, give = call(pack, [slab, slab, corner, corner], after(uvw, rows))
    from_same = moved(to_same, same)
    from_cross = moved(to_cross, beside)
    corner = call(pick_corner, corner, keep, to_other(give))
    corner = moved(corner, across_beside)
    other = to_other(uvw)
    shared = to_other(after(got, from_same, from_cross, corner))
    parts = (uvw, other, got, shared, from_same, from_cross, corner)
    stack = shape(STEPS, PLANE, 128)
    work = [pltpu.VMEM((2, PLANE, 128), F32), pltpu.VMEM((4, PLANE, 128), F32)]
    uvs = call(assemble, shape(2 * STEPS, PLANE, 128), *parts, scratch=work)
    ws = None
    pieces, before = (), ()
    whole_stack = [pltpu.VMEM((PLANE, 128), F32)]
    for active in range(depth - 1, 0, -1):
        swap = (depth - 1 - active) % 2 == 1
        layers, main, side, strip = call(
            functools.partial(section, active, swap),
            [stack, shape(152 if swap else 192, 128), shape(64, 128), shape(24, 128)],
            uvs, *pieces, *before, scratch=whole_stack,
        )
        before = (layers,)

        def down(where):
            def to(z, y, x):
                target = where(z, y, x) if z == active else None
                return target and (z - 1,) + target[1:]
            return to

        def over(z, y, x):
            return (z, y ^ 2, x)

        def beyond(z, y, x):
            return beside(z, y, x) if on_grid(x + (1 if y & 1 else -1)) else None

        def corner_of(z, y, x):
            target = beyond(z, y, x)
            return target and (z, target[1] ^ 2, target[2])

        side = moved(side, down(beyond))
        edge_piece = moved(strip, down(corner_of))
        halo = strip
        if swap:
            main, halo = call(merge, [shape(256, 128), shape(24, 128)], main, to_other(main))
        main = moved(main, down(lambda z, y, x: (z, y, x)))
        halo = moved(halo, down(over))
        pieces = (main, side, halo, edge_piece)
        if ws is None:
            ws = call(assemble_w, stack, after(uvw, side), *parts[1:], scratch=work)
    top_layers = call(
        section_top, shape(STEPS - LOW, PLANE, 128), uvs, *pieces, layers, scratch=whole_stack
    )

    def work_for(count):
        return [
            pltpu.VMEM((4, PLANE, 128), F32), pltpu.VMEM((count, 128, 128), F32), pltpu.VMEM((256, 128), jnp.bfloat16)
        ]

    kept, given = call(
        smooth_first, [shape(8, 128, 128), shape(4, 128, 128)], top_layers, layers, ws, scratch=work_for(8)
    )
    top, bottom = call(ends, [shape(RADIUS + 1, 128, 128), shape(RADIUS - 1, 128, 128)], kept, to_other(given))
    below = moved(top, lambda z, y, x: (z + 1, y, x))
    over = moved(bottom, lambda z, y, x: (z - 1, y, x))
    rest = call(section_rest, shape(LOW, PLANE, 128), uvs, after(top_layers, top), layers)
    third = shape(3, 128, 128)
    kept, given, given_more = call(
        smooth_rest, [shape(LOW, 128, 128), third, third], rest, ws, scratch=work_for(LOW)
    )
    return call(
        finish, shape(LAYERS, 128, 128),
        kept, to_other(given), to_other(given_more), top, below, over, passive,
        scratch=[pltpu.VMEM((LOW, 128, 128), F32)],
    )


def solution(mesh):
    spec = P(*AXES)
    return jax.shard_map(
        per_device, mesh=mesh, in_specs=(spec,) * 4, out_specs=spec, check_vma=False
    )
```

```python
import functools
import math

import jax
import jax.numpy as jnp
from jax import lax
from jax.experimental import pallas as pl
from jax.experimental.pallas import tpu as pltpu
from jax.sharding import PartitionSpec as P

RADIUS = 4
PENALTY = 40.0
EXPONENT = PENALTY + math.log(5.0) / math.log(0.5)
SMOOTH = 0.001
AXES = ("gz", "gy", "gx")
F32 = jnp.float32

LAYERS = 16
STEPS = LAYERS + 1
PLANE = 288
VECTORS = PLANE // 8
REACH = RADIUS + STEPS
LOW = LAYERS - RADIUS
SLABS = ((16, 15, 14, 3), (13, 12, 11, 8, 0), (10, 9, 7, 6, 5, 2), (4, 1))
FOLDED = 32
SLAB_ROWS = 3 * 128 + FOLDED + 64
CORNERS = ((0, 24), (24, 24), (48, 16), (64, 8), (72, 8))
CORNER_ROWS = 80


def width_of(layer):
    return RADIUS + layer


def rows_of(layer):
    return -(-width_of(layer) // 8) * 8


MICROSECONDS = {"all_terms": 2.5, "assemble": 2.5, "section": 1.5, "section_rest": 3.0, "smooth_rest": 3.0, "finish": 3.0}
VMEM_LIMIT = {"edges": 52 << 20}


def strips():
    out = []
    for slab, layers in enumerate(SLABS):
        at = 0
        for layer in layers:
            for name in ("u", "v"):
                out.append((name, layer, slab, at))
                at += width_of(layer)
        assert at <= (128 if slab < 3 else FOLDED)
    return out


def row_places():
    places, at = {}, 0
    for layer in range(STEPS):
        for name in ("u", "v", "w"):
            if (name, layer) == ("w", 0):
                continue
            rows = 8 if name == "w" else rows_of(layer)
            places[name, layer] = (at, rows)
            at += rows
    return places, at


ROW_PLACES, ROW_TOTAL = row_places()


def moved(value, where):
    sizes = tuple(lax.axis_size(axis) for axis in AXES)
    pairs = []
    for z in range(sizes[0]):
        for y in range(sizes[1]):
            for x in range(sizes[2]):
                to = where(z, y, x)
                if to is not None:
                    tz, ty, tx = to[0] % sizes[0], to[1], to[2] % sizes[2]
                    pairs.append(((z * sizes[1] + y) * sizes[2] + x, (tz * sizes[1] + ty) * sizes[2] + tx))
    return lax.ppermute(value, AXES, pairs)


def shape(*dims):
    return jax.ShapeDtypeStruct(dims, F32)


def call(kernel, outs, *args, scratch=(), in_specs=None, **more):
    name = kernel.func.__name__ if isinstance(kernel, functools.partial) else kernel.__name__
    if in_specs is not None:
        more["in_specs"] = in_specs
    return pl.pallas_call(
        kernel,
        out_shape=outs,
        scratch_shapes=list(scratch),
        compiler_params=pltpu.CompilerParams(vmem_limit_bytes=VMEM_LIMIT.get(name, 40 << 20)),
        cost_estimate=pl.CostEstimate(flops=0, bytes_accessed=int(MICROSECONDS.get(name, 0.5) * 3e6), transcendentals=0),
        name=name,
        **more,
    )(*args)


def lanes(rows):
    return lax.broadcasted_iota(jnp.int32, (rows, 128), 1)


def core():
    return lax.axis_index("gy") & 1


def seam():
    return lax.axis_index("gy") >> 1


def one_if(condition):
    return jnp.where(condition, 1.0, 0.0)


def outside():
    x, c = lax.axis_index("gx"), core()
    return ((c == 0) & (x == 0)) | ((c == 1) & (x == lax.axis_size("gx") - 1))


def plain_to_plane(ref):
    return jnp.concatenate([ref[pl.ds(t, 8, stride=VECTORS), :] for t in range(VECTORS)], axis=0)


def plane_to_plain(value, ref):
    for t in range(VECTORS):
        ref[pl.ds(t, 8, stride=VECTORS), :] = value[8 * t:8 * t + 8]


def aligned(value, to):
    return pl.multiple_of(value, to)


def power40(p):
    x = p + p
    x2 = x * x
    x4 = x2 * x2
    x8 = x4 * x4
    x32 = x8 * x8
    x32 = x32 * x32
    return x32 * x8


def power39(p):
    x = p + p
    x2 = x * x
    x4 = x2 * x2
    x8 = x4 * x4
    x32 = x8 * x8
    x32 = x32 * x32
    return x32 * (x4 * (x2 * x))


def edges(p_hbm, f_hbm, s_hbm, lowest_ref, inner_ref, outer_ref, along_ref, back_ref, turned, p_ref, sems):
    planes = [pltpu.make_async_copy(p_hbm.at[pl.ds(4 * i, 4)], p_ref.at[pl.ds(4 * i, 4)], sems.at[i]) for i in range(4)]
    copies = [pltpu.make_async_copy(ref.at[0], lowest_ref.at[i + 1], sems.at[4 + i]) for i, ref in enumerate((f_hbm, s_hbm))]
    for copy in planes + copies:
        copy.start()
    lane = lanes(128)
    c = core()
    packed = jnp.zeros((128, 128), F32)
    for layer in range(LAYERS):
        if layer % 4 == 0:
            planes[layer // 4].wait()
        inner_ref[pl.ds(layer, 1), :] = p_ref[layer, pl.ds(127 * (1 - c), 1), :]
        outer_ref[pl.ds(layer, 1), :] = p_ref[layer, pl.ds(127 * c, 1), :]
        rolled = pltpu.roll(p_ref[layer], 2 * layer + 1, 1)
        packed = jnp.where((lane >> 1) == layer, rolled, packed)
    turned[...] = packed.T
    right, left = turned[pl.ds(0, 16, stride=2), :], turned[pl.ds(1, 16, stride=2), :]
    along_ref[...] = jnp.where(c == 0, right, left)
    back_ref[...] = jnp.where(c == 0, left, right)
    lowest_ref[0] = p_ref[0]
    for copy in copies:
        copy.wait()


def early(p_ref, f_ref, s_ref, out_ref):
    out_ref[...] = p_ref[0, pl.ds(0, 8), :] + f_ref[0, pl.ds(0, 8), :] + s_ref[0, pl.ds(0, 8), :]


def norm_of(position, extent):
    def missing(k):
        k = jnp.maximum(k, 0)
        return (k * (k + 1)) >> 1

    return ((RADIUS + 1) ** 2 - missing(RADIUS - position) - missing(RADIUS - (extent - 1 - position))).astype(F32)


def terms(total, density, sens, p39):
    total = jnp.maximum(total, 1e-30)
    offset = PENALTY * math.log(2.0) / EXPONENT
    smax = jnp.exp(jnp.log(total) * (1.0 / EXPONENT) - offset)
    gap = density - smax
    half = 0.5 * gap * lax.rsqrt(gap * gap + SMOOTH)
    low = 0.5 - half
    top = (0.5 + half) * (2.0 * PENALTY / EXPONENT) * smax
    h = top / total
    return h * sens, h * p39, low, total / top


def plane_norms(sizes):
    row0 = lax.axis_index("gy") * 128
    col0 = lax.axis_index("gx") * 128
    rows = lax.broadcasted_iota(jnp.int32, (128, 128), 0) + row0
    cols = lax.broadcasted_iota(jnp.int32, (128, 128), 1) + col0
    return norm_of(rows, sizes[1] * 128) * norm_of(cols, sizes[2] * 128)


def neighbours(p, layer, inner_ref, outer_ref, beside, powers):
    c = core()
    lane = lanes(128)
    own = power40(p)
    powers[pl.ds(8, 128), :] = own
    y = lax.axis_index("gy")
    there = one_if((y == 1) | (y == 2))
    powers[pl.ds(7 + 129 * (1 - c), 1), :] = power40(inner_ref[pl.ds(layer, 1), :])
    powers[pl.ds(7 + 129 * c, 1), :] = power40(outer_ref[pl.ds(layer, 1), :]) * there
    side = pltpu.roll(beside, (128 - (2 * layer + 1)) % 128, 1)
    right = jnp.where(lane == 127, side, pltpu.roll(own, 127, 1))
    left = jnp.where(lane == 0, side, pltpu.roll(own, 1, 1))
    return (own + right) + left + (powers[pl.ds(7, 128), :] + powers[pl.ds(9, 128), :])


def columns_beside(along_ref, back_ref, turned):
    x = lax.axis_index("gx")
    turned[...] = jnp.zeros((128, 128), F32)
    first = core() == 0
    right = jnp.where(first, back_ref[...], along_ref[...])
    left = jnp.where(first, along_ref[...], back_ref[...])
    turned[pl.ds(0, 16, stride=2), :] = right * one_if(x < lax.axis_size("gx") - 1)
    turned[pl.ds(1, 16, stride=2), :] = left * one_if(x > 0)
    return power40(turned[...].T)


def all_terms(
    sizes, p_ref, f_ref, s_ref, above_ref, inner_ref, outer_ref, along_ref, back_ref, early_ref, uvw_ref, powers, turned
):
    beside = columns_beside(along_ref, back_ref, turned)
    norms = 1.0 / plane_norms(sizes)
    gz = lax.axis_index("gz")
    layer0 = gz * LAYERS
    uvw_ref[0] = s_ref[0]
    uvw_ref[STEPS] = power39(p_ref[0])
    uvw_ref[2 * STEPS] = norms * (1.0 / norm_of(0 * layer0, sizes[0] * LAYERS))
    for layer in range(1, STEPS):
        total = neighbours(p_ref[layer - 1], layer - 1, inner_ref, outer_ref, beside, powers)
        if layer < LAYERS:
            p, f, s = p_ref[layer], f_ref[layer], s_ref[layer]
        else:
            p, f, s = above_ref[0], above_ref[1], above_ref[2]
        u, v, low, inverse = terms(total, f, s, power39(p))
        if layer == LAYERS:
            there = one_if(gz < sizes[0] - 1)
            u, v = u * there, v * there
        norm_z = norm_of(layer0 + layer, sizes[0] * LAYERS)
        uvw_ref[layer] = u
        uvw_ref[STEPS + layer] = v
        uvw_ref[2 * STEPS + layer] = low * inverse * (norms * (1.0 / norm_z))


def plane_of(uvw_ref, name, layer):
    return uvw_ref.at[STEPS * "uvw".index(name) + layer]


def pack_rows(uvw_ref, rows_ref):
    c = core()
    for (name, layer), (at, rows) in ROW_PLACES.items():
        start = aligned(c * (128 - rows), 8)
        rows_ref[pl.ds(at, rows), :] = plane_of(uvw_ref, name, layer)[pl.ds(start, rows), :]


def pack(uvw_ref, same_ref, cross_ref, keep_ref, give_ref):
    c = core()

    def put(at, left, right):
        count = left.shape[0]
        same_ref[pl.ds(at, count), :] = jnp.where(c == 0, right, left)
        cross_ref[pl.ds(at, count), :] = jnp.where(c == 0, left, right)

    def put_corner(slab, left, right):
        at, rows = CORNERS[slab]
        first, last = slice(0, rows), slice(left.shape[0] - rows, left.shape[0])
        keep_ref[pl.ds(at, rows), :] = jnp.where(c == 0, left[first], right[last])
        give_ref[pl.ds(at, rows), :] = jnp.where(c == 0, right[first], left[last])

    lane = lanes(128)
    for slab in range(4):
        left = right = jnp.zeros((128, 128), F32)
        for name, layer, where, at in strips():
            if where == slab:
                width = width_of(layer)
                plane = plane_of(uvw_ref, name, layer)[...]
                inside = (lane >= at) & (lane < at + width)
                left = jnp.where(inside, pltpu.roll(plane, at, 1) if at else plane, left)
                right = jnp.where(inside, pltpu.roll(plane, (at + width) % 128, 1), right)
        if slab < 3:
            put(128 * slab, left, right)
            put_corner(slab, left, right)
            continue
        put_corner(slab, left, right)
        folded = []
        for value in (left, right):
            total = value[:FOLDED]
            for i in range(1, 4):
                total = total + pltpu.roll(value[FOLDED * i:FOLDED * (i + 1)], FOLDED * i, 1)
            folded.append(total)
        put(384, *folded)
    lane = lanes(64)
    left = right = jnp.zeros((64, 128), F32)
    for layer in range(1, STEPS):
        ref = plane_of(uvw_ref, "w", layer)
        for half in range(2):
            plane = ref[pl.ds(64 * half, 64), :]
            at = 64 * half + RADIUS * (layer - 1)
            inside = (lane >= at) & (lane < at + RADIUS)
            left = jnp.where(inside, pltpu.roll(plane, at, 1) if at else plane, left)
            right = jnp.where(inside, pltpu.roll(plane, (at + RADIUS) % 128, 1), right)
    put(384 + FOLDED, left, right)
    put_corner(4, left, right)


def pick_corner(keep_ref, got_ref, corner_ref):
    corner_ref[...] = jnp.where((core() ^ seam()) == 1, keep_ref[...], got_ref[...])


def slab_plane(plain, same, cross, corner):
    c = core()
    inside = one_if(jnp.logical_not(outside()))
    plain[pl.ds(256, 32), :] = jnp.zeros((32, 128), F32)
    plain[pl.ds(aligned(c * 128, 128), 128), :] = same * inside
    plain[pl.ds(aligned((1 - c) * 128, 128), 128), :] = cross * inside
    rows = corner.shape[0]
    plain[pl.ds(aligned(256 + seam() * (32 - rows), 8), rows), :] = corner * inside


def full_plane(plain, name, layer, uvw_ref, other_ref, got_ref, shared_ref):
    c = core()
    plain[pl.ds(aligned(c * 128, 128), 128), :] = plane_of(uvw_ref, name, layer)[...]
    plain[pl.ds(aligned((1 - c) * 128, 128), 128), :] = plane_of(other_ref, name, layer)[...]
    plain[pl.ds(256, 32), :] = jnp.zeros((32, 128), F32)
    start, rows = ROW_PLACES[name, layer]
    here = pl.ds(start, rows)
    to = aligned(256 + seam() * (32 - rows), 8)
    plain[pl.ds(to, rows), :] = jnp.where((c ^ seam()) == 1, got_ref[here, :], shared_ref[here, :])
    return plain_to_plane(plain)


def with_columns(base, columns, at, width):
    c = core()
    lane = lanes(PLANE)
    columns = pltpu.roll(columns, (128 - at - (1 - c) * width) & 127, 1)
    begin = (1 - c) * (128 - width)
    return jnp.where((lane >= begin) & (lane < begin + width), columns, base)


def assemble(
    uvw_ref, other_ref, got_ref, shared_ref, same_ref, cross_ref, corner_ref, uv_ref, plain, slabs
):
    c = core()
    for slab in range(4):
        if slab < 3:
            here = pl.ds(128 * slab, 128)
            same, cross = same_ref[here, :], cross_ref[here, :]
            here = pl.ds(*CORNERS[slab])
        else:
            here = pl.ds(384, FOLDED)
            same, cross = (
                jnp.concatenate([value] + [pltpu.roll(value, 128 - FOLDED * i, 1) for i in range(1, 4)], axis=0)
                for value in (same_ref[here, :], cross_ref[here, :])
            )
            here = pl.ds(*CORNERS[3])
        corner = corner_ref[here, :]
        slot = plain.at[slab % 2]
        slab_plane(slot, same, cross, corner)
        slabs[slab] = plain_to_plane(slot)
    for place, (name, layer, slab, at) in enumerate(strips()):
        base = full_plane(plain.at[place % 2], name, layer, uvw_ref, other_ref, got_ref, shared_ref)
        uv_ref[2 * (LAYERS - layer) + (name == "v")] = with_columns(base, slabs[slab], at, width_of(layer))


def assemble_w(
    uvw_ref, other_ref, got_ref, shared_ref, same_ref, cross_ref, corner_ref, w_ref, plain, slabs
):
    c = core()

    def unfolded(ref):
        value = ref[pl.ds(384 + FOLDED, 64), :]
        return jnp.concatenate([value, pltpu.roll(value, 64, 1)], axis=0)

    here = pl.ds(*CORNERS[4])
    corner = corner_ref[here, :]
    corner = pltpu.roll(corner, 64 * seam(), 1)
    slab_plane(plain.at[0], unfolded(same_ref), unfolded(cross_ref), corner)
    slabs[0] = plain_to_plane(plain.at[0])
    for layer in range(1, STEPS):
        base = full_plane(plain.at[layer % 2], "w", layer, uvw_ref, other_ref, got_ref, shared_ref)
        w_ref[layer] = with_columns(base, slabs[0], RADIUS * (layer - 1), RADIUS)
    row = lax.broadcasted_iota(jnp.int32, (PLANE, 128), 0)
    col = lax.broadcasted_iota(jnp.int32, (PLANE, 128), 1)
    a = seam()
    row = jnp.where((a == 1) & (row >= 256), row - PLANE, row) + 256 * a
    width = jnp.where(c == 0, 108, 20)
    col = jnp.where((c == 0) & (col >= width), col - 128, jnp.where((c == 1) & (col < width), col + 128, col))
    col = col + 128 * lax.axis_index("gx")
    rows, cols = 128 * lax.axis_size("gy"), 128 * lax.axis_size("gx")
    norm = norm_of(row, rows) * norm_of(col, cols) * norm_of(0 * a, LAYERS * lax.axis_size("gz"))
    inside = (row >= 0) & (row < rows) & (col >= 0) & (col < cols)
    plain[0] = jnp.where(inside, 1.0 / jnp.where(inside, norm, 1.0), 0.0)
    w_ref[0] = plain_to_plane(plain.at[0])


def step_down(values, u_ref, v_ref, out_ref):
    new = []
    for t, value in enumerate(values):
        before = values[t - 1] if t > 0 else pltpu.roll(values[-1], 1, 0)
        behind = values[t + 1] if t < VECTORS - 1 else pltpu.roll(values[0], 7, 0)
        total = (value + before) + (behind + pltpu.roll(value, 1, 1)) + pltpu.roll(value, 127, 1)
        here = pl.ds(8 * t, 8)
        new.append(u_ref[here, :] + v_ref[here, :] * total)
        out_ref[here, :] = new[-1]
    return new


def set_carry(carry, main_ref, outer_ref, halo_ref, halo_outer_ref):
    c = core()
    lane = lanes(64)
    mine = (lane >> 6) == c
    inside = one_if(jnp.logical_not(outside()))
    begin = (1 - c) * (128 - REACH)
    beyond = (lane >= begin) & (lane < begin + REACH)
    for i in range(4):
        if main_ref.shape[0] == 256:
            value = main_ref[pl.ds(64 * i, 64), :]
        else:
            value = main_ref[pl.ds(64 * (i % 2), 64), :]
            if i >= 2:
                value = pltpu.roll(value, 64, 1)
            inner = pltpu.roll(main_ref[pl.ds(128, 64), :], (32 * (2 - c) - 32 * i) & 127, 1)
            value = jnp.where(mine, value, inner)
        outer = pltpu.roll(outer_ref[...], (128 - 32 * i) % 128, 1) if i else outer_ref[...]
        carry[pl.ds(64 * i, 64), :] = jnp.where(beyond, outer * inside, value)
    lane = lanes(24)
    beyond = (lane >= begin) & (lane < begin + REACH)
    carry[pl.ds(256, 32), :] = jnp.zeros((32, 128), F32)
    carry[pl.ds(aligned(256 + 8 * seam(), 8), 24), :] = jnp.where(beyond, halo_outer_ref[...] * inside, halo_ref[...])


def merge(give_ref, got_ref, down_ref, halo_ref):
    mine = (lanes(128) >> 6) == core()
    rows = pl.ds(0, 128)
    own, other = give_ref[rows, :], got_ref[rows, :]
    down_ref[rows, :] = jnp.where(mine, own, other)
    down_ref[pl.ds(128, 128), :] = pltpu.roll(jnp.where(mine, other, own), 64, 1)
    rows = pl.ds(128, 24)
    halo_ref[...] = jnp.where(mine[:24], give_ref[rows, :], got_ref[rows, :])


def load_carry(pieces, carry):
    set_carry(carry, *pieces)
    return [carry[pl.ds(t, 8, stride=VECTORS), :] for t in range(VECTORS)]


def run_down(values, uv_ref, layers_ref, first, last, base=0):
    for layer in range(first, last - 1, -1):
        at = 2 * (LAYERS - layer)
        values = step_down(values, uv_ref.at[at], uv_ref.at[at + 1], layers_ref.at[layer - base])
    return values


def section(active, shared, *refs):
    uv_ref, refs = refs[0], refs[1:]
    pieces, before_ref = (), None
    if len(refs) > 5:
        pieces, before_ref, refs = refs[:4], refs[4], refs[5:]
    layers_ref, down_ref, outer_ref, strip_ref, carry = refs

    @pl.when(lax.axis_index("gz") == active)
    def _():
        values = load_carry(pieces, carry) if pieces else [jnp.zeros((8, 128), F32)] * VECTORS
        values = run_down(values, uv_ref, layers_ref, LAYERS, 1)
        layers_ref[0] = layers_ref[1]
        for t in range(VECTORS):
            carry[pl.ds(t, 8, stride=VECTORS), :] = values[t]
        c = core()
        mine = (lanes(128) >> 6) == c
        down_ref[pl.ds(0, 128), :] = jnp.where(
            mine, carry[pl.ds(0, 128), :], pltpu.roll(carry[pl.ds(128, 128), :], 64, 1)
        )
        lane = lanes(64)
        slab = inner = jnp.zeros((64, 128), F32)
        for i in range(4):
            block = carry[pl.ds(64 * i, 64), :]
            rolled = pltpu.roll(block, 32 * i, 1) if i else block
            begin = (32 * i + 128 - c * 32) & 127
            slab = jnp.where(((lane - begin) & 127) < 32, rolled, slab)
            if not shared:
                inner = jnp.where((lane >> 5) == i, pltpu.roll(block, (32 * i - 32 * (2 - c)) & 127, 1), inner)
        outer_ref[...] = slab
        strip = carry[pl.ds(aligned((1 - seam()) * 232, 8), 24), :]
        strip_ref[...] = strip
        if shared:
            down_ref[pl.ds(128, 24), :] = strip
        else:
            down_ref[pl.ds(128, 64), :] = inner

    if before_ref is not None:
        @pl.when(lax.axis_index("gz") != active)
        def _():
            layers_ref[...] = before_ref[...]


def section_top(uv_ref, main_ref, outer_ref, halo_ref, halo_outer_ref, before_ref, top_ref, carry):
    @pl.when(lax.axis_index("gz") == 0)
    def _():
        values = load_carry((main_ref, outer_ref, halo_ref, halo_outer_ref), carry)
        run_down(values, uv_ref, top_ref, LAYERS, LOW, LOW)

    @pl.when(lax.axis_index("gz") != 0)
    def _():
        top_ref[...] = before_ref[pl.ds(LOW, STEPS - LOW)]


def section_rest(uv_ref, top_ref, before_ref, layers_ref):
    @pl.when(lax.axis_index("gz") == 0)
    def _():
        values = [top_ref[0, pl.ds(8 * t, 8), :] for t in range(VECTORS)]
        run_down(values, uv_ref, layers_ref, LOW - 1, 0)

    @pl.when(lax.axis_index("gz") != 0)
    def _():
        layers_ref[...] = before_ref[pl.ds(0, LOW)]


def box(values):
    two = [values[i] + values[i + 1] for i in range(len(values) - 1)]
    four = [two[i] + two[i + 2] for i in range(len(two) - 2)]
    return [four[i] + values[i + 4] for i in range(len(values) - 4)]


def smooth(layers, kept_ref, plains, others, tent):
    c = core()
    row = lax.broadcasted_iota(jnp.int32, (256, 128), 0)
    col = lax.broadcasted_iota(jnp.int32, (256, 128), 1)
    distance = (row - col + RADIUS) & 127
    weight = jnp.where(distance <= 2 * RADIUS, RADIUS + 1 - jnp.abs(distance - RADIUS), 0)
    tent[...] = weight.astype(F32).astype(jnp.bfloat16)
    for k, (layer_ref, w_ref) in enumerate(layers):
        plain = plains.at[k % 4]
        values = [layer_ref[pl.ds(8 * t, 8), :] * w_ref[pl.ds(8 * t, 8), :] for t in range(VECTORS)]
        first = [pltpu.roll(value, 1, 0) for value in values[VECTORS - RADIUS:]]
        last = [pltpu.roll(value, 7, 0) for value in values[:RADIUS]]
        total = jnp.concatenate(box(box(first + values + last)), axis=0)
        high = total.astype(jnp.bfloat16)
        rest = total - high.astype(F32)
        middle = rest.astype(jnp.bfloat16)
        small = (rest - middle.astype(F32)).astype(jnp.bfloat16)
        value = jnp.dot(jnp.concatenate([high, middle], axis=1), tent[...], preferred_element_type=F32)
        value = value + jnp.dot(small, tent[pl.ds(0, 128), :], preferred_element_type=F32)
        plane_to_plain(value, plain)
        kept_ref[k] = plain[pl.ds(aligned(c * 128, 128), 128), :]
        others[k] = plain[pl.ds(aligned((1 - c) * 128, 128), 128), :]


def pair_up(others, first, count, give_ref):
    mine = (lanes(128) >> 6) == core()
    for k in range(count):
        give_ref[k] = jnp.where(mine, others[first + k], pltpu.roll(others[first + count + k], 64, 1))


def smooth_first(top_ref, before_ref, w_ref, kept_ref, give_ref, plains, others, tent):
    layers = [(top_ref.at[k], w_ref.at[LOW + k]) for k in range(STEPS - LOW)]
    layers += [(before_ref.at[k], w_ref.at[k]) for k in range(1, RADIUS)]
    smooth(layers, kept_ref, plains, others, tent)
    pair_up(others, 0, 4, give_ref)


def smooth_rest(layers_ref, w_ref, kept_ref, give_ref, give_more_ref, plains, others, tent):
    smooth([(layers_ref.at[k], w_ref.at[k]) for k in range(LOW)], kept_ref, plains, others, tent)
    pair_up(others, 0, 3, give_ref)
    pair_up(others, 6, 3, give_more_ref)


def whole(kept, got, second):
    mine = (lanes(128) >> 6) == core()
    return jnp.where(mine, kept, pltpu.roll(got, 64, 1) if second else got)


def ends(kept_ref, got_ref, top_ref, bottom_ref):
    for k in range(8):
        value = whole(kept_ref[k], got_ref[k % 4], k >= 4)
        if k < STEPS - LOW:
            top_ref[k] = value
        else:
            bottom_ref[k - (STEPS - LOW)] = value


def finish(kept_ref, got_ref, got_more_ref, top_ref, below_ref, above_ref, passive_ref, out_ref, tile):
    gz = lax.axis_index("gz")
    for k in range(LOW):
        got = got_ref if k < 6 else got_more_ref
        tile[k] = whole(kept_ref[k], got[k % 3], k % 6 >= 3)

    def layer(k):
        if k < 0:
            return jnp.where(gz > 0, below_ref[k + RADIUS], 0.0)
        if k == 0:
            return jnp.where(gz == 0, tile[0], below_ref[RADIUS])
        if k > LAYERS:
            return jnp.where(gz < lax.axis_size("gz") - 1, above_ref[k - STEPS], 0.0)
        return tile[k] if k < LOW else top_ref[k - LOW]

    for k in range(LAYERS):
        total = layer(k) * 5.0
        for offset in range(1, RADIUS + 1):
            total = total + (layer(k - offset) + layer(k + offset)) * (5.0 - offset)
        out_ref[k] = jnp.where(passive_ref[k] > 0, 0.0, total)


def to_other(value):
    return moved(value, lambda z, y, x: (z, y ^ 1, x))


def after(value, *others):
    return lax.optimization_barrier((value,) + others)[0]


def per_device(filtered, printed, sensitivity, passive):
    sizes = tuple(lax.axis_size(axis) for axis in AXES)
    depth = sizes[0]
    plane = shape(128, 128)
    edge = shape(16, 128)

    def across(z, y, x):
        return (z, y ^ 3, x) if y in (1, 2) else None

    def on_grid(x):
        return 0 <= x < sizes[2]

    def beside(z, y, x):
        to = x + (1 if y & 1 else -1)
        return (z, y ^ 1, to) if on_grid(to) else (z, y ^ 2, x)

    def same(z, y, x):
        to = x + (-1 if y & 1 else 1)
        return (z, y, to) if on_grid(to) else (z, y ^ 1, x)

    def opposite(z, y, x):
        to = x + (1 if y & 1 else -1)
        return (z, y, to) if on_grid(to) else (z, y ^ 1, x)

    def across_beside(z, y, x):
        to = x + (1 if y & 1 else -1)
        return (z, 3 - y, to) if on_grid(to) else (z, y ^ 2, x)

    hbm = pl.BlockSpec(memory_space=pltpu.HBM)
    lowest_planes, inner, outer, along, back = call(
        edges, [shape(3, 128, 128)] + [edge] * 4, printed, filtered, sensitivity,
        in_specs=[hbm] * 3,
        scratch=[pltpu.VMEM((128, 128), F32), pltpu.VMEM((LAYERS, 128, 128), F32), pltpu.SemaphoreType.DMA((6,))],
    )
    above = moved(lowest_planes, lambda z, y, x: (z - 1, y, x))
    along, back = moved(along, same), moved(back, opposite)
    outer = moved(outer, lambda z, y, x: (z, y ^ 3, x))
    inner = to_other(inner)
    ready = call(early, shape(8, 128), printed, filtered, after(sensitivity, inner))
    uvw = call(
        functools.partial(all_terms, sizes), shape(3 * STEPS, 128, 128),
        printed, filtered, sensitivity, above, inner, outer, along, back, ready,
        scratch=[
            pltpu.VMEM((144, 128), F32), pltpu.VMEM((128, 128), F32),
        ],
    )
    slab, corner = shape(SLAB_ROWS, 128), shape(CORNER_ROWS, 128)
    rows = call(pack_rows, shape(ROW_TOTAL, 128), uvw)
    got = moved(rows, across)
    to_same, to_cross, keep, give = call(pack, [slab, slab, corner, corner], after(uvw, rows))
    from_same = moved(to_same, same)
    from_cross = moved(to_cross, beside)
    corner = call(pick_corner, corner, keep, to_other(give))
    corner = moved(corner, across_beside)
    other = to_other(uvw)
    shared = to_other(after(got, from_same, from_cross, corner))
    parts = (uvw, other, got, shared, from_same, from_cross, corner)
    stack = shape(STEPS, PLANE, 128)
    work = [pltpu.VMEM((2, PLANE, 128), F32), pltpu.VMEM((4, PLANE, 128), F32)]
    uvs = call(assemble, shape(2 * STEPS, PLANE, 128), *parts, scratch=work)
    ws = None
    pieces, before = (), ()
    whole_stack = [pltpu.VMEM((PLANE, 128), F32)]
    for active in range(depth - 1, 0, -1):
        swap = (depth - 1 - active) % 2 == 1
        layers, main, side, strip = call(
            functools.partial(section, active, swap),
            [stack, shape(152 if swap else 192, 128), shape(64, 128), shape(24, 128)],
            uvs, *pieces, *before, scratch=whole_stack,
        )
        before = (layers,)

        def down(where):
            def to(z, y, x):
                target = where(z, y, x) if z == active else None
                return target and (z - 1,) + target[1:]
            return to

        def over(z, y, x):
            return (z, y ^ 2, x)

        def beyond(z, y, x):
            return beside(z, y, x) if on_grid(x + (1 if y & 1 else -1)) else None

        def corner_of(z, y, x):
            target = beyond(z, y, x)
            return target and (z, target[1] ^ 2, target[2])

        side = moved(side, down(beyond))
        edge_piece = moved(strip, down(corner_of))
        halo = strip
        if swap:
            main, halo = call(merge, [shape(256, 128), shape(24, 128)], main, to_other(main))
        main = moved(main, down(lambda z, y, x: (z, y, x)))
        halo = moved(halo, down(over))
        pieces = (main, side, halo, edge_piece)
        if ws is None:
            ws = call(assemble_w, stack, after(uvw, side), *parts[1:], scratch=work)
    top_layers = call(
        section_top, shape(STEPS - LOW, PLANE, 128), uvs, *pieces, layers, scratch=whole_stack
    )

    def work_for(count):
        return [
            pltpu.VMEM((4, PLANE, 128), F32), pltpu.VMEM((count, 128, 128), F32), pltpu.VMEM((256, 128), jnp.bfloat16)
        ]

    kept, given = call(
        smooth_first, [shape(8, 128, 128), shape(4, 128, 128)], top_layers, layers, ws, scratch=work_for(8)
    )
    top, bottom = call(ends, [shape(RADIUS + 1, 128, 128), shape(RADIUS - 1, 128, 128)], kept, to_other(given))
    below = moved(top, lambda z, y, x: (z + 1, y, x) if z < depth - 1 else None)
    over = moved(bottom, lambda z, y, x: (z - 1, y, x) if z > 0 else None)
    rest = call(section_rest, shape(LOW, PLANE, 128), uvs, after(top_layers, top), layers)
    third = shape(3, 128, 128)
    kept, given, given_more = call(
        smooth_rest, [shape(LOW, 128, 128), third, third], rest, ws, scratch=work_for(LOW)
    )
    return call(
        finish, shape(LAYERS, 128, 128),
        kept, to_other(given), to_other(given_more), top, below, over, passive,
        scratch=[pltpu.VMEM((LOW, 128, 128), F32)],
    )


def solution(mesh):
    spec = P(*AXES)
    return jax.shard_map(
        per_device, mesh=mesh, in_specs=(spec,) * 4, out_specs=spec, check_vma=False
    )
```

```python
import functools
import math

import jax
import jax.numpy as jnp
from jax import lax
from jax.experimental import pallas as pl
from jax.experimental.pallas import tpu as pltpu
from jax.sharding import PartitionSpec as P

RADIUS = 4
PENALTY = 40.0
EXPONENT = PENALTY + math.log(5.0) / math.log(0.5)
SMOOTH = 0.001
AXES = ("gz", "gy", "gx")
F32 = jnp.float32

LAYERS = 16
STEPS = LAYERS + 1
PLANE = 288
VECTORS = PLANE // 8
REACH = RADIUS + STEPS
LOW = LAYERS - RADIUS
SLABS = ((16, 15, 14, 3), (13, 12, 11, 8, 0), (10, 9, 7, 6, 5, 2), (4, 1))
FOLDED = 32
SLAB_ROWS = 3 * 128 + FOLDED + 64
CORNERS = ((0, 24), (24, 24), (48, 16), (64, 8), (72, 8))
CORNER_ROWS = 80


def width_of(layer):
    return RADIUS + layer


def rows_of(layer):
    return -(-width_of(layer) // 8) * 8


MICROSECONDS = {"all_terms": 2.5, "assemble": 2.5, "section": 1.5, "section_rest": 3.0, "smooth_rest": 3.0, "finish": 3.0}
VMEM_LIMIT = {"edges": 52 << 20}


def strips():
    out = []
    for slab, layers in enumerate(SLABS):
        at = 0
        for layer in layers:
            for name in ("u", "v"):
                out.append((name, layer, slab, at))
                at += width_of(layer)
        assert at <= (128 if slab < 3 else FOLDED)
    return out


def row_places():
    places, at = {}, 0
    for layer in range(STEPS):
        for name in ("u", "v", "w"):
            if (name, layer) == ("w", 0):
                continue
            rows = 8 if name == "w" else rows_of(layer)
            places[name, layer] = (at, rows)
            at += rows
    return places, at


ROW_PLACES, ROW_TOTAL = row_places()


def moved(value, where):
    sizes = tuple(lax.axis_size(axis) for axis in AXES)
    pairs = []
    for z in range(sizes[0]):
        for y in range(sizes[1]):
            for x in range(sizes[2]):
                to = where(z, y, x)
                if to is not None:
                    tz, ty, tx = to[0] % sizes[0], to[1], to[2] % sizes[2]
                    pairs.append(((z * sizes[1] + y) * sizes[2] + x, (tz * sizes[1] + ty) * sizes[2] + tx))
    return lax.ppermute(value, AXES, pairs)


def shape(*dims):
    return jax.ShapeDtypeStruct(dims, F32)


def call(kernel, outs, *args, scratch=(), in_specs=None, **more):
    name = kernel.func.__name__ if isinstance(kernel, functools.partial) else kernel.__name__
    if in_specs is not None:
        more["in_specs"] = in_specs
    return pl.pallas_call(
        kernel,
        out_shape=outs,
        scratch_shapes=list(scratch),
        compiler_params=pltpu.CompilerParams(vmem_limit_bytes=VMEM_LIMIT.get(name, 40 << 20)),
        cost_estimate=pl.CostEstimate(flops=0, bytes_accessed=int(MICROSECONDS.get(name, 0.5) * 3e6), transcendentals=0),
        name=name,
        **more,
    )(*args)


def lanes(rows):
    return lax.broadcasted_iota(jnp.int32, (rows, 128), 1)


def core():
    return lax.axis_index("gy") & 1


def seam():
    return lax.axis_index("gy") >> 1


def one_if(condition):
    return jnp.where(condition, 1.0, 0.0)


def outside():
    x, c = lax.axis_index("gx"), core()
    return ((c == 0) & (x == 0)) | ((c == 1) & (x == lax.axis_size("gx") - 1))


def plain_to_plane(ref):
    return jnp.concatenate([ref[pl.ds(t, 8, stride=VECTORS), :] for t in range(VECTORS)], axis=0)


def plane_to_plain(value, ref):
    for t in range(VECTORS):
        ref[pl.ds(t, 8, stride=VECTORS), :] = value[8 * t:8 * t + 8]


def aligned(value, to):
    return pl.multiple_of(value, to)


def power40(p):
    x = p + p
    x2 = x * x
    x4 = x2 * x2
    x8 = x4 * x4
    x32 = x8 * x8
    x32 = x32 * x32
    return x32 * x8


def power39(p):
    x = p + p
    x2 = x * x
    x4 = x2 * x2
    x8 = x4 * x4
    x32 = x8 * x8
    x32 = x32 * x32
    return x32 * (x4 * (x2 * x))


def edges(p_hbm, f_hbm, s_hbm, lowest_ref, inner_ref, outer_ref, along_ref, back_ref, turned, p_ref, sems):
    planes = [pltpu.make_async_copy(p_hbm.at[pl.ds(4 * i, 4)], p_ref.at[pl.ds(4 * i, 4)], sems.at[i]) for i in range(4)]
    copies = [pltpu.make_async_copy(ref.at[0], lowest_ref.at[i + 1], sems.at[4 + i]) for i, ref in enumerate((f_hbm, s_hbm))]
    for copy in planes + copies:
        copy.start()
    lane = lanes(128)
    c = core()
    packed = jnp.zeros((128, 128), F32)
    for layer in range(LAYERS):
        if layer % 4 == 0:
            planes[layer // 4].wait()
        inner_ref[pl.ds(layer, 1), :] = p_ref[layer, pl.ds(127 * (1 - c), 1), :]
        outer_ref[pl.ds(layer, 1), :] = p_ref[layer, pl.ds(127 * c, 1), :]
        rolled = pltpu.roll(p_ref[layer], 2 * layer + 1, 1)
        packed = jnp.where((lane >> 1) == layer, rolled, packed)
    turned[...] = packed.T
    right, left = turned[pl.ds(0, 16, stride=2), :], turned[pl.ds(1, 16, stride=2), :]
    along_ref[...] = jnp.where(c == 0, right, left)
    back_ref[...] = jnp.where(c == 0, left, right)
    lowest_ref[0] = p_ref[0]
    for copy in copies:
        copy.wait()


def early(p_ref, f_ref, s_ref, out_ref):
    out_ref[...] = p_ref[0, pl.ds(0, 8), :] + f_ref[0, pl.ds(0, 8), :] + s_ref[0, pl.ds(0, 8), :]


def norm_of(position, extent):
    def missing(k):
        k = jnp.maximum(k, 0)
        return (k * (k + 1)) >> 1

    return ((RADIUS + 1) ** 2 - missing(RADIUS - position) - missing(RADIUS - (extent - 1 - position))).astype(F32)


def terms(total, density, sens, p39):
    total = jnp.maximum(total, 1e-30)
    offset = PENALTY * math.log(2.0) / EXPONENT
    smax = jnp.exp(jnp.log(total) * (1.0 / EXPONENT) - offset)
    gap = density - smax
    half = 0.5 * gap * lax.rsqrt(gap * gap + SMOOTH)
    low = 0.5 - half
    top = (0.5 + half) * (2.0 * PENALTY / EXPONENT) * smax
    h = top / total
    return h * sens, h * p39, low, total / top


def plane_norms(sizes):
    row0 = lax.axis_index("gy") * 128
    col0 = lax.axis_index("gx") * 128
    rows = lax.broadcasted_iota(jnp.int32, (128, 128), 0) + row0
    cols = lax.broadcasted_iota(jnp.int32, (128, 128), 1) + col0
    return norm_of(rows, sizes[1] * 128) * norm_of(cols, sizes[2] * 128)


def neighbours(p, layer, inner_ref, outer_ref, beside, powers):
    c = core()
    lane = lanes(128)
    own = power40(p)
    powers[pl.ds(8, 128), :] = own
    y = lax.axis_index("gy")
    there = one_if((y == 1) | (y == 2))
    powers[pl.ds(7 + 129 * (1 - c), 1), :] = power40(inner_ref[pl.ds(layer, 1), :])
    powers[pl.ds(7 + 129 * c, 1), :] = power40(outer_ref[pl.ds(layer, 1), :]) * there
    side = pltpu.roll(beside, (128 - (2 * layer + 1)) % 128, 1)
    right = jnp.where(lane == 127, side, pltpu.roll(own, 127, 1))
    left = jnp.where(lane == 0, side, pltpu.roll(own, 1, 1))
    return (own + right) + left + (powers[pl.ds(7, 128), :] + powers[pl.ds(9, 128), :])


def columns_beside(along_ref, back_ref, turned):
    x = lax.axis_index("gx")
    turned[...] = jnp.zeros((128, 128), F32)
    first = core() == 0
    right = jnp.where(first, back_ref[...], along_ref[...])
    left = jnp.where(first, along_ref[...], back_ref[...])
    turned[pl.ds(0, 16, stride=2), :] = right * one_if(x < lax.axis_size("gx") - 1)
    turned[pl.ds(1, 16, stride=2), :] = left * one_if(x > 0)
    return power40(turned[...].T)


def all_terms(
    sizes, p_ref, f_ref, s_ref, above_ref, inner_ref, outer_ref, along_ref, back_ref, early_ref, uvw_ref, powers, turned
):
    beside = columns_beside(along_ref, back_ref, turned)
    norms = 1.0 / plane_norms(sizes)
    gz = lax.axis_index("gz")
    layer0 = gz * LAYERS
    uvw_ref[0] = s_ref[0]
    uvw_ref[STEPS] = power39(p_ref[0])
    uvw_ref[2 * STEPS] = norms * (1.0 / norm_of(0 * layer0, sizes[0] * LAYERS))
    for layer in range(1, STEPS):
        total = neighbours(p_ref[layer - 1], layer - 1, inner_ref, outer_ref, beside, powers)
        if layer < LAYERS:
            p, f, s = p_ref[layer], f_ref[layer], s_ref[layer]
        else:
            p, f, s = above_ref[0], above_ref[1], above_ref[2]
        u, v, low, inverse = terms(total, f, s, power39(p))
        if layer == LAYERS:
            there = one_if(gz < sizes[0] - 1)
            u, v = u * there, v * there
        norm_z = norm_of(layer0 + layer, sizes[0] * LAYERS)
        uvw_ref[layer] = u
        uvw_ref[STEPS + layer] = v
        uvw_ref[2 * STEPS + layer] = low * inverse * (norms * (1.0 / norm_z))


def plane_of(uvw_ref, name, layer):
    return uvw_ref.at[STEPS * "uvw".index(name) + layer]


def pack_rows(uvw_ref, rows_ref):
    c = core()
    for (name, layer), (at, rows) in ROW_PLACES.items():
        start = aligned(c * (128 - rows), 8)
        rows_ref[pl.ds(at, rows), :] = plane_of(uvw_ref, name, layer)[pl.ds(start, rows), :]


def pack(uvw_ref, same_ref, cross_ref, keep_ref, give_ref):
    c = core()

    def put(at, left, right):
        count = left.shape[0]
        same_ref[pl.ds(at, count), :] = jnp.where(c == 0, right, left)
        cross_ref[pl.ds(at, count), :] = jnp.where(c == 0, left, right)

    def put_corner(slab, left, right):
        at, rows = CORNERS[slab]
        first, last = slice(0, rows), slice(left.shape[0] - rows, left.shape[0])
        keep_ref[pl.ds(at, rows), :] = jnp.where(c == 0, left[first], right[last])
        give_ref[pl.ds(at, rows), :] = jnp.where(c == 0, right[first], left[last])

    lane = lanes(128)
    for slab in range(4):
        left = right = jnp.zeros((128, 128), F32)
        for name, layer, where, at in strips():
            if where == slab:
                width = width_of(layer)
                plane = plane_of(uvw_ref, name, layer)[...]
                inside = (lane >= at) & (lane < at + width)
                left = jnp.where(inside, pltpu.roll(plane, at, 1) if at else plane, left)
                right = jnp.where(inside, pltpu.roll(plane, (at + width) % 128, 1), right)
        if slab < 3:
            put(128 * slab, left, right)
            put_corner(slab, left, right)
            continue
        put_corner(slab, left, right)
        folded = []
        for value in (left, right):
            total = value[:FOLDED]
            for i in range(1, 4):
                total = total + pltpu.roll(value[FOLDED * i:FOLDED * (i + 1)], FOLDED * i, 1)
            folded.append(total)
        put(384, *folded)
    lane = lanes(64)
    left = right = jnp.zeros((64, 128), F32)
    for layer in range(1, STEPS):
        ref = plane_of(uvw_ref, "w", layer)
        for half in range(2):
            plane = ref[pl.ds(64 * half, 64), :]
            at = 64 * half + RADIUS * (layer - 1)
            inside = (lane >= at) & (lane < at + RADIUS)
            left = jnp.where(inside, pltpu.roll(plane, at, 1) if at else plane, left)
            right = jnp.where(inside, pltpu.roll(plane, (at + RADIUS) % 128, 1), right)
    put(384 + FOLDED, left, right)
    put_corner(4, left, right)


def pick_corner(keep_ref, got_ref, corner_ref):
    corner_ref[...] = jnp.where((core() ^ seam()) == 1, keep_ref[...], got_ref[...])


def slab_plane(plain, same, cross, corner):
    c = core()
    inside = one_if(jnp.logical_not(outside()))
    plain[pl.ds(256, 32), :] = jnp.zeros((32, 128), F32)
    plain[pl.ds(aligned(c * 128, 128), 128), :] = same * inside
    plain[pl.ds(aligned((1 - c) * 128, 128), 128), :] = cross * inside
    rows = corner.shape[0]
    plain[pl.ds(aligned(256 + seam() * (32 - rows), 8), rows), :] = corner * inside


def full_plane(plain, name, layer, uvw_ref, other_ref, got_ref, shared_ref):
    c = core()
    plain[pl.ds(aligned(c * 128, 128), 128), :] = plane_of(uvw_ref, name, layer)[...]
    plain[pl.ds(aligned((1 - c) * 128, 128), 128), :] = plane_of(other_ref, name, layer)[...]
    plain[pl.ds(256, 32), :] = jnp.zeros((32, 128), F32)
    start, rows = ROW_PLACES[name, layer]
    here = pl.ds(start, rows)
    to = aligned(256 + seam() * (32 - rows), 8)
    plain[pl.ds(to, rows), :] = jnp.where((c ^ seam()) == 1, got_ref[here, :], shared_ref[here, :])
    return plain_to_plane(plain)


def with_columns(base, columns, at, width):
    c = core()
    lane = lanes(PLANE)
    columns = pltpu.roll(columns, (128 - at - (1 - c) * width) & 127, 1)
    begin = (1 - c) * (128 - width)
    return jnp.where((lane >= begin) & (lane < begin + width), columns, base)


def assemble(
    uvw_ref, other_ref, got_ref, shared_ref, same_ref, cross_ref, corner_ref, uv_ref, plain, slabs
):
    c = core()
    for slab in range(4):
        if slab < 3:
            here = pl.ds(128 * slab, 128)
            same, cross = same_ref[here, :], cross_ref[here, :]
            here = pl.ds(*CORNERS[slab])
        else:
            here = pl.ds(384, FOLDED)
            same, cross = (
                jnp.concatenate([value] + [pltpu.roll(value, 128 - FOLDED * i, 1) for i in range(1, 4)], axis=0)
                for value in (same_ref[here, :], cross_ref[here, :])
            )
            here = pl.ds(*CORNERS[3])
        corner = corner_ref[here, :]
        slot = plain.at[slab % 2]
        slab_plane(slot, same, cross, corner)
        slabs[slab] = plain_to_plane(slot)
    for place, (name, layer, slab, at) in enumerate(strips()):
        base = full_plane(plain.at[place % 2], name, layer, uvw_ref, other_ref, got_ref, shared_ref)
        uv_ref[2 * (LAYERS - layer) + (name == "v")] = with_columns(base, slabs[slab], at, width_of(layer))


def assemble_w(
    uvw_ref, other_ref, got_ref, shared_ref, same_ref, cross_ref, corner_ref, w_ref, plain, slabs
):
    c = core()

    def unfolded(ref):
        value = ref[pl.ds(384 + FOLDED, 64), :]
        return jnp.concatenate([value, pltpu.roll(value, 64, 1)], axis=0)

    here = pl.ds(*CORNERS[4])
    corner = corner_ref[here, :]
    corner = pltpu.roll(corner, 64 * seam(), 1)
    slab_plane(plain.at[0], unfolded(same_ref), unfolded(cross_ref), corner)
    slabs[0] = plain_to_plane(plain.at[0])
    for layer in range(1, STEPS):
        base = full_plane(plain.at[layer % 2], "w", layer, uvw_ref, other_ref, got_ref, shared_ref)
        w_ref[layer] = with_columns(base, slabs[0], RADIUS * (layer - 1), RADIUS)
    row = lax.broadcasted_iota(jnp.int32, (PLANE, 128), 0)
    col = lax.broadcasted_iota(jnp.int32, (PLANE, 128), 1)
    a = seam()
    row = jnp.where((a == 1) & (row >= 256), row - PLANE, row) + 256 * a
    width = jnp.where(c == 0, 108, 20)
    col = jnp.where((c == 0) & (col >= width), col - 128, jnp.where((c == 1) & (col < width), col + 128, col))
    col = col + 128 * lax.axis_index("gx")
    rows, cols = 128 * lax.axis_size("gy"), 128 * lax.axis_size("gx")
    norm = norm_of(row, rows) * norm_of(col, cols) * norm_of(0 * a, LAYERS * lax.axis_size("gz"))
    inside = (row >= 0) & (row < rows) & (col >= 0) & (col < cols)
    plain[0] = jnp.where(inside, 1.0 / jnp.where(inside, norm, 1.0), 0.0)
    w_ref[0] = plain_to_plane(plain.at[0])


def step_down(values, u_ref, v_ref, out_ref):
    new = []
    for t, value in enumerate(values):
        before = values[t - 1] if t > 0 else pltpu.roll(values[-1], 1, 0)
        behind = values[t + 1] if t < VECTORS - 1 else pltpu.roll(values[0], 7, 0)
        total = (value + before) + (behind + pltpu.roll(value, 1, 1)) + pltpu.roll(value, 127, 1)
        here = pl.ds(8 * t, 8)
        new.append(u_ref[here, :] + v_ref[here, :] * total)
        out_ref[here, :] = new[-1]
    return new


def set_carry(carry, main_ref, outer_ref, halo_ref, halo_outer_ref):
    c = core()
    lane = lanes(64)
    mine = (lane >> 6) == c
    inside = one_if(jnp.logical_not(outside()))
    begin = (1 - c) * (128 - REACH)
    beyond = (lane >= begin) & (lane < begin + REACH)
    for i in range(4):
        if main_ref.shape[0] == 256:
            value = main_ref[pl.ds(64 * i, 64), :]
        else:
            value = main_ref[pl.ds(64 * (i % 2), 64), :]
            if i >= 2:
                value = pltpu.roll(value, 64, 1)
            inner = pltpu.roll(main_ref[pl.ds(128, 64), :], (32 * (2 - c) - 32 * i) & 127, 1)
            value = jnp.where(mine, value, inner)
        outer = pltpu.roll(outer_ref[...], (128 - 32 * i) % 128, 1) if i else outer_ref[...]
        carry[pl.ds(64 * i, 64), :] = jnp.where(beyond, outer * inside, value)
    lane = lanes(24)
    beyond = (lane >= begin) & (lane < begin + REACH)
    carry[pl.ds(256, 32), :] = jnp.zeros((32, 128), F32)
    carry[pl.ds(aligned(256 + 8 * seam(), 8), 24), :] = jnp.where(beyond, halo_outer_ref[...] * inside, halo_ref[...])


def merge(give_ref, got_ref, down_ref, halo_ref):
    mine = (lanes(128) >> 6) == core()
    rows = pl.ds(0, 128)
    own, other = give_ref[rows, :], got_ref[rows, :]
    down_ref[rows, :] = jnp.where(mine, own, other)
    down_ref[pl.ds(128, 128), :] = pltpu.roll(jnp.where(mine, other, own), 64, 1)
    rows = pl.ds(128, 24)
    halo_ref[...] = jnp.where(mine[:24], give_ref[rows, :], got_ref[rows, :])


def load_carry(pieces, carry):
    set_carry(carry, *pieces)
    return [carry[pl.ds(t, 8, stride=VECTORS), :] for t in range(VECTORS)]


def run_down(values, uv_ref, layers_ref, first, last, base=0):
    for layer in range(first, last - 1, -1):
        at = 2 * (LAYERS - layer)
        values = step_down(values, uv_ref.at[at], uv_ref.at[at + 1], layers_ref.at[layer - base])
    return values


def section(active, shared, *refs):
    uv_ref, refs = refs[0], refs[1:]
    pieces, before_ref = (), None
    if len(refs) > 5:
        pieces, before_ref, refs = refs[:4], refs[4], refs[5:]
    layers_ref, down_ref, outer_ref, strip_ref, carry = refs

    @pl.when(lax.axis_index("gz") == active)
    def _():
        values = load_carry(pieces, carry) if pieces else [jnp.zeros((8, 128), F32)] * VECTORS
        values = run_down(values, uv_ref, layers_ref, LAYERS, 1)
        layers_ref[0] = layers_ref[1]
        for t in range(VECTORS):
            carry[pl.ds(t, 8, stride=VECTORS), :] = values[t]
        c = core()
        mine = (lanes(128) >> 6) == c
        down_ref[pl.ds(0, 128), :] = jnp.where(
            mine, carry[pl.ds(0, 128), :], pltpu.roll(carry[pl.ds(128, 128), :], 64, 1)
        )
        lane = lanes(64)
        slab = inner = jnp.zeros((64, 128), F32)
        for i in range(4):
            block = carry[pl.ds(64 * i, 64), :]
            rolled = pltpu.roll(block, 32 * i, 1) if i else block
            begin = (32 * i + 128 - c * 32) & 127
            slab = jnp.where(((lane - begin) & 127) < 32, rolled, slab)
            if not shared:
                inner = jnp.where((lane >> 5) == i, pltpu.roll(block, (32 * i - 32 * (2 - c)) & 127, 1), inner)
        outer_ref[...] = slab
        strip = carry[pl.ds(aligned((1 - seam()) * 232, 8), 24), :]
        strip_ref[...] = strip
        if shared:
            down_ref[pl.ds(128, 24), :] = strip
        else:
            down_ref[pl.ds(128, 64), :] = inner

    if before_ref is not None:
        @pl.when(lax.axis_index("gz") != active)
        def _():
            layers_ref[...] = before_ref[...]


def section_top(uv_ref, main_ref, outer_ref, halo_ref, halo_outer_ref, before_ref, top_ref, carry):
    @pl.when(lax.axis_index("gz") == 0)
    def _():
        values = load_carry((main_ref, outer_ref, halo_ref, halo_outer_ref), carry)
        run_down(values, uv_ref, top_ref, LAYERS, LOW, LOW)

    @pl.when(lax.axis_index("gz") != 0)
    def _():
        top_ref[...] = before_ref[pl.ds(LOW, STEPS - LOW)]


def section_rest(uv_ref, top_ref, before_ref, layers_ref):
    @pl.when(lax.axis_index("gz") == 0)
    def _():
        values = [top_ref[0, pl.ds(8 * t, 8), :] for t in range(VECTORS)]
        run_down(values, uv_ref, layers_ref, LOW - 1, 0)

    @pl.when(lax.axis_index("gz") != 0)
    def _():
        layers_ref[...] = before_ref[pl.ds(0, LOW)]


def box(values):
    two = [values[i] + values[i + 1] for i in range(len(values) - 1)]
    four = [two[i] + two[i + 2] for i in range(len(two) - 2)]
    return [four[i] + values[i + 4] for i in range(len(values) - 4)]


def smooth(layers, kept_ref, plains, others, tent):
    c = core()
    row = lax.broadcasted_iota(jnp.int32, (256, 128), 0)
    col = lax.broadcasted_iota(jnp.int32, (256, 128), 1)
    distance = (row - col + RADIUS) & 127
    weight = jnp.where(distance <= 2 * RADIUS, RADIUS + 1 - jnp.abs(distance - RADIUS), 0)
    tent[...] = weight.astype(F32).astype(jnp.bfloat16)
    for k, (layer_ref, w_ref) in enumerate(layers):
        plain = plains.at[k % 4]
        values = [layer_ref[pl.ds(8 * t, 8), :] * w_ref[pl.ds(8 * t, 8), :] for t in range(VECTORS)]
        first = [pltpu.roll(value, 1, 0) for value in values[VECTORS - RADIUS:]]
        last = [pltpu.roll(value, 7, 0) for value in values[:RADIUS]]
        total = jnp.concatenate(box(box(first + values + last)), axis=0)
        high = total.astype(jnp.bfloat16)
        rest = total - high.astype(F32)
        middle = rest.astype(jnp.bfloat16)
        small = (rest - middle.astype(F32)).astype(jnp.bfloat16)
        value = jnp.dot(jnp.concatenate([high, middle], axis=1), tent[...], preferred_element_type=F32)
        value = value + jnp.dot(small, tent[pl.ds(0, 128), :], preferred_element_type=F32)
        plane_to_plain(value, plain)
        kept_ref[k] = plain[pl.ds(aligned(c * 128, 128), 128), :]
        others[k] = plain[pl.ds(aligned((1 - c) * 128, 128), 128), :]


def pair_up(others, first, count, give_ref):
    mine = (lanes(128) >> 6) == core()
    for k in range(count):
        give_ref[k] = jnp.where(mine, others[first + k], pltpu.roll(others[first + count + k], 64, 1))


def smooth_first(top_ref, before_ref, w_ref, kept_ref, give_ref, plains, others, tent):
    layers = [(top_ref.at[k], w_ref.at[LOW + k]) for k in range(STEPS - LOW)]
    layers += [(before_ref.at[k], w_ref.at[k]) for k in range(1, RADIUS)]
    smooth(layers, kept_ref, plains, others, tent)
    pair_up(others, 0, 4, give_ref)


def smooth_rest(layers_ref, w_ref, kept_ref, first_ref, second_ref, third_ref, plains, others, tent):
    smooth([(layers_ref.at[k], w_ref.at[k]) for k in range(LOW)], kept_ref, plains, others, tent)
    for i, give_ref in enumerate((first_ref, second_ref, third_ref)):
        pair_up(others, 4 * i, 2, give_ref)


def whole(kept, got, second):
    mine = (lanes(128) >> 6) == core()
    return jnp.where(mine, kept, pltpu.roll(got, 64, 1) if second else got)


def ends(kept_ref, got_ref, top_ref, bottom_ref):
    for k in range(8):
        value = whole(kept_ref[k], got_ref[k % 4], k >= 4)
        if k < STEPS - LOW:
            top_ref[k] = value
        else:
            bottom_ref[k - (STEPS - LOW)] = value


def finish(kept_ref, first_ref, second_ref, third_ref, top_ref, below_ref, above_ref, passive_ref, out_ref, tile):
    gz = lax.axis_index("gz")
    for k in range(LOW):
        got = (first_ref, second_ref, third_ref)[k // 4]
        tile[k] = whole(kept_ref[k], got[k % 2], k % 4 >= 2)

    def layer(k):
        if k < 0:
            return jnp.where(gz > 0, below_ref[k + RADIUS], 0.0)
        if k == 0:
            return jnp.where(gz == 0, tile[0], below_ref[RADIUS])
        if k > LAYERS:
            return jnp.where(gz < lax.axis_size("gz") - 1, above_ref[k - STEPS], 0.0)
        return tile[k] if k < LOW else top_ref[k - LOW]

    for k in range(LAYERS):
        total = layer(k) * 5.0
        for offset in range(1, RADIUS + 1):
            total = total + (layer(k - offset) + layer(k + offset)) * (5.0 - offset)
        out_ref[k] = jnp.where(passive_ref[k] > 0, 0.0, total)


def to_other(value):
    return moved(value, lambda z, y, x: (z, y ^ 1, x))


def after(value, *others):
    return lax.optimization_barrier((value,) + others)[0]


def per_device(filtered, printed, sensitivity, passive):
    sizes = tuple(lax.axis_size(axis) for axis in AXES)
    depth = sizes[0]
    plane = shape(128, 128)
    edge = shape(16, 128)

    def across(z, y, x):
        return (z, y ^ 3, x) if y in (1, 2) else None

    def on_grid(x):
        return 0 <= x < sizes[2]

    def beside(z, y, x):
        to = x + (1 if y & 1 else -1)
        return (z, y ^ 1, to) if on_grid(to) else (z, y ^ 2, x)

    def same(z, y, x):
        to = x + (-1 if y & 1 else 1)
        return (z, y, to) if on_grid(to) else (z, y ^ 1, x)

    def opposite(z, y, x):
        to = x + (1 if y & 1 else -1)
        return (z, y, to) if on_grid(to) else (z, y ^ 1, x)

    def across_beside(z, y, x):
        to = x + (1 if y & 1 else -1)
        return (z, 3 - y, to) if on_grid(to) else (z, y ^ 2, x)

    hbm = pl.BlockSpec(memory_space=pltpu.HBM)
    lowest_planes, inner, outer, along, back = call(
        edges, [shape(3, 128, 128)] + [edge] * 4, printed, filtered, sensitivity,
        in_specs=[hbm] * 3,
        scratch=[pltpu.VMEM((128, 128), F32), pltpu.VMEM((LAYERS, 128, 128), F32), pltpu.SemaphoreType.DMA((6,))],
    )
    above = moved(lowest_planes, lambda z, y, x: (z - 1, y, x))
    along, back = moved(along, same), moved(back, opposite)
    outer = moved(outer, lambda z, y, x: (z, y ^ 3, x))
    inner = to_other(inner)
    ready = call(early, shape(8, 128), printed, filtered, after(sensitivity, inner))
    uvw = call(
        functools.partial(all_terms, sizes), shape(3 * STEPS, 128, 128),
        printed, filtered, sensitivity, above, inner, outer, along, back, ready,
        scratch=[
            pltpu.VMEM((144, 128), F32), pltpu.VMEM((128, 128), F32),
        ],
    )
    slab, corner = shape(SLAB_ROWS, 128), shape(CORNER_ROWS, 128)
    rows = call(pack_rows, shape(ROW_TOTAL, 128), uvw)
    got = moved(rows, across)
    to_same, to_cross, keep, give = call(pack, [slab, slab, corner, corner], after(uvw, rows))
    from_same = moved(to_same, same)
    from_cross = moved(to_cross, beside)
    corner = call(pick_corner, corner, keep, to_other(give))
    corner = moved(corner, across_beside)
    other = to_other(uvw)
    shared = to_other(after(got, from_same, from_cross, corner))
    parts = (uvw, other, got, shared, from_same, from_cross, corner)
    stack = shape(STEPS, PLANE, 128)
    work = [pltpu.VMEM((2, PLANE, 128), F32), pltpu.VMEM((4, PLANE, 128), F32)]
    uvs = call(assemble, shape(2 * STEPS, PLANE, 128), *parts, scratch=work)
    ws = None
    pieces, before = (), ()
    whole_stack = [pltpu.VMEM((PLANE, 128), F32)]
    for active in range(depth - 1, 0, -1):
        swap = (depth - 1 - active) % 2 == 1
        layers, main, side, strip = call(
            functools.partial(section, active, swap),
            [stack, shape(152 if swap else 192, 128), shape(64, 128), shape(24, 128)],
            uvs, *pieces, *before, scratch=whole_stack,
        )
        before = (layers,)

        def down(where):
            def to(z, y, x):
                target = where(z, y, x) if z == active else None
                return target and (z - 1,) + target[1:]
            return to

        def over(z, y, x):
            return (z, y ^ 2, x)

        def beyond(z, y, x):
            return beside(z, y, x) if on_grid(x + (1 if y & 1 else -1)) else None

        def corner_of(z, y, x):
            target = beyond(z, y, x)
            return target and (z, target[1] ^ 2, target[2])

        side = moved(side, down(beyond))
        edge_piece = moved(strip, down(corner_of))
        halo = strip
        if swap:
            main, halo = call(merge, [shape(256, 128), shape(24, 128)], main, to_other(main))
        main = moved(main, down(lambda z, y, x: (z, y, x)))
        halo = moved(halo, down(over))
        pieces = (main, side, halo, edge_piece)
        if ws is None:
            ws = call(assemble_w, stack, after(uvw, side), *parts[1:], scratch=work)
    top_layers = call(
        section_top, shape(STEPS - LOW, PLANE, 128), uvs, *pieces, layers, scratch=whole_stack
    )

    def work_for(count):
        return [
            pltpu.VMEM((4, PLANE, 128), F32), pltpu.VMEM((count, 128, 128), F32), pltpu.VMEM((256, 128), jnp.bfloat16)
        ]

    kept, given = call(
        smooth_first, [shape(8, 128, 128), shape(4, 128, 128)], top_layers, layers, ws, scratch=work_for(8)
    )
    top, bottom = call(ends, [shape(RADIUS + 1, 128, 128), shape(RADIUS - 1, 128, 128)], kept, to_other(given))
    below = moved(top, lambda z, y, x: (z + 1, y, x))
    over = moved(bottom, lambda z, y, x: (z - 1, y, x))
    rest = call(section_rest, shape(LOW, PLANE, 128), uvs, after(top_layers, top), layers)
    third = shape(2, 128, 128)
    kept, *given = call(
        smooth_rest, [shape(LOW, 128, 128), third, third, third], rest, ws, scratch=work_for(LOW)
    )
    return call(
        finish, shape(LAYERS, 128, 128),
        kept, *(to_other(part) for part in given), top, below, over, passive,
        scratch=[pltpu.VMEM((LOW, 128, 128), F32)],
    )


def solution(mesh):
    spec = P(*AXES)
    return jax.shard_map(
        per_device, mesh=mesh, in_specs=(spec,) * 4, out_specs=spec, check_vma=False
    )
```

```python
import functools
import math

import jax
import jax.numpy as jnp
from jax import lax
from jax.experimental import pallas as pl
from jax.experimental.pallas import tpu as pltpu
from jax.sharding import PartitionSpec as P

RADIUS = 4
PENALTY = 40.0
EXPONENT = PENALTY + math.log(5.0) / math.log(0.5)
SMOOTH = 0.001
AXES = ("gz", "gy", "gx")
F32 = jnp.float32

LAYERS = 16
STEPS = LAYERS + 1
PLANE = 288
VECTORS = PLANE // 8
REACH = RADIUS + STEPS
LOW = LAYERS - RADIUS
SLABS = ((16, 15, 14, 3), (13, 12, 11, 8, 0), (10, 9, 7, 6, 5, 2), (4, 1))
FOLDED = 32
SLAB_ROWS = 3 * 128 + FOLDED + 64
CORNERS = ((0, 24), (24, 24), (48, 16), (64, 8), (72, 8))
CORNER_ROWS = 80


def width_of(layer):
    return RADIUS + layer


def rows_of(layer):
    return -(-width_of(layer) // 8) * 8


MICROSECONDS = {"all_terms": 2.5, "assemble": 2.5, "section": 1.5, "section_rest": 3.0, "smooth_rest": 3.0, "finish": 3.0}
VMEM_LIMIT = {"edges": 52 << 20}


def strips():
    out = []
    for slab, layers in enumerate(SLABS):
        at = 0
        for layer in layers:
            for name in ("u", "v"):
                out.append((name, layer, slab, at))
                at += width_of(layer)
        assert at <= (128 if slab < 3 else FOLDED)
    return out


def row_places():
    places, at = {}, 0
    for layer in range(STEPS):
        for name in ("u", "v", "w"):
            if (name, layer) == ("w", 0):
                continue
            rows = 8 if name == "w" else rows_of(layer)
            places[name, layer] = (at, rows)
            at += rows
    return places, at


ROW_PLACES, ROW_TOTAL = row_places()


def moved(value, where):
    sizes = tuple(lax.axis_size(axis) for axis in AXES)
    pairs = []
    for z in range(sizes[0]):
        for y in range(sizes[1]):
            for x in range(sizes[2]):
                to = where(z, y, x)
                if to is not None:
                    tz, ty, tx = to[0] % sizes[0], to[1], to[2] % sizes[2]
                    pairs.append(((z * sizes[1] + y) * sizes[2] + x, (tz * sizes[1] + ty) * sizes[2] + tx))
    return lax.ppermute(value, AXES, pairs)


def shape(*dims):
    return jax.ShapeDtypeStruct(dims, F32)


def call(kernel, outs, *args, scratch=(), in_specs=None, **more):
    name = kernel.func.__name__ if isinstance(kernel, functools.partial) else kernel.__name__
    if in_specs is not None:
        more["in_specs"] = in_specs
    return pl.pallas_call(
        kernel,
        out_shape=outs,
        scratch_shapes=list(scratch),
        compiler_params=pltpu.CompilerParams(vmem_limit_bytes=VMEM_LIMIT.get(name, 40 << 20)),
        cost_estimate=pl.CostEstimate(flops=0, bytes_accessed=int(MICROSECONDS.get(name, 0.5) * 3e6), transcendentals=0),
        name=name,
        **more,
    )(*args)


def lanes(rows):
    return lax.broadcasted_iota(jnp.int32, (rows, 128), 1)


def core():
    return lax.axis_index("gy") & 1


def seam():
    return lax.axis_index("gy") >> 1


def one_if(condition):
    return jnp.where(condition, 1.0, 0.0)


def outside():
    x, c = lax.axis_index("gx"), core()
    return ((c == 0) & (x == 0)) | ((c == 1) & (x == lax.axis_size("gx") - 1))


def plain_to_plane(ref):
    return jnp.concatenate([ref[pl.ds(t, 8, stride=VECTORS), :] for t in range(VECTORS)], axis=0)


def plane_to_plain(value, ref):
    for t in range(VECTORS):
        ref[pl.ds(t, 8, stride=VECTORS), :] = value[8 * t:8 * t + 8]


def aligned(value, to):
    return pl.multiple_of(value, to)


def power40(p):
    x = p + p
    x2 = x * x
    x4 = x2 * x2
    x8 = x4 * x4
    x32 = x8 * x8
    x32 = x32 * x32
    return x32 * x8


def power39(p):
    x = p + p
    x2 = x * x
    x4 = x2 * x2
    x8 = x4 * x4
    x32 = x8 * x8
    x32 = x32 * x32
    return x32 * (x4 * (x2 * x))


def edges(p_hbm, f_hbm, s_hbm, lowest_ref, inner_ref, outer_ref, along_ref, back_ref, turned, p_ref, sems):
    planes = [pltpu.make_async_copy(p_hbm.at[pl.ds(4 * i, 4)], p_ref.at[pl.ds(4 * i, 4)], sems.at[i]) for i in range(4)]
    copies = [pltpu.make_async_copy(ref.at[0], lowest_ref.at[i + 1], sems.at[4 + i]) for i, ref in enumerate((f_hbm, s_hbm))]
    for copy in planes + copies:
        copy.start()
    lane = lanes(128)
    c = core()
    packed = jnp.zeros((128, 128), F32)
    for layer in range(LAYERS):
        if layer % 4 == 0:
            planes[layer // 4].wait()
        inner_ref[pl.ds(layer, 1), :] = p_ref[layer, pl.ds(127 * (1 - c), 1), :]
        outer_ref[pl.ds(layer, 1), :] = p_ref[layer, pl.ds(127 * c, 1), :]
        rolled = pltpu.roll(p_ref[layer], 2 * layer + 1, 1)
        packed = jnp.where((lane >> 1) == layer, rolled, packed)
    turned[...] = packed.T
    right, left = turned[pl.ds(0, 16, stride=2), :], turned[pl.ds(1, 16, stride=2), :]
    along_ref[...] = jnp.where(c == 0, right, left)
    back_ref[...] = jnp.where(c == 0, left, right)
    lowest_ref[0] = p_ref[0]
    for copy in copies:
        copy.wait()


def early(p_ref, f_ref, s_ref, out_ref):
    out_ref[...] = p_ref[0, pl.ds(0, 8), :] + f_ref[0, pl.ds(0, 8), :] + s_ref[0, pl.ds(0, 8), :]


def norm_of(position, extent):
    def missing(k):
        k = jnp.maximum(k, 0)
        return (k * (k + 1)) >> 1

    return ((RADIUS + 1) ** 2 - missing(RADIUS - position) - missing(RADIUS - (extent - 1 - position))).astype(F32)


def terms(total, density, sens, p39):
    total = jnp.maximum(total, 1e-30)
    offset = PENALTY * math.log(2.0) / EXPONENT
    smax = jnp.exp(jnp.log(total) * (1.0 / EXPONENT) - offset)
    gap = density - smax
    half = 0.5 * gap * lax.rsqrt(gap * gap + SMOOTH)
    low = 0.5 - half
    top = (0.5 + half) * (2.0 * PENALTY / EXPONENT) * smax
    h = top / total
    return h * sens, h * p39, low, total / top


def plane_norms(sizes):
    row0 = lax.axis_index("gy") * 128
    col0 = lax.axis_index("gx") * 128
    rows = lax.broadcasted_iota(jnp.int32, (128, 128), 0) + row0
    cols = lax.broadcasted_iota(jnp.int32, (128, 128), 1) + col0
    return norm_of(rows, sizes[1] * 128) * norm_of(cols, sizes[2] * 128)


def neighbours(p, layer, inner_ref, outer_ref, beside, powers):
    c = core()
    lane = lanes(128)
    own = power40(p)
    powers[pl.ds(8, 128), :] = own
    y = lax.axis_index("gy")
    there = one_if((y == 1) | (y == 2))
    powers[pl.ds(7 + 129 * (1 - c), 1), :] = power40(inner_ref[pl.ds(layer, 1), :])
    powers[pl.ds(7 + 129 * c, 1), :] = power40(outer_ref[pl.ds(layer, 1), :]) * there
    side = pltpu.roll(beside, (128 - (2 * layer + 1)) % 128, 1)
    right = jnp.where(lane == 127, side, pltpu.roll(own, 127, 1))
    left = jnp.where(lane == 0, side, pltpu.roll(own, 1, 1))
    return (own + right) + left + (powers[pl.ds(7, 128), :] + powers[pl.ds(9, 128), :])


def columns_beside(along_ref, back_ref, turned):
    x = lax.axis_index("gx")
    turned[...] = jnp.zeros((128, 128), F32)
    first = core() == 0
    right = jnp.where(first, back_ref[...], along_ref[...])
    left = jnp.where(first, along_ref[...], back_ref[...])
    turned[pl.ds(0, 16, stride=2), :] = right * one_if(x < lax.axis_size("gx") - 1)
    turned[pl.ds(1, 16, stride=2), :] = left * one_if(x > 0)
    return power40(turned[...].T)


def all_terms(
    sizes, p_ref, f_ref, s_ref, above_ref, inner_ref, outer_ref, along_ref, back_ref, early_ref, uvw_ref, powers, turned
):
    beside = columns_beside(along_ref, back_ref, turned)
    norms = 1.0 / plane_norms(sizes)
    gz = lax.axis_index("gz")
    layer0 = gz * LAYERS
    uvw_ref[0] = s_ref[0]
    uvw_ref[STEPS] = power39(p_ref[0])
    uvw_ref[2 * STEPS] = norms * (1.0 / norm_of(0 * layer0, sizes[0] * LAYERS))
    for layer in range(1, STEPS):
        total = neighbours(p_ref[layer - 1], layer - 1, inner_ref, outer_ref, beside, powers)
        if layer < LAYERS:
            p, f, s = p_ref[layer], f_ref[layer], s_ref[layer]
        else:
            p, f, s = above_ref[0], above_ref[1], above_ref[2]
        u, v, low, inverse = terms(total, f, s, power39(p))
        if layer == LAYERS:
            there = one_if(gz < sizes[0] - 1)
            u, v = u * there, v * there
        norm_z = norm_of(layer0 + layer, sizes[0] * LAYERS)
        uvw_ref[layer] = u
        uvw_ref[STEPS + layer] = v
        uvw_ref[2 * STEPS + layer] = low * inverse * (norms * (1.0 / norm_z))


def plane_of(uvw_ref, name, layer):
    return uvw_ref.at[STEPS * "uvw".index(name) + layer]


def pack_rows(uvw_ref, rows_ref):
    c = core()
    for (name, layer), (at, rows) in ROW_PLACES.items():
        start = aligned(c * (128 - rows), 8)
        rows_ref[pl.ds(at, rows), :] = plane_of(uvw_ref, name, layer)[pl.ds(start, rows), :]


def pack(uvw_ref, same_ref, cross_ref, keep_ref, give_ref):
    c = core()

    def put(at, left, right):
        count = left.shape[0]
        same_ref[pl.ds(at, count), :] = jnp.where(c == 0, right, left)
        cross_ref[pl.ds(at, count), :] = jnp.where(c == 0, left, right)

    def put_corner(slab, left, right):
        at, rows = CORNERS[slab]
        first, last = slice(0, rows), slice(left.shape[0] - rows, left.shape[0])
        keep_ref[pl.ds(at, rows), :] = jnp.where(c == 0, left[first], right[last])
        give_ref[pl.ds(at, rows), :] = jnp.where(c == 0, right[first], left[last])

    lane = lanes(128)
    for slab in range(4):
        left = right = jnp.zeros((128, 128), F32)
        for name, layer, where, at in strips():
            if where == slab:
                width = width_of(layer)
                plane = plane_of(uvw_ref, name, layer)[...]
                inside = (lane >= at) & (lane < at + width)
                left = jnp.where(inside, pltpu.roll(plane, at, 1) if at else plane, left)
                right = jnp.where(inside, pltpu.roll(plane, (at + width) % 128, 1), right)
        if slab < 3:
            put(128 * slab, left, right)
            put_corner(slab, left, right)
            continue
        put_corner(slab, left, right)
        folded = []
        for value in (left, right):
            total = value[:FOLDED]
            for i in range(1, 4):
                total = total + pltpu.roll(value[FOLDED * i:FOLDED * (i + 1)], FOLDED * i, 1)
            folded.append(total)
        put(384, *folded)
    lane = lanes(64)
    left = right = jnp.zeros((64, 128), F32)
    for layer in range(1, STEPS):
        ref = plane_of(uvw_ref, "w", layer)
        for half in range(2):
            plane = ref[pl.ds(64 * half, 64), :]
            at = 64 * half + RADIUS * (layer - 1)
            inside = (lane >= at) & (lane < at + RADIUS)
            left = jnp.where(inside, pltpu.roll(plane, at, 1) if at else plane, left)
            right = jnp.where(inside, pltpu.roll(plane, (at + RADIUS) % 128, 1), right)
    put(384 + FOLDED, left, right)
    put_corner(4, left, right)


def pick_corner(keep_ref, got_ref, corner_ref):
    corner_ref[...] = jnp.where((core() ^ seam()) == 1, keep_ref[...], got_ref[...])


def slab_plane(plain, same, cross, corner):
    c = core()
    inside = one_if(jnp.logical_not(outside()))
    plain[pl.ds(256, 32), :] = jnp.zeros((32, 128), F32)
    plain[pl.ds(aligned(c * 128, 128), 128), :] = same * inside
    plain[pl.ds(aligned((1 - c) * 128, 128), 128), :] = cross * inside
    rows = corner.shape[0]
    plain[pl.ds(aligned(256 + seam() * (32 - rows), 8), rows), :] = corner * inside


def full_plane(plain, name, layer, uvw_ref, other_ref, got_ref, shared_ref):
    c = core()
    plain[pl.ds(aligned(c * 128, 128), 128), :] = plane_of(uvw_ref, name, layer)[...]
    plain[pl.ds(aligned((1 - c) * 128, 128), 128), :] = plane_of(other_ref, name, layer)[...]
    plain[pl.ds(256, 32), :] = jnp.zeros((32, 128), F32)
    start, rows = ROW_PLACES[name, layer]
    here = pl.ds(start, rows)
    to = aligned(256 + seam() * (32 - rows), 8)
    plain[pl.ds(to, rows), :] = jnp.where((c ^ seam()) == 1, got_ref[here, :], shared_ref[here, :])
    return plain_to_plane(plain)


def with_columns(base, columns, at, width):
    c = core()
    lane = lanes(PLANE)
    columns = pltpu.roll(columns, (128 - at - (1 - c) * width) & 127, 1)
    begin = (1 - c) * (128 - width)
    return jnp.where((lane >= begin) & (lane < begin + width), columns, base)


def assemble(
    uvw_ref, other_ref, got_ref, shared_ref, same_ref, cross_ref, corner_ref, uv_ref, plain, slabs
):
    c = core()
    for slab in range(4):
        if slab < 3:
            here = pl.ds(128 * slab, 128)
            same, cross = same_ref[here, :], cross_ref[here, :]
            here = pl.ds(*CORNERS[slab])
        else:
            here = pl.ds(384, FOLDED)
            same, cross = (
                jnp.concatenate([value] + [pltpu.roll(value, 128 - FOLDED * i, 1) for i in range(1, 4)], axis=0)
                for value in (same_ref[here, :], cross_ref[here, :])
            )
            here = pl.ds(*CORNERS[3])
        corner = corner_ref[here, :]
        slot = plain.at[slab % 2]
        slab_plane(slot, same, cross, corner)
        slabs[slab] = plain_to_plane(slot)
    for place, (name, layer, slab, at) in enumerate(strips()):
        base = full_plane(plain.at[place % 2], name, layer, uvw_ref, other_ref, got_ref, shared_ref)
        uv_ref[2 * (LAYERS - layer) + (name == "v")] = with_columns(base, slabs[slab], at, width_of(layer))


def assemble_w(
    uvw_ref, other_ref, got_ref, shared_ref, same_ref, cross_ref, corner_ref, w_ref, plain, slabs
):
    c = core()

    def unfolded(ref):
        value = ref[pl.ds(384 + FOLDED, 64), :]
        return jnp.concatenate([value, pltpu.roll(value, 64, 1)], axis=0)

    here = pl.ds(*CORNERS[4])
    corner = corner_ref[here, :]
    corner = pltpu.roll(corner, 64 * seam(), 1)
    slab_plane(plain.at[0], unfolded(same_ref), unfolded(cross_ref), corner)
    slabs[0] = plain_to_plane(plain.at[0])
    for layer in range(1, STEPS):
        base = full_plane(plain.at[layer % 2], "w", layer, uvw_ref, other_ref, got_ref, shared_ref)
        w_ref[layer] = with_columns(base, slabs[0], RADIUS * (layer - 1), RADIUS)
    row = lax.broadcasted_iota(jnp.int32, (PLANE, 128), 0)
    col = lax.broadcasted_iota(jnp.int32, (PLANE, 128), 1)
    a = seam()
    row = jnp.where((a == 1) & (row >= 256), row - PLANE, row) + 256 * a
    width = jnp.where(c == 0, 108, 20)
    col = jnp.where((c == 0) & (col >= width), col - 128, jnp.where((c == 1) & (col < width), col + 128, col))
    col = col + 128 * lax.axis_index("gx")
    rows, cols = 128 * lax.axis_size("gy"), 128 * lax.axis_size("gx")
    norm = norm_of(row, rows) * norm_of(col, cols) * norm_of(0 * a, LAYERS * lax.axis_size("gz"))
    inside = (row >= 0) & (row < rows) & (col >= 0) & (col < cols)
    plain[0] = jnp.where(inside, 1.0 / jnp.where(inside, norm, 1.0), 0.0)
    w_ref[0] = plain_to_plane(plain.at[0])


def step_down(values, u_ref, v_ref, out_ref):
    new = []
    for t, value in enumerate(values):
        before = values[t - 1] if t > 0 else pltpu.roll(values[-1], 1, 0)
        behind = values[t + 1] if t < VECTORS - 1 else pltpu.roll(values[0], 7, 0)
        total = (value + before) + (behind + pltpu.roll(value, 1, 1)) + pltpu.roll(value, 127, 1)
        here = pl.ds(8 * t, 8)
        new.append(u_ref[here, :] + v_ref[here, :] * total)
        out_ref[here, :] = new[-1]
    return new


def set_carry(carry, main_ref, outer_ref, halo_ref, halo_outer_ref):
    c = core()
    lane = lanes(64)
    mine = (lane >> 6) == c
    inside = one_if(jnp.logical_not(outside()))
    begin = (1 - c) * (128 - REACH)
    beyond = (lane >= begin) & (lane < begin + REACH)
    for i in range(4):
        if main_ref.shape[0] == 256:
            value = main_ref[pl.ds(64 * i, 64), :]
        else:
            value = main_ref[pl.ds(64 * (i % 2), 64), :]
            if i >= 2:
                value = pltpu.roll(value, 64, 1)
            inner = pltpu.roll(main_ref[pl.ds(128, 64), :], (32 * (2 - c) - 32 * i) & 127, 1)
            value = jnp.where(mine, value, inner)
        outer = pltpu.roll(outer_ref[...], (128 - 32 * i) % 128, 1) if i else outer_ref[...]
        carry[pl.ds(64 * i, 64), :] = jnp.where(beyond, outer * inside, value)
    lane = lanes(24)
    beyond = (lane >= begin) & (lane < begin + REACH)
    carry[pl.ds(256, 32), :] = jnp.zeros((32, 128), F32)
    carry[pl.ds(aligned(256 + 8 * seam(), 8), 24), :] = jnp.where(beyond, halo_outer_ref[...] * inside, halo_ref[...])


def merge(give_ref, got_ref, down_ref, halo_ref):
    mine = (lanes(128) >> 6) == core()
    rows = pl.ds(0, 128)
    own, other = give_ref[rows, :], got_ref[rows, :]
    down_ref[rows, :] = jnp.where(mine, own, other)
    down_ref[pl.ds(128, 128), :] = pltpu.roll(jnp.where(mine, other, own), 64, 1)
    rows = pl.ds(128, 24)
    halo_ref[...] = jnp.where(mine[:24], give_ref[rows, :], got_ref[rows, :])


def load_carry(pieces, carry):
    set_carry(carry, *pieces)
    return [carry[pl.ds(t, 8, stride=VECTORS), :] for t in range(VECTORS)]


def run_down(values, uv_ref, layers_ref, first, last, base=0):
    for layer in range(first, last - 1, -1):
        at = 2 * (LAYERS - layer)
        values = step_down(values, uv_ref.at[at], uv_ref.at[at + 1], layers_ref.at[layer - base])
    return values


def section(active, shared, *refs):
    uv_ref, refs = refs[0], refs[1:]
    pieces, before_ref = (), None
    if len(refs) > 5:
        pieces, before_ref, refs = refs[:4], refs[4], refs[5:]
    layers_ref, down_ref, outer_ref, strip_ref, carry = refs

    @pl.when(lax.axis_index("gz") == active)
    def _():
        values = load_carry(pieces, carry) if pieces else [jnp.zeros((8, 128), F32)] * VECTORS
        values = run_down(values, uv_ref, layers_ref, LAYERS, 1)
        layers_ref[0] = layers_ref[1]
        for t in range(VECTORS):
            carry[pl.ds(t, 8, stride=VECTORS), :] = values[t]
        c = core()
        mine = (lanes(128) >> 6) == c
        down_ref[pl.ds(0, 128), :] = jnp.where(
            mine, carry[pl.ds(0, 128), :], pltpu.roll(carry[pl.ds(128, 128), :], 64, 1)
        )
        lane = lanes(64)
        slab = inner = jnp.zeros((64, 128), F32)
        for i in range(4):
            block = carry[pl.ds(64 * i, 64), :]
            rolled = pltpu.roll(block, 32 * i, 1) if i else block
            begin = (32 * i + 128 - c * 32) & 127
            slab = jnp.where(((lane - begin) & 127) < 32, rolled, slab)
            if not shared:
                inner = jnp.where((lane >> 5) == i, pltpu.roll(block, (32 * i - 32 * (2 - c)) & 127, 1), inner)
        outer_ref[...] = slab
        strip = carry[pl.ds(aligned((1 - seam()) * 232, 8), 24), :]
        strip_ref[...] = strip
        if shared:
            down_ref[pl.ds(128, 24), :] = strip
        else:
            down_ref[pl.ds(128, 64), :] = inner

    if before_ref is not None:
        @pl.when(lax.axis_index("gz") != active)
        def _():
            layers_ref[...] = before_ref[...]


def section_top(uv_ref, main_ref, outer_ref, halo_ref, halo_outer_ref, before_ref, top_ref, carry):
    @pl.when(lax.axis_index("gz") == 0)
    def _():
        values = load_carry((main_ref, outer_ref, halo_ref, halo_outer_ref), carry)
        run_down(values, uv_ref, top_ref, LAYERS, LOW, LOW)

    @pl.when(lax.axis_index("gz") != 0)
    def _():
        top_ref[...] = before_ref[pl.ds(LOW, STEPS - LOW)]


def section_rest(uv_ref, top_ref, before_ref, layers_ref):
    @pl.when(lax.axis_index("gz") == 0)
    def _():
        values = [top_ref[0, pl.ds(8 * t, 8), :] for t in range(VECTORS)]
        run_down(values, uv_ref, layers_ref, LOW - 1, 0)

    @pl.when(lax.axis_index("gz") != 0)
    def _():
        layers_ref[...] = before_ref[pl.ds(0, LOW)]


def box(values):
    two = [values[i] + values[i + 1] for i in range(len(values) - 1)]
    four = [two[i] + two[i + 2] for i in range(len(two) - 2)]
    return [four[i] + values[i + 4] for i in range(len(values) - 4)]


def smooth(layers, kept_ref, plains, others, tent):
    c = core()
    row = lax.broadcasted_iota(jnp.int32, (256, 128), 0)
    col = lax.broadcasted_iota(jnp.int32, (256, 128), 1)
    distance = (row - col + RADIUS) & 127
    weight = jnp.where(distance <= 2 * RADIUS, RADIUS + 1 - jnp.abs(distance - RADIUS), 0)
    tent[...] = weight.astype(F32).astype(jnp.bfloat16)
    for k, (layer_ref, w_ref) in enumerate(layers):
        plain = plains.at[k % 4]
        values = [layer_ref[pl.ds(8 * t, 8), :] * w_ref[pl.ds(8 * t, 8), :] for t in range(VECTORS)]
        first = [pltpu.roll(value, 1, 0) for value in values[VECTORS - RADIUS:]]
        last = [pltpu.roll(value, 7, 0) for value in values[:RADIUS]]
        total = jnp.concatenate(box(box(first + values + last)), axis=0)
        high = total.astype(jnp.bfloat16)
        rest = total - high.astype(F32)
        middle = rest.astype(jnp.bfloat16)
        small = (rest - middle.astype(F32)).astype(jnp.bfloat16)
        value = jnp.dot(jnp.concatenate([high, middle], axis=1), tent[...], preferred_element_type=F32)
        value = value + jnp.dot(small, tent[pl.ds(0, 128), :], preferred_element_type=F32)
        plane_to_plain(value, plain)
        kept_ref[k] = plain[pl.ds(aligned(c * 128, 128), 128), :]
        others[k] = plain[pl.ds(aligned((1 - c) * 128, 128), 128), :]


def pair_up(others, first, count, give_ref):
    mine = (lanes(128) >> 6) == core()
    for k in range(count):
        give_ref[k] = jnp.where(mine, others[first + k], pltpu.roll(others[first + count + k], 64, 1))


def smooth_first(top_ref, before_ref, w_ref, kept_ref, give_ref, plains, others, tent):
    layers = [(top_ref.at[k], w_ref.at[LOW + k]) for k in range(STEPS - LOW)]
    layers += [(before_ref.at[k], w_ref.at[k]) for k in range(1, RADIUS)]
    smooth(layers, kept_ref, plains, others, tent)
    pair_up(others, 0, 4, give_ref)


def smooth_rest(layers_ref, w_ref, kept_ref, give_ref, give_more_ref, plains, others, tent):
    smooth([(layers_ref.at[k], w_ref.at[k]) for k in range(LOW)], kept_ref, plains, others, tent)
    pair_up(others, 0, 3, give_ref)
    pair_up(others, 6, 3, give_more_ref)


def whole(kept, got, second):
    mine = (lanes(128) >> 6) == core()
    return jnp.where(mine, kept, pltpu.roll(got, 64, 1) if second else got)


def ends(kept_ref, got_ref, top_ref, bottom_ref):
    for k in range(8):
        value = whole(kept_ref[k], got_ref[k % 4], k >= 4)
        if k < STEPS - LOW:
            top_ref[k] = value
        else:
            bottom_ref[k - (STEPS - LOW)] = value


def finish(kept_ref, got_ref, got_more_ref, top_ref, below_ref, above_ref, passive_ref, out_ref, tile):
    gz = lax.axis_index("gz")
    for k in range(LOW):
        got = got_ref if k < 6 else got_more_ref
        tile[k] = whole(kept_ref[k], got[k % 3], k % 6 >= 3)

    def layer(k):
        if k < 0:
            return jnp.where(gz > 0, below_ref[k + RADIUS], 0.0)
        if k == 0:
            return jnp.where(gz == 0, tile[0], below_ref[RADIUS])
        if k > LAYERS:
            return jnp.where(gz < lax.axis_size("gz") - 1, above_ref[k - STEPS], 0.0)
        return tile[k] if k < LOW else top_ref[k - LOW]

    for k in range(LAYERS):
        total = layer(k) * 5.0
        for offset in range(1, RADIUS + 1):
            total = total + (layer(k - offset) + layer(k + offset)) * (5.0 - offset)
        out_ref[k] = jnp.where(passive_ref[k] > 0, 0.0, total)


def to_other(value):
    return moved(value, lambda z, y, x: (z, y ^ 1, x))


def after(value, *others):
    return lax.optimization_barrier((value,) + others)[0]


def per_device(filtered, printed, sensitivity, passive):
    sizes = tuple(lax.axis_size(axis) for axis in AXES)
    depth = sizes[0]
    plane = shape(128, 128)
    edge = shape(16, 128)

    def across(z, y, x):
        return (z, y ^ 3, x) if y in (1, 2) else None

    def on_grid(x):
        return 0 <= x < sizes[2]

    def beside(z, y, x):
        to = x + (1 if y & 1 else -1)
        return (z, y ^ 1, to) if on_grid(to) else (z, y ^ 2, x)

    def same(z, y, x):
        to = x + (-1 if y & 1 else 1)
        return (z, y, to) if on_grid(to) else (z, y ^ 1, x)

    def opposite(z, y, x):
        to = x + (1 if y & 1 else -1)
        return (z, y, to) if on_grid(to) else (z, y ^ 1, x)

    def across_beside(z, y, x):
        to = x + (1 if y & 1 else -1)
        return (z, 3 - y, to) if on_grid(to) else (z, y ^ 2, x)

    hbm = pl.BlockSpec(memory_space=pltpu.HBM)
    lowest_planes, inner, outer, along, back = call(
        edges, [shape(3, 128, 128)] + [edge] * 4, printed, filtered, sensitivity,
        in_specs=[hbm] * 3,
        scratch=[pltpu.VMEM((128, 128), F32), pltpu.VMEM((LAYERS, 128, 128), F32), pltpu.SemaphoreType.DMA((6,))],
    )
    above = moved(lowest_planes, lambda z, y, x: (z - 1, y, x) if z > 0 else None)
    along, back = moved(along, same), moved(back, opposite)
    outer = moved(outer, lambda z, y, x: (z, y ^ 3, x))
    inner = to_other(inner)
    ready = call(early, shape(8, 128), printed, filtered, after(sensitivity, inner))
    uvw = call(
        functools.partial(all_terms, sizes), shape(3 * STEPS, 128, 128),
        printed, filtered, sensitivity, above, inner, outer, along, back, ready,
        scratch=[
            pltpu.VMEM((144, 128), F32), pltpu.VMEM((128, 128), F32),
        ],
    )
    slab, corner = shape(SLAB_ROWS, 128), shape(CORNER_ROWS, 128)
    rows = call(pack_rows, shape(ROW_TOTAL, 128), uvw)
    got = moved(rows, across)
    to_same, to_cross, keep, give = call(pack, [slab, slab, corner, corner], after(uvw, rows))
    from_same = moved(to_same, same)
    from_cross = moved(to_cross, beside)
    corner = call(pick_corner, corner, keep, to_other(give))
    corner = moved(corner, across_beside)
    other = to_other(uvw)
    shared = to_other(after(got, from_same, from_cross, corner))
    parts = (uvw, other, got, shared, from_same, from_cross, corner)
    stack = shape(STEPS, PLANE, 128)
    work = [pltpu.VMEM((2, PLANE, 128), F32), pltpu.VMEM((4, PLANE, 128), F32)]
    uvs = call(assemble, shape(2 * STEPS, PLANE, 128), *parts, scratch=work)
    ws = None
    pieces, before = (), ()
    whole_stack = [pltpu.VMEM((PLANE, 128), F32)]
    for active in range(depth - 1, 0, -1):
        swap = (depth - 1 - active) % 2 == 1
        layers, main, side, strip = call(
            functools.partial(section, active, swap),
            [stack, shape(152 if swap else 192, 128), shape(64, 128), shape(24, 128)],
            uvs, *pieces, *before, scratch=whole_stack,
        )
        before = (layers,)

        def down(where):
            def to(z, y, x):
                target = where(z, y, x) if z == active else None
                return target and (z - 1,) + target[1:]
            return to

        def over(z, y, x):
            return (z, y ^ 2, x)

        def beyond(z, y, x):
            return beside(z, y, x) if on_grid(x + (1 if y & 1 else -1)) else None

        def corner_of(z, y, x):
            target = beyond(z, y, x)
            return target and (z, target[1] ^ 2, target[2])

        side = moved(side, down(beyond))
        edge_piece = moved(strip, down(corner_of))
        halo = strip
        if swap:
            main, halo = call(merge, [shape(256, 128), shape(24, 128)], main, to_other(main))
        main = moved(main, down(lambda z, y, x: (z, y, x)))
        halo = moved(halo, down(over))
        pieces = (main, side, halo, edge_piece)
        if ws is None:
            ws = call(assemble_w, stack, after(uvw, side), *parts[1:], scratch=work)
    top_layers = call(
        section_top, shape(STEPS - LOW, PLANE, 128), uvs, *pieces, layers, scratch=whole_stack
    )

    def work_for(count):
        return [
            pltpu.VMEM((4, PLANE, 128), F32), pltpu.VMEM((count, 128, 128), F32), pltpu.VMEM((256, 128), jnp.bfloat16)
        ]

    kept, given = call(
        smooth_first, [shape(8, 128, 128), shape(4, 128, 128)], top_layers, layers, ws, scratch=work_for(8)
    )
    top, bottom = call(ends, [shape(RADIUS + 1, 128, 128), shape(RADIUS - 1, 128, 128)], kept, to_other(given))
    below = moved(top, lambda z, y, x: (z + 1, y, x))
    over = moved(bottom, lambda z, y, x: (z - 1, y, x))
    rest = call(section_rest, shape(LOW, PLANE, 128), uvs, after(top_layers, top), layers)
    third = shape(3, 128, 128)
    kept, given, given_more = call(
        smooth_rest, [shape(LOW, 128, 128), third, third], rest, ws, scratch=work_for(LOW)
    )
    return call(
        finish, shape(LAYERS, 128, 128),
        kept, to_other(given), to_other(given_more), top, below, over, passive,
        scratch=[pltpu.VMEM((LOW, 128, 128), F32)],
    )


def solution(mesh):
    spec = P(*AXES)
    return jax.shard_map(
        per_device, mesh=mesh, in_specs=(spec,) * 4, out_specs=spec, check_vma=False
    )
```
